256 devices in a mesh: col: 32 (over y, x, core), sec: 8 (over z).
Axes of the slice: x: 4, y: 4, z: 8, core: 2. Of those that a mesh axis runs over, the one named last changes fastest.
Arguments:
- boundaries: bfloat16 [8, 2, 32, 64, 4096], P('sec', None, 'col'), may hold values from -6 to 6
- row_ops: bfloat16 [2, 32, 8, 8, 64, 64], P(None, 'col'), may hold values from -0.25 to 0.25
- ranks: int32 [8, 2, 32], P('sec', None, 'col'), may hold values from 32 to 64, as said below
Outputs:
- canonical: bfloat16 [8, 2, 32, 64, 4096], P('sec', None, 'col')
The draws below stay inside these ranges and needn't reach their ends.
Inputs may be any that keep to these rules, and one draw needn't show every extreme that they name: `ranks`: for every boundary and column, at least one sector block keeps all 64.
All inputs are finite; a program needn't handle non-finite values.
Results may differ from the reference program's by a relative error of at most 0.0012.
Values may be sent and summed in bfloat16 or wider, within the bound.
A program may use at most 128 MiB of HBM per device.

```python
import jax
import jax.numpy as jnp
from jax import lax

P_SIZE = 64
PH = 64
NS = 8
NC = 32


def draw_ranks(key, part):
    first = jax.random.fold_in(key, 11)
    second = jax.random.fold_in(key, 23)
    base = jax.random.randint(first, (NS, 2, NC), P_SIZE // 2, P_SIZE + 1)
    chosen = jax.random.randint(second, (2, NC), 0, NS)
    sector_ids = jnp.arange(NS, dtype=jnp.int32)[:, None, None]
    return jnp.where(sector_ids == chosen[None], P_SIZE, base).astype(jnp.int32)


def column_maps(key, spread):
    perm_keys = jax.random.split(jax.random.fold_in(key, 5), 2 * NC)
    orders = jax.vmap(lambda one: jax.random.permutation(one, P_SIZE))(perm_keys).reshape(2, NC, P_SIZE)
    onehot = (jnp.arange(P_SIZE, dtype=jnp.int32)[None, None, :, None] == orders[:, :, None, :]).astype(jnp.float32)
    flips = 2.0 * jax.random.randint(jax.random.fold_in(key, 6), (2, NC, 1, P_SIZE), 0, 2).astype(jnp.float32) - 1.0
    jitter = jax.random.normal(jax.random.fold_in(key, 7), (2, NC, P_SIZE, P_SIZE), jnp.float32)
    maps = onehot * flips + spread / float(P_SIZE) ** 0.5 * jitter
    return maps.reshape(2, NC, P_SIZE * P_SIZE)


def draw_boundaries(key, part):
    key = jax.random.fold_in(key, 37)
    sigma = 0.6 / float(P_SIZE) ** 0.5
    weights = jax.random.uniform(jax.random.fold_in(key, 1), (NS, 2, NC, PH), jnp.float32, -1.0, 1.0)
    maps = column_maps(key, 0.4)
    noise = sigma * jax.random.normal(jax.random.fold_in(key, 2), (NS, 2, NC, PH, P_SIZE * P_SIZE), jnp.float32)
    values = 2.5 * weights[..., None] * maps[None, :, :, None, :] + noise
    return jnp.clip(values, -6.0, 6.0).astype(jnp.bfloat16)


def shard_levels(stream_key, dims, cuts, low, largest):
    level = 1.0
    for axis_at, parts in cuts:
        heights = jax.random.uniform(jax.random.fold_in(jax.random.fold_in(stream_key, 6), axis_at), (parts,), jnp.float32, low / len(cuts), largest / len(cuts))
        level = level * jnp.repeat(jnp.exp(heights), dims[axis_at] // parts).reshape((-1,) + (1,) * (len(dims) - 1 - axis_at))
    return level


def gaussian(key, shape, scale, bound, cuts=(), kind=jnp.bfloat16):
    gain = shard_levels(key, shape, cuts, -0.22, 0.18) if cuts else 1.0
    values = jax.random.normal(key, shape, jnp.float32) * scale * gain
    return jnp.minimum(jnp.maximum(values, -bound), bound).astype(kind)


def setup_inputs(seed: int = 0) -> dict:
    arg_keys = jax.random.split(jax.random.key(seed), 4)
    boundaries = draw_boundaries(jax.random.fold_in(arg_keys[3], 71), 0)
    row_ops = gaussian(arg_keys[1], (2, NC, NS, NS, PH, PH), (NS * PH) ** -0.5, 0.25, ((1, 32),))
    ranks = draw_ranks(jax.random.fold_in(arg_keys[3], 71), 0)
    return {"boundaries": boundaries, "row_ops": row_ops, "ranks": ranks}


def reference(boundaries, row_ops, ranks):
    high = lax.Precision.HIGHEST
    index = jnp.arange(P_SIZE, dtype=jnp.int32)
    factor = float(PH * P_SIZE) ** 0.5
    start = jnp.broadcast_to(jnp.eye(P_SIZE, dtype=jnp.float32), (NS, 2, P_SIZE, P_SIZE))

    def column(left, col_index):
        blocks = lax.dynamic_index_in_dim(boundaries, col_index, 2, keepdims=False).astype(jnp.float32)
        operators = lax.dynamic_index_in_dim(row_ops, col_index, 1, keepdims=False).astype(jnp.float32)
        absorbed = jnp.einsum('sbpx,bstpq->tbqx', blocks, operators, precision=high)
        field = absorbed.reshape(NS, 2, PH, P_SIZE, P_SIZE)
        mixed = jnp.einsum('tbak,tbpkr->tbpar', left, field, precision=high)
        flat = mixed.reshape(NS, 2, PH * P_SIZE, P_SIZE)
        gram = jnp.einsum('tbxr,tbxq->tbrq', flat, flat, precision=high)
        lower = jnp.linalg.cholesky(gram)
        ortho = lax.linalg.triangular_solve(lower, flat, left_side=False, lower=True, transpose_a=True)
        limit = lax.dynamic_index_in_dim(ranks, col_index, 2, keepdims=False)
        keep = (index[None, None, :] < limit[:, :, None]).astype(jnp.float32)
        result = (factor * ortho * keep[:, :, None, :]).astype(jnp.bfloat16).reshape(NS, 2, PH, P_SIZE * P_SIZE)
        upper = jnp.swapaxes(lower, -1, -2) * keep[:, :, :, None]
        scale = lax.rsqrt(lax.optimization_barrier(jnp.mean(upper * upper, axis=(-2, -1), keepdims=True)) + 1e-06)
        return (upper * scale, result)
    _, outputs = lax.scan(column, start, jnp.arange(NC, dtype=jnp.int32))
    return jnp.moveaxis(outputs, 0, 2)
```

```python
import functools
import math

import jax
import jax.numpy as jnp
from jax import lax
from jax.experimental import pallas as pl
from jax.experimental.pallas import tpu as pltpu
from jax.sharding import PartitionSpec as P

MESH = pl.DeviceIdType.MESH
N = 64
NT = (((1,), (1,)), ((), ()))
NN = (((1,), (0,)), ((), ()))


def dot(a, b, dims):
    return lax.dot_general(a, b, dims, preferred_element_type=jnp.float32)


def split(x):
    hi = x.astype(jnp.bfloat16)
    lo = (x - hi.astype(jnp.float32)).astype(jnp.bfloat16)
    return hi, lo


def factor_pairs(grams):
    count = len(grams)
    rows = [[g[8 * i : 8 * i + 8] for i in range(8)] for g, _ in grams]
    out = [[None] * N for _ in grams]
    wide = (8, 128)
    for p in range(8):
        cols = [{} for _ in grams]
        for n in range(count):
            base = grams[n][1] + 8 * p
            for r in range(p, 8):
                cols[n][r] = [jnp.broadcast_to(rows[n][r][:, base + a : base + a + 1], wide) for a in range(8)]
        for a in range(8):
            for n in range(count):
                pivot = jnp.broadcast_to(cols[n][p][a][a : a + 1, :], wide)
                inverse = 1.0 / pivot
                row = jnp.broadcast_to(rows[n][p][a : a + 1, :], wide)
                out[n][8 * p + a] = row[0:1] * lax.rsqrt(pivot[0:1])
                heads = [jnp.broadcast_to(cols[n][p][b][a : a + 1, :], wide) if b > a else None for b in range(8)]
                for r in range(p, 8):
                    times = cols[n][r][a] * inverse
                    for b in range(a + 1, 8):
                        cols[n][r][b] = cols[n][r][b] - times * heads[b]
                    rows[n][r] = rows[n][r] - times * row
    return [jnp.concatenate(o, 0) for o in out]


def chain_kernel(ranks_ref, at_ref, out_ref, at_hi, at_lo, mixed, l_in, l_out, send_sem, recv_sem):
    me = lax.axis_index("col")
    last = lax.axis_size("col") - 1
    sec = lax.axis_index("sec")
    barrier = pltpu.get_barrier_semaphore()

    @pl.when(me > 0)
    def _():
        pl.semaphore_signal(barrier, inc=1, device_id=(me - 1, sec), device_id_type=MESH)

    for b in range(2):
        for c in range(8):
            hi, lo = split(at_ref[b, 128 * c : 128 * c + 128, :])
            at_hi[b, 128 * c : 128 * c + 128, :] = hi
            at_lo[b, 128 * c : 128 * c + 128, :] = lo

    lane = lax.broadcasted_iota(jnp.int32, (N, 128), 1)
    line = lax.broadcasted_iota(jnp.int32, (N, 128), 0)
    low = lane < N
    place = jnp.where(low, lane, lane - N)
    eye = jnp.where(place == line, 1.0, 0.0).astype(jnp.float32)
    keep = line < jnp.where(low, ranks_ref[0], ranks_ref[1])
    copy = pltpu.make_async_remote_copy(
        src_ref=l_out, dst_ref=l_in, send_sem=send_sem, recv_sem=recv_sem,
        device_id=(jnp.minimum(me + 1, last), sec), device_id_type=MESH,
    )

    @pl.when(me < last)
    def _():
        pl.semaphore_wait(barrier, 1)

    @pl.when(me == 0)
    def _():
        l_in[...] = eye

    @pl.when(me > 0)
    def _():
        copy.wait_recv()

    left = l_in[...]
    turned = pltpu.roll(left, N, 1)
    squares = left * left
    scales = []
    grams = []
    for b in range(2):
        at_low = jnp.where(low, left if b == 0 else turned, 0.0)
        at_high = jnp.where(low, 0.0, turned if b == 0 else left)
        zero = jnp.zeros((N, 128), jnp.bfloat16)
        low_hi, low_lo = split(at_low)
        high_hi, high_lo = split(at_high)

        def diagonal(x, y):
            return jnp.concatenate(
                [jnp.concatenate([x, y, zero, zero], 0), jnp.concatenate([zero, zero, x, y], 0)], 1
            )

        w_hi, w_lo = diagonal(low_hi, high_hi), diagonal(low_lo, high_lo)
        for c in range(8):
            a_hi = at_hi[b, 128 * c : 128 * c + 128, :]
            a_lo = at_lo[b, 128 * c : 128 * c + 128, :]
            x = dot(a_hi, w_hi, NT) + dot(a_lo, w_hi, NT) + dot(a_hi, w_lo, NT)
            hi, lo = split(x)
            mixed[b, 0:128, 256 * c : 256 * c + 256] = hi
            mixed[b, 128:256, 256 * c : 256 * c + 256] = lo
        y = mixed[b]
        g = dot(y, y, NT)
        g = g[0:128] + g[128:256]
        g = g[:, 0:128] + g[:, 128:256]
        even, odd = g[0:N], g[N:]
        total = jnp.sum(jnp.where(low == (b == 0), squares, 0.0), keepdims=True)
        scale = lax.rsqrt(total * (1.0 / (N * N)) + 1e-06)
        scale = jnp.where(me == 0, jnp.ones_like(scale), scale)
        scales.append(scale)
        if b == 0:
            full = (even + pltpu.roll(odd, N, 1)) * (scale * scale)
            grams.append((jnp.where(low, full, eye), 0))
        else:
            full = (pltpu.roll(even, N, 1) + odd) * (scale * scale)
            grams.append((jnp.where(low, eye, full), N))
    first, second = factor_pairs(grams)
    upper = jnp.where(low, first, second)
    l_out[...] = jnp.where(jnp.logical_and(keep, place >= line), upper, 0.0)

    @pl.when(me < last)
    def _():
        copy.start()

    factor = math.sqrt(N * N)
    for b in range(2):
        inverse = second if b else first
        mask = low if b else jnp.logical_not(low)
        rank = ranks_ref[b]
        inverse = jnp.where(jnp.logical_and(mask, line < rank), inverse, 0.0) * (scales[b] * factor)
        other = pltpu.roll(inverse, N, 1)
        pair = jnp.concatenate([inverse, other], 0) if b else jnp.concatenate([other, inverse], 0)
        p_hi, p_lo = split(pair)
        wide_hi = jnp.concatenate([p_hi, p_hi], 1)
        for c in range(8):
            y = mixed[b, :, 256 * c : 256 * c + 256]
            o = dot(wide_hi, y, NN) + dot(p_lo, y[0:128], NN)
            out_ref[b, 128 * c : 128 * c + 128, :] = o.astype(jnp.bfloat16)

    @pl.when(me < last)
    def _():
        copy.wait_send()


def chain(at, ranks):
    vmem = pl.BlockSpec(memory_space=pltpu.VMEM)
    return pl.pallas_call(
        chain_kernel,
        out_shape=jax.ShapeDtypeStruct((2, 1024, 256), jnp.bfloat16),
        in_specs=[pl.BlockSpec(memory_space=pltpu.SMEM), vmem],
        out_specs=vmem,
        scratch_shapes=[
            pltpu.VMEM((2, 1024, 256), jnp.bfloat16),
            pltpu.VMEM((2, 1024, 256), jnp.bfloat16),
            pltpu.VMEM((2, 256, 2048), jnp.bfloat16),
            pltpu.VMEM((N, 128), jnp.float32),
            pltpu.VMEM((N, 128), jnp.float32),
            pltpu.SemaphoreType.DMA,
            pltpu.SemaphoreType.DMA,
        ],
        compiler_params=pltpu.CompilerParams(
            collective_id=0, has_side_effects=True, vmem_limit_bytes=40 * 1024 * 1024
        ),
    )(ranks, at)


def on_device(boundaries, row_ops, ranks):
    my_sector = lax.axis_index("sec")
    ops_mine = lax.dynamic_slice_in_dim(row_ops, my_sector, 1, 3)
    absorbed = jnp.einsum(
        "sbcpx,bcstpq->tbcqx",
        lax.all_gather(boundaries, "sec", axis=0, tiled=True),
        ops_mine,
        preferred_element_type=jnp.float32,
    )
    at = absorbed.reshape(2, 16, 4, N, N).transpose(0, 1, 4, 2, 3).reshape(2, 1024, 256)
    out = chain(at, ranks.reshape(2))
    out = out.reshape(2, 16, N, 4, N).transpose(0, 1, 3, 4, 2)
    return out.reshape(1, 2, 1, N, N * N)


def solution(mesh):
    placed = (
        P("sec", None, "col", None, None),
        P(None, "col", None, None, None, None),
        P("sec", None, "col"),
    )
    return jax.shard_map(
        on_device,
        mesh=mesh,
        in_specs=placed,
        out_specs=P("sec", None, "col", None, None),
        check_vma=False,
    )
```

```python
import functools
import math

import jax
import jax.numpy as jnp
from jax import lax
from jax.experimental import pallas as pl
from jax.experimental.pallas import tpu as pltpu
from jax.sharding import PartitionSpec as P

MESH = pl.DeviceIdType.MESH
N = 64
NT = (((1,), (1,)), ((), ()))
NN = (((1,), (0,)), ((), ()))


def dot(a, b, dims):
    return lax.dot_general(a, b, dims, preferred_element_type=jnp.float32)


def split(x):
    hi = x.astype(jnp.bfloat16)
    lo = (x - hi.astype(jnp.float32)).astype(jnp.bfloat16)
    return hi, lo


def factor_pairs(grams):
    count = len(grams)
    rows = [[g[8 * i : 8 * i + 8] for i in range(8)] for g, _ in grams]
    out = [[None] * N for _ in grams]
    wide = (8, 128)
    for p in range(8):
        cols = [{} for _ in grams]
        for n in range(count):
            base = grams[n][1] + 8 * p
            for r in range(p, 8):
                cols[n][r] = [jnp.broadcast_to(rows[n][r][:, base + a : base + a + 1], wide) for a in range(8)]
        for a in range(8):
            for n in range(count):
                pivot = jnp.broadcast_to(cols[n][p][a][a : a + 1, :], wide)
                inverse = 1.0 / pivot
                row = jnp.broadcast_to(rows[n][p][a : a + 1, :], wide)
                out[n][8 * p + a] = row[0:1] * lax.rsqrt(pivot[0:1])
                heads = [jnp.broadcast_to(cols[n][p][b][a : a + 1, :], wide) if b > a else None for b in range(8)]
                for r in range(p, 8):
                    times = cols[n][r][a] * inverse
                    for b in range(a + 1, 8):
                        cols[n][r][b] = cols[n][r][b] - times * heads[b]
                    rows[n][r] = rows[n][r] - times * row
    return [jnp.concatenate(o, 0) for o in out]


def patterns():
    lane = lax.broadcasted_iota(jnp.int32, (N, 128), 1)
    line = lax.broadcasted_iota(jnp.int32, (N, 128), 0)
    low = lane < N
    place = jnp.where(low, lane, lane - N)
    eye = jnp.where(place == line, 1.0, 0.0).astype(jnp.float32)
    return line, low, place, eye


def absorb(ops, blocks, acc, q, sectors, first):
    lhs = [ops[q, s] for s in sectors]

    def tile(n, carry):
        at = pl.ds(pl.multiple_of(n * 512, 512), 512)
        total = dot(lhs[0], blocks[q, sectors[0], :, at], NN)
        for left, s in zip(lhs[1:], sectors[1:]):
            total = total + dot(left, blocks[q, s, :, at], NN)
        acc[:, at] = total if first else acc[:, at] + total
        return carry

    lax.fori_loop(0, 8, tile, 0)


def to_columns(acc, rows, at_hi, at_lo, q):
    low = lax.broadcasted_iota(jnp.int32, (32, 128), 1) < N
    for m in range(32):
        v = acc[:, 128 * m : 128 * m + 128]
        w = pltpu.roll(v, N, 1)
        rows[pl.ds(2 * m, 32, stride=N), :] = jnp.where(low, v[0:32], w[32:64])
        rows[pl.ds(2 * m + 1, 32, stride=N), :] = jnp.where(low, w[0:32], v[32:64])
    for t in range(16):
        hi, lo = split(rows[128 * t : 128 * t + 128, :].T)
        c, half = t // 2, 128 * (t % 2)
        at_hi[q, 128 * c : 128 * c + 128, half : half + 128] = hi
        at_lo[q, 128 * c : 128 * c + 128, half : half + 128] = lo


def diagonal(x, y):
    zero = jnp.zeros((N, 128), jnp.bfloat16)
    return jnp.concatenate([jnp.concatenate([x, y, zero, zero], 0), jnp.concatenate([zero, zero, x, y], 0)], 1)


def advance(left, unit, keep, at_hi, at_lo, mixed, q):
    line, low, place, eye = patterns()
    turned = pltpu.roll(left, N, 1)
    low_hi, low_lo = split(jnp.where(low, left, 0.0))
    high_hi, high_lo = split(jnp.where(low, 0.0, turned))
    w_hi, w_lo = diagonal(low_hi, high_hi), diagonal(low_lo, high_lo)
    for c in range(8):
        a_hi = at_hi[q, 128 * c : 128 * c + 128, :]
        a_lo = at_lo[q, 128 * c : 128 * c + 128, :]
        x = dot(a_hi, w_hi, NT) + dot(a_lo, w_hi, NT) + dot(a_hi, w_lo, NT)
        hi, lo = split(x)
        mixed[q, 0:128, 256 * c : 256 * c + 256] = hi
        mixed[q, 128:256, 256 * c : 256 * c + 256] = lo
    y = mixed[q]
    g = dot(y, y, NT)
    g = g[0:128] + g[128:256]
    g = g[:, 0:128] + g[:, 128:256]
    total = jnp.sum(jnp.where(low, left * left, 0.0), keepdims=True)
    scale = lax.rsqrt(total * (1.0 / (N * N)) + 1e-06)
    scale = jnp.where(unit, jnp.ones_like(scale), scale)
    full = (g[0:N] + pltpu.roll(g[N:], N, 1)) * (scale * scale)
    (rows,) = factor_pairs([(jnp.where(low, full, eye), 0)])
    upper = jnp.where(jnp.logical_and(keep, place >= line), rows, 0.0)
    inverse = jnp.where(jnp.logical_or(low, jnp.logical_not(keep)), 0.0, rows) * (scale * float(N))
    return upper, inverse


def results(inverse, mixed, rows, out, q):
    pair = jnp.concatenate([pltpu.roll(inverse, N, 1), inverse], 0)
    p_hi, p_lo = split(pair)
    wide = jnp.concatenate([p_hi, p_hi], 1)
    for c in range(8):
        y = mixed[q, :, 256 * c : 256 * c + 256]
        o = dot(wide, y, NN) + dot(p_lo, y[0:128], NN)
        rows[256 * c : 256 * c + 128, :] = o[:, 0:128].T
        rows[256 * c + 128 : 256 * c + 256, :] = o[:, 128:256].T
    low = lax.broadcasted_iota(jnp.int32, (32, 128), 1) < N
    for m in range(32):
        e = rows[pl.ds(2 * m, 32, stride=N), :]
        d = rows[pl.ds(2 * m + 1, 32, stride=N), :]
        at = slice(128 * m, 128 * m + 128)
        out[q, 0:32, at] = jnp.where(low, e, pltpu.roll(d, N, 1)).astype(jnp.bfloat16)
        out[q, 32:64, at] = jnp.where(low, pltpu.roll(e, N, 1), d).astype(jnp.bfloat16)


def sweep_kernel(
    ops_ref, limit_ref, bnd_ref, out_ref,
    blocks, ops, limits, acc, rows, at_hi, at_lo, mixed, out, l_in, l_out, left_ref,
    part_send, part_recv, own_sem, ring_send, ring_recv, l_send, l_recv, out_send, out_recv, out_own,
):
    me = lax.axis_index("col")
    last = lax.axis_size("col") - 2
    z = lax.axis_index("sec")
    size = lax.axis_size("sec")
    core = lax.rem(me, 2)
    partner = me + 1 - 2 * core
    up, down = lax.rem(z + 1, size), lax.rem(z + size - 1, size)
    has_next = me < last
    has_before = me >= 2

    barrier = pltpu.get_barrier_semaphore()
    for to in ((partner, z), (me, up), (me, down)):
        pl.semaphore_signal(barrier, inc=1, device_id=to, device_id_type=MESH)

    @pl.when(has_before)
    def _():
        pl.semaphore_signal(barrier, inc=1, device_id=(me - 2, z), device_id_type=MESH)

    @pl.when(has_next)
    def _():
        pl.semaphore_wait(barrier, 4)

    @pl.when(jnp.logical_not(has_next))
    def _():
        pl.semaphore_wait(barrier, 3)

    def to_partner(n, source, target):
        return pltpu.make_async_remote_copy(
            src_ref=source, dst_ref=target, send_sem=part_send.at[n], recv_sem=part_recv.at[n],
            device_id=(partner, z), device_id_type=MESH,
        )

    crossing = [
        to_partner(0, bnd_ref.at[0, 1 - core, 0], blocks.at[core, z]),
        to_partner(1, ops_ref.at[1 - core], ops.at[core]),
        to_partner(2, limit_ref.at[1 - core], limits.at[core]),
    ]
    staying = [
        pltpu.make_async_copy(bnd_ref.at[0, core, 0], blocks.at[core, z], own_sem.at[0]),
        pltpu.make_async_copy(ops_ref.at[core], ops.at[core], own_sem.at[1]),
        pltpu.make_async_copy(limit_ref.at[core], limits.at[core], own_sem.at[2]),
    ]
    for copy in crossing + staying:
        copy.start()

    def ring(q, way, d, half):
        block = lax.rem(z + size + (d - 1 if way else 1 - d), size)
        part = blocks.at[q, block, 32 * half : 32 * half + 32]
        return pltpu.make_async_remote_copy(
            src_ref=part, dst_ref=part, send_sem=ring_send.at[q, way, d - 1, half], recv_sem=ring_recv.at[q, way, d - 1, half],
            device_id=(me, down if way else up), device_id_type=MESH,
        )

    def exists(way, d, half):
        return d < 4 or (d == 4 and half == way)

    def begin(q):
        @pl.when(core == q)
        def _():
            staying[0].wait()

        @pl.when(core != q)
        def _():
            crossing[0].wait_recv()

        for half in range(2):
            for way in range(2):
                ring(q, way, 1, half).start()

    def turn(q, d):
        for half in range(2):
            for way in range(2):
                if exists(way, d, half):
                    ring(q, way, d, half).wait_recv()
                    if exists(way, d + 1, half):
                        ring(q, way, d + 1, half).start()

    def sectors(d):
        before, after = lax.rem(z + size - d, size), lax.rem(z + d, size)
        return [z] if d == 0 else [after] if d == 4 else [before, after]

    begin(0)
    for copy in staying[1:]:
        copy.wait()
    for copy in crossing[1:]:
        copy.wait_recv()
    for d in range(5):
        if d > 0:
            turn(0, d)
        if d == 3:
            begin(1)
        absorb(ops, blocks, acc, 0, sectors(d), d == 0)
    turn(1, 1)
    to_columns(acc, rows, at_hi, at_lo, 0)
    absorb(ops, blocks, acc, 1, sectors(0), True)
    absorb(ops, blocks, acc, 1, sectors(1), False)
    for d in range(2, 5):
        turn(1, d)
        absorb(ops, blocks, acc, 1, sectors(d), False)
    to_columns(acc, rows, at_hi, at_lo, 1)

    line, low, place, eye = patterns()
    along = pltpu.make_async_remote_copy(
        src_ref=l_out, dst_ref=l_in, send_sem=l_send, recv_sem=l_recv,
        device_id=(jnp.where(has_next, me + 2, me), z), device_id_type=MESH,
    )

    @pl.when(jnp.logical_not(has_before))
    def _():
        left_ref[...] = eye

    @pl.when(has_before)
    def _():
        along.wait_recv()
        left_ref[...] = l_in[...]

    def keep(q):
        return line.astype(jnp.float32) < limits[q, 0:1, :]

    upper, inverse0 = advance(left_ref[...], jnp.logical_not(has_before), keep(0), at_hi, at_lo, mixed, 0)
    upper, inverse1 = advance(upper, False, keep(1), at_hi, at_lo, mixed, 1)
    l_out[...] = upper

    @pl.when(has_next)
    def _():
        along.start()

    across = pltpu.make_async_remote_copy(
        src_ref=out.at[1 - core], dst_ref=out_ref.at[0, core, 0], send_sem=out_send, recv_sem=out_recv,
        device_id=(partner, z), device_id_type=MESH,
    )
    home = pltpu.make_async_copy(out.at[core], out_ref.at[0, core, 0], out_own)

    for q, inverse in ((0, inverse0), (1, inverse1)):
        results(inverse, mixed, rows, out, q)

        @pl.when(core == q)
        def _():
            home.start()

        @pl.when(core != q)
        def _():
            across.start()

    home.wait()
    across.wait()

    @pl.when(has_next)
    def _():
        along.wait_send()

    for copy in crossing:
        copy.wait_send()
    for q in range(2):
        for d in range(1, 5):
            for half in range(2):
                for way in range(2):
                    if exists(way, d, half):
                        ring(q, way, d, half).wait_send()


def sweep(ops, limits, boundaries):
    vmem = pl.BlockSpec(memory_space=pltpu.VMEM)
    anywhere = pl.BlockSpec(memory_space=pl.ANY)
    bf16, f32 = jnp.bfloat16, jnp.float32
    dma = pltpu.SemaphoreType.DMA
    return pl.pallas_call(
        sweep_kernel,
        out_shape=jax.ShapeDtypeStruct(boundaries.shape, bf16),
        in_specs=[vmem, vmem, anywhere],
        out_specs=anywhere,
        scratch_shapes=[
            pltpu.VMEM((2, 8, N, N * N), bf16),
            pltpu.VMEM((2, 8, N, N), bf16),
            pltpu.VMEM((2, 8, 128), f32),
            pltpu.VMEM((N, N * N), f32),
            pltpu.VMEM((2048, 128), f32),
            pltpu.VMEM((2, 1024, 256), bf16),
            pltpu.VMEM((2, 1024, 256), bf16),
            pltpu.VMEM((2, 256, 2048), bf16),
            pltpu.VMEM((2, N, N * N), bf16),
            pltpu.VMEM((N, 128), f32),
            pltpu.VMEM((N, 128), f32),
            pltpu.VMEM((N, 128), f32),
            dma((3,)), dma((3,)), dma((3,)),
            dma((2, 2, 4, 2)), dma((2, 2, 4, 2)),
            dma, dma, dma, dma, dma,
        ],
        compiler_params=pltpu.CompilerParams(
            collective_id=0, has_side_effects=True, vmem_limit_bytes=40 * 1024 * 1024
        ),
    )(ops, limits, boundaries)


def on_device(boundaries, row_ops, ranks):
    my_sector = lax.axis_index("sec")
    ops = lax.dynamic_slice_in_dim(row_ops, my_sector, 1, 3).reshape(2, 8, N, N)
    ops = jnp.swapaxes(ops, 2, 3)
    limits = jnp.broadcast_to(ranks.reshape(2, 1, 1).astype(jnp.float32), (2, 8, 128))
    return sweep(ops, limits, boundaries)


def solution(mesh):
    placed = (
        P("sec", None, "col", None, None),
        P(None, "col", None, None, None, None),
        P("sec", None, "col"),
    )
    return jax.shard_map(
        on_device,
        mesh=mesh,
        in_specs=placed,
        out_specs=P("sec", None, "col", None, None),
        check_vma=False,
    )
```

```python
import functools
import math

import jax
import jax.numpy as jnp
from jax import lax
from jax.experimental import pallas as pl
from jax.experimental.pallas import tpu as pltpu
from jax.sharding import PartitionSpec as P

MESH = pl.DeviceIdType.MESH
N = 64
NT = (((1,), (1,)), ((), ()))
NN = (((1,), (0,)), ((), ()))


def dot(a, b, dims):
    return lax.dot_general(a, b, dims, preferred_element_type=jnp.float32)


def split(x):
    hi = x.astype(jnp.bfloat16)
    lo = (x - hi.astype(jnp.float32)).astype(jnp.bfloat16)
    return hi, lo


WIDE = (8, 128)


def on_lines(x, i):
    return jnp.broadcast_to(x[i : i + 1, :], WIDE)


def on_lanes(x, i):
    return jnp.broadcast_to(x[:, i : i + 1], WIDE)


def factor(g, emit):
    rows = [g[8 * i : 8 * i + 8] for i in range(8)]
    cols = [on_lanes(rows[0], a) for a in range(8)]
    for p in range(8):
        mine, steps, done = rows[p], [], []
        if p < 7:
            beside = [on_lanes(rows[p + 1], 8 * p + a) for a in range(8)]
            ahead = [on_lanes(rows[p + 1], 8 * p + 8 + a) for a in range(8)]
        for a in range(8):
            pivot = on_lines(cols[a], a)
            inverse = 1.0 / pivot
            row = on_lines(mine, a)
            done.append(row[0:1] * lax.rsqrt(pivot[0:1]))
            heads = [on_lines(cols[b], a) if b > a else None for b in range(8)]
            times = cols[a] * inverse
            for b in range(a + 1, 8):
                cols[b] = cols[b] - times * heads[b]
            mine = mine - times * row
            if p < 7:
                times = beside[a] * inverse
                for b in range(a + 1, 8):
                    beside[b] = beside[b] - times * heads[b]
                for b in range(8):
                    ahead[b] = ahead[b] - times * on_lines(beside[a], b)
                rows[p + 1] = rows[p + 1] - times * row
            steps.append((inverse, row, heads))
        for r in range(p + 2, 8):
            below = [on_lanes(rows[r], 8 * p + a) for a in range(8)]
            for a, (inverse, row, heads) in enumerate(steps):
                times = below[a] * inverse
                for b in range(a + 1, 8):
                    below[b] = below[b] - times * heads[b]
                rows[r] = rows[r] - times * row
        emit(p, jnp.concatenate(done, 0))
        if p < 7:
            cols = ahead


def patterns():
    lane = lax.broadcasted_iota(jnp.int32, (N, 128), 1)
    line = lax.broadcasted_iota(jnp.int32, (N, 128), 0)
    low = lane < N
    place = jnp.where(low, lane, lane - N)
    eye = jnp.where(place == line, 1.0, 0.0).astype(jnp.float32)
    return line, low, place, eye


def absorb(ops, blocks, acc, q, sectors, first):
    lhs = [ops[q, s] for s in sectors]

    def tile(n, carry):
        at = pl.ds(pl.multiple_of(n * 512, 512), 512)
        total = dot(lhs[0], blocks[q, sectors[0], :, at], NN)
        for left, s in zip(lhs[1:], sectors[1:]):
            total = total + dot(left, blocks[q, s, :, at], NN)
        acc[:, at] = total if first else acc[:, at] + total
        return carry

    lax.fori_loop(0, 8, tile, 0)


def to_columns(acc, rows, at, q):
    low = lax.broadcasted_iota(jnp.int32, (32, 128), 1) < N
    for m in range(32):
        v = acc[:, 128 * m : 128 * m + 128]
        w = pltpu.roll(v, N, 1)
        rows[pl.ds(2 * m, 32, stride=N), :] = jnp.where(low, v[0:32], w[32:64])
        rows[pl.ds(2 * m + 1, 32, stride=N), :] = jnp.where(low, w[0:32], v[32:64])
    for t in range(16):
        hi, lo = split(rows[128 * t : 128 * t + 128, :].T)
        at[q, 128 * t : 128 * t + 128, 0:128] = hi
        at[q, 128 * t : 128 * t + 128, 128:256] = lo


def advance(left, unit, keep, at, mixed, next_left, inverses, q, begin):
    line, low, place, eye = patterns()
    both = jnp.concatenate([jnp.where(low, left, 0.0), jnp.where(low, 0.0, pltpu.roll(left, N, 1))], 0)
    hi, lo = split(both)
    weights = jnp.concatenate(
        [jnp.concatenate([hi, hi], 1), jnp.concatenate([lo, jnp.zeros_like(lo)], 1)], 0
    )
    for t in range(0, 16, 2):
        o = dot(at[q, 128 * t : 128 * t + 256, :], weights, NT)
        hi, lo = split(o[:, 0:128] + o[:, 128:256])
        for u in range(2):
            lanes = slice(128 * (t + u), 128 * (t + u) + 128)
            mixed[q, 0:128, lanes] = hi[128 * u : 128 * u + 128]
            mixed[q, 128:256, lanes] = lo[128 * u : 128 * u + 128]
    y = mixed[q]
    g = dot(y, y, NT)
    g = g[0:128] + g[128:256]
    g = g[:, 0:128] + g[:, 128:256]
    total = jnp.sum(jnp.where(low, left * left, 0.0), keepdims=True)
    scale = lax.rsqrt(total * (1.0 / (N * N)) + 1e-06)
    scale = jnp.where(unit, jnp.ones_like(scale), scale)
    full = (g[0:N] + pltpu.roll(g[N:], N, 1)) * (scale * scale)

    def emit(p, rows):
        part = slice(8 * p, 8 * p + 8)
        upper = jnp.logical_and(low[part], place[part] >= line[part])
        next_left[part, :] = jnp.where(jnp.logical_and(keep[part], upper), rows, 0.0)
        inverses[q, part, :] = jnp.where(jnp.logical_or(low[part], jnp.logical_not(keep[part])), 0.0, rows) * (scale * float(N))
        if begin is not None:
            begin(p)

    factor(jnp.where(low, full, eye), emit)


def results(inverses, mixed, rows, out, q):
    inverse = inverses[q]
    pair = jnp.concatenate([pltpu.roll(inverse, N, 1), inverse], 0)
    p_hi, p_lo = split(pair)
    wide = jnp.concatenate([p_hi, p_hi], 1)
    for c in range(8):
        y = mixed[q, :, 256 * c : 256 * c + 256]
        o = dot(wide, y, NN) + dot(p_lo, y[0:128], NN)
        rows[256 * c : 256 * c + 128, :] = o[:, 0:128].T
        rows[256 * c + 128 : 256 * c + 256, :] = o[:, 128:256].T
    low = lax.broadcasted_iota(jnp.int32, (32, 128), 1) < N
    for m in range(32):
        e = rows[pl.ds(2 * m, 32, stride=N), :]
        d = rows[pl.ds(2 * m + 1, 32, stride=N), :]
        at = slice(128 * m, 128 * m + 128)
        out[q, 0:32, at] = jnp.where(low, e, pltpu.roll(d, N, 1)).astype(jnp.bfloat16)
        out[q, 32:64, at] = jnp.where(low, pltpu.roll(e, N, 1), d).astype(jnp.bfloat16)


def sweep_kernel(
    ops_ref, limit_ref, bnd_ref, out_ref,
    blocks, ops, limits, acc, rows, at, mixed, out, inverses, l_in, l_out, left_ref,
    part_send, part_recv, own_sem, ring_send, ring_recv, l_send, l_recv, out_send, out_recv, out_own,
):
    me = lax.axis_index("col")
    columns = lax.axis_size("col")
    z = lax.axis_index("sec")
    size = lax.axis_size("sec")
    core = lax.rem(me, 2)
    partner = me + 1 - 2 * core
    up, down = lax.rem(z + 1, size), lax.rem(z + size - 1, size)
    after, before = lax.rem(me + 2, columns), lax.rem(me + columns - 2, columns)
    is_first = me < 2

    barrier = pltpu.get_barrier_semaphore()
    for to in ((partner, z), (me, up), (me, down), (before, z)):
        pl.semaphore_signal(barrier, inc=1, device_id=to, device_id_type=MESH)
    pl.semaphore_wait(barrier, 4)

    def to_partner(n, source, target):
        return pltpu.make_async_remote_copy(
            src_ref=source, dst_ref=target, send_sem=part_send.at[n], recv_sem=part_recv.at[n],
            device_id=(partner, z), device_id_type=MESH,
        )

    crossing = [
        to_partner(0, bnd_ref.at[0, 1 - core, 0], blocks.at[core, z]),
        to_partner(1, ops_ref.at[1 - core], ops.at[core]),
        to_partner(2, limit_ref.at[1 - core], limits.at[core]),
    ]
    staying = [
        pltpu.make_async_copy(bnd_ref.at[0, core, 0], blocks.at[core, z], own_sem.at[0]),
        pltpu.make_async_copy(ops_ref.at[core], ops.at[core], own_sem.at[1]),
        pltpu.make_async_copy(limit_ref.at[core], limits.at[core], own_sem.at[2]),
    ]
    for copy in crossing + staying:
        copy.start()

    def ring(q, way, d, half):
        block = lax.rem(z + size + (d - 1 if way else 1 - d), size)
        part = blocks.at[q, block, 32 * half : 32 * half + 32]
        return pltpu.make_async_remote_copy(
            src_ref=part, dst_ref=part, send_sem=ring_send.at[q, way, d - 1, half], recv_sem=ring_recv.at[q, way, d - 1, half],
            device_id=(me, down if way else up), device_id_type=MESH,
        )

    def exists(way, d, half):
        return d < 4 or (d == 4 and half == way)

    def begin(q):
        @pl.when(core == q)
        def _():
            staying[0].wait()

        @pl.when(core != q)
        def _():
            crossing[0].wait_recv()

        for half in range(2):
            for way in range(2):
                ring(q, way, 1, half).start()

    def turn(q, d):
        for half in range(2):
            for way in range(2):
                if exists(way, d, half):
                    ring(q, way, d, half).wait_recv()
                    if exists(way, d + 1, half):
                        ring(q, way, d + 1, half).start()

    def sectors(d):
        before, after = lax.rem(z + size - d, size), lax.rem(z + d, size)
        return [z] if d == 0 else [after] if d == 4 else [before, after]

    begin(0)
    for copy in staying[1:]:
        copy.wait()
    for copy in crossing[1:]:
        copy.wait_recv()
    for d in range(5):
        if d > 0:
            turn(0, d)
        if d == 3:
            begin(1)
        absorb(ops, blocks, acc, 0, sectors(d), d == 0)
    turn(1, 1)
    to_columns(acc, rows, at, 0)
    absorb(ops, blocks, acc, 1, sectors(0), True)
    absorb(ops, blocks, acc, 1, sectors(1), False)
    for d in range(2, 5):
        turn(1, d)
        absorb(ops, blocks, acc, 1, sectors(d), False)
    to_columns(acc, rows, at, 1)

    line, low, place, eye = patterns()

    def along(part, start, size):
        return pltpu.make_async_remote_copy(
            src_ref=l_out.at[start : start + size], dst_ref=l_in.at[start : start + size],
            send_sem=l_send.at[part], recv_sem=l_recv.at[part], device_id=(after, z), device_id_type=MESH,
        )

    pieces = {5: along(0, 0, 48), 7: along(1, 48, 16)}

    @pl.when(is_first)
    def _():
        left_ref[...] = eye

    @pl.when(jnp.logical_not(is_first))
    def _():
        for piece in pieces.values():
            piece.wait_recv()
        left_ref[...] = l_in[...]

    def keep(q):
        return line.astype(jnp.float32) < limits[q, 0:1, :]

    def begin_piece(p):
        if p in pieces:
            pieces[p].start()

    advance(left_ref[...], is_first, keep(0), at, mixed, left_ref, inverses, 0, None)
    advance(left_ref[...], False, keep(1), at, mixed, l_out, inverses, 1, begin_piece)

    across = pltpu.make_async_remote_copy(
        src_ref=out.at[1 - core], dst_ref=out_ref.at[0, core, 0], send_sem=out_send, recv_sem=out_recv,
        device_id=(partner, z), device_id_type=MESH,
    )
    home = pltpu.make_async_copy(out.at[core], out_ref.at[0, core, 0], out_own)

    for q in range(2):
        results(inverses, mixed, rows, out, q)

        @pl.when(core == q)
        def _():
            home.start()

        @pl.when(core != q)
        def _():
            across.start()

    home.wait()
    across.wait()

    for piece in pieces.values():
        piece.wait_send()

    @pl.when(is_first)
    def _():
        for piece in pieces.values():
            piece.wait_recv()

    for copy in crossing:
        copy.wait_send()
    for q in range(2):
        for d in range(1, 5):
            for half in range(2):
                for way in range(2):
                    if exists(way, d, half):
                        ring(q, way, d, half).wait_send()


def sweep(ops, limits, boundaries):
    vmem = pl.BlockSpec(memory_space=pltpu.VMEM)
    anywhere = pl.BlockSpec(memory_space=pl.ANY)
    bf16, f32 = jnp.bfloat16, jnp.float32
    dma = pltpu.SemaphoreType.DMA
    return pl.pallas_call(
        sweep_kernel,
        out_shape=jax.ShapeDtypeStruct(boundaries.shape, bf16),
        in_specs=[vmem, vmem, anywhere],
        out_specs=anywhere,
        scratch_shapes=[
            pltpu.VMEM((2, 8, N, N * N), bf16),
            pltpu.VMEM((2, 8, N, N), bf16),
            pltpu.VMEM((2, 8, 128), f32),
            pltpu.VMEM((N, N * N), f32),
            pltpu.VMEM((2048, 128), f32),
            pltpu.VMEM((2, 2048, 256), bf16),
            pltpu.VMEM((2, 256, 2048), bf16),
            pltpu.VMEM((2, N, N * N), bf16),
            pltpu.VMEM((2, N, 128), f32),
            pltpu.VMEM((N, 128), f32),
            pltpu.VMEM((N, 128), f32),
            pltpu.VMEM((N, 128), f32),
            dma((3,)), dma((3,)), dma((3,)),
            dma((2, 2, 4, 2)), dma((2, 2, 4, 2)),
            dma((2,)), dma((2,)), dma, dma, dma,
        ],
        compiler_params=pltpu.CompilerParams(
            collective_id=0, has_side_effects=True, vmem_limit_bytes=40 * 1024 * 1024
        ),
    )(ops, limits, boundaries)


def on_device(boundaries, row_ops, ranks):
    my_sector = lax.axis_index("sec")
    ops = lax.dynamic_slice_in_dim(row_ops, my_sector, 1, 3).reshape(2, 8, N, N)
    ops = jnp.swapaxes(ops, 2, 3)
    limits = jnp.broadcast_to(ranks.reshape(2, 1, 1).astype(jnp.float32), (2, 8, 128))
    return sweep(ops, limits, boundaries)


def solution(mesh):
    placed = (
        P("sec", None, "col", None, None),
        P(None, "col", None, None, None, None),
        P("sec", None, "col"),
    )
    return jax.shard_map(
        on_device,
        mesh=mesh,
        in_specs=placed,
        out_specs=P("sec", None, "col", None, None),
        check_vma=False,
    )
```

```python
import functools
import math

import jax
import jax.numpy as jnp
from jax import lax
from jax.experimental import pallas as pl
from jax.experimental.pallas import tpu as pltpu
from jax.sharding import PartitionSpec as P

MESH = pl.DeviceIdType.MESH
N = 64
OWN = 1408
NT = (((1,), (1,)), ((), ()))
NN = (((1,), (0,)), ((), ()))


def dot(a, b, dims):
    return lax.dot_general(a, b, dims, preferred_element_type=jnp.float32)


def split(x):
    hi = x.astype(jnp.bfloat16)
    lo = (x - hi.astype(jnp.float32)).astype(jnp.bfloat16)
    return hi, lo


WIDE = (8, 128)


def on_lines(x, i):
    return jnp.broadcast_to(x[i : i + 1, :], WIDE)


def on_lanes(x, i):
    return jnp.broadcast_to(x[:, i : i + 1], WIDE)


def factor(g, emit):
    rows = [g[8 * i : 8 * i + 8] for i in range(8)]
    cols = [on_lanes(rows[0], a) for a in range(8)]
    for p in range(8):
        mine, steps, done = rows[p], [], []
        if p < 7:
            beside = [on_lanes(rows[p + 1], 8 * p + a) for a in range(8)]
            ahead = [on_lanes(rows[p + 1], 8 * p + 8 + a) for a in range(8)]
        for a in range(8):
            pivot = on_lines(cols[a], a)
            inverse = 1.0 / pivot
            row = on_lines(mine, a)
            done.append(row[0:1] * lax.rsqrt(pivot[0:1]))
            heads = [on_lines(cols[b], a) if b > a else None for b in range(8)]
            times = cols[a] * inverse
            for b in range(a + 1, 8):
                cols[b] = cols[b] - times * heads[b]
            mine = mine - times * row
            if p < 7:
                times = beside[a] * inverse
                for b in range(a + 1, 8):
                    beside[b] = beside[b] - times * heads[b]
                for b in range(8):
                    ahead[b] = ahead[b] - times * on_lines(beside[a], b)
                rows[p + 1] = rows[p + 1] - times * row
            steps.append((inverse, row, heads))
        for r in range(p + 2, 8):
            below = [on_lanes(rows[r], 8 * p + a) for a in range(8)]
            for a, (inverse, row, heads) in enumerate(steps):
                times = below[a] * inverse
                for b in range(a + 1, 8):
                    below[b] = below[b] - times * heads[b]
                rows[r] = rows[r] - times * row
        emit(p, jnp.concatenate(done, 0))
        if p < 7:
            cols = ahead


def patterns():
    lane = lax.broadcasted_iota(jnp.int32, (N, 128), 1)
    line = lax.broadcasted_iota(jnp.int32, (N, 128), 0)
    low = lane < N
    place = jnp.where(low, lane, lane - N)
    eye = jnp.where(place == line, 1.0, 0.0).astype(jnp.float32)
    return line, low, place, eye


def absorb(ops, blocks, acc, q, sectors, first):
    lhs = [ops[q, s] for s in sectors]

    def tile(n, carry):
        at = pl.ds(pl.multiple_of(n * 512, 512), 512)
        total = dot(lhs[0], blocks[q, sectors[0], :, at], NN)
        for left, s in zip(lhs[1:], sectors[1:]):
            total = total + dot(left, blocks[q, s, :, at], NN)
        acc[:, at] = total if first else acc[:, at] + total
        return carry

    lax.fori_loop(0, 8, tile, 0)


def to_columns(acc, rows, at, q):
    low = lax.broadcasted_iota(jnp.int32, (32, 128), 1) < N
    for m in range(32):
        v = acc[:, 128 * m : 128 * m + 128]
        w = pltpu.roll(v, N, 1)
        rows[pl.ds(2 * m, 32, stride=N), :] = jnp.where(low, v[0:32], w[32:64])
        rows[pl.ds(2 * m + 1, 32, stride=N), :] = jnp.where(low, w[0:32], v[32:64])
    for t in range(16):
        hi, lo = split(rows[128 * t : 128 * t + 128, :].T)
        at[q, 128 * t : 128 * t + 128, 0:128] = hi
        at[q, 128 * t : 128 * t + 128, 128:256] = lo


def advance(left, unit, keep, at, mixed, next_left, inverses, q, begin):
    line, low, place, eye = patterns()
    both = jnp.concatenate([jnp.where(low, left, 0.0), jnp.where(low, 0.0, pltpu.roll(left, N, 1))], 0)
    hi, lo = split(both)
    weights = jnp.concatenate(
        [jnp.concatenate([hi, hi], 1), jnp.concatenate([lo, jnp.zeros_like(lo)], 1)], 0
    )
    for t in range(0, 16, 2):
        o = dot(at[q, 128 * t : 128 * t + 256, :], weights, NT)
        hi, lo = split(o[:, 0:128] + o[:, 128:256])
        for u in range(2):
            lanes = slice(128 * (t + u), 128 * (t + u) + 128)
            mixed[q, 0:128, lanes] = hi[128 * u : 128 * u + 128]
            mixed[q, 128:256, lanes] = lo[128 * u : 128 * u + 128]
    y = mixed[q]
    g = dot(y, y, NT)
    g = g[0:128] + g[128:256]
    g = g[:, 0:128] + g[:, 128:256]
    total = jnp.sum(jnp.where(low, left * left, 0.0), keepdims=True)
    scale = lax.rsqrt(total * (1.0 / (N * N)) + 1e-06)
    scale = jnp.where(unit, jnp.ones_like(scale), scale)
    full = (g[0:N] + pltpu.roll(g[N:], N, 1)) * (scale * scale)

    def emit(p, rows):
        part = slice(8 * p, 8 * p + 8)
        upper = jnp.logical_and(low[part], place[part] >= line[part])
        next_left[part, :] = jnp.where(jnp.logical_and(keep[part], upper), rows, 0.0)
        inverses[q, part, :] = jnp.where(jnp.logical_or(low[part], jnp.logical_not(keep[part])), 0.0, rows) * (scale * float(N))
        if begin is not None:
            begin(p)

    factor(jnp.where(low, full, eye), emit)


def results(inverses, mixed, rows, out, q):
    inverse = inverses[q]
    pair = jnp.concatenate([pltpu.roll(inverse, N, 1), inverse], 0)
    p_hi, p_lo = split(pair)
    wide = jnp.concatenate([p_hi, p_hi], 1)
    for c in range(8):
        y = mixed[q, :, 256 * c : 256 * c + 256]
        o = dot(wide, y, NN) + dot(p_lo, y[0:128], NN)
        rows[256 * c : 256 * c + 128, :] = o[:, 0:128].T
        rows[256 * c + 128 : 256 * c + 256, :] = o[:, 128:256].T
    low = lax.broadcasted_iota(jnp.int32, (32, 128), 1) < N
    for m in range(32):
        e = rows[pl.ds(2 * m, 32, stride=N), :]
        d = rows[pl.ds(2 * m + 1, 32, stride=N), :]
        at = slice(128 * m, 128 * m + 128)
        out[q, 0:32, at] = jnp.where(low, e, pltpu.roll(d, N, 1)).astype(jnp.bfloat16)
        out[q, 32:64, at] = jnp.where(low, pltpu.roll(e, N, 1), d).astype(jnp.bfloat16)


def sweep_kernel(
    ops_ref, limit_ref, bnd_ref, out_ref,
    blocks, ops, limits, acc, rows, at, mixed, out, inverses, l_in, l_out, left_ref,
    guests, part_send, part_recv, own_sem, ring_send, ring_recv, l_send, l_recv, out_send, out_recv, out_own,
    gift_send, gift_recv, back_send, back_recv,
):
    me = lax.axis_index("col")
    columns = lax.axis_size("col")
    z = lax.axis_index("sec")
    size = lax.axis_size("sec")
    core = lax.rem(me, 2)
    partner = me + 1 - 2 * core
    up, down = lax.rem(z + 1, size), lax.rem(z + size - 1, size)
    after, before = lax.rem(me + 2, columns), lax.rem(me + columns - 2, columns)
    is_first = me < 2
    band = columns // 4
    row = me // band
    is_early, is_helper = row == 0, row == 3
    peer = me + band * (3 - 2 * row)

    barrier = pltpu.get_barrier_semaphore()
    for to in ((partner, z), (me, up), (me, down), (before, z), (peer, z)):
        pl.semaphore_signal(barrier, inc=1, device_id=to, device_id_type=MESH)
    pl.semaphore_wait(barrier, 5)

    def to_partner(n, source, target):
        return pltpu.make_async_remote_copy(
            src_ref=source, dst_ref=target, send_sem=part_send.at[n], recv_sem=part_recv.at[n],
            device_id=(partner, z), device_id_type=MESH,
        )

    crossing = [
        to_partner(0, bnd_ref.at[0, 1 - core, 0], blocks.at[core, z]),
        to_partner(1, ops_ref.at[1 - core], ops.at[core]),
        to_partner(2, limit_ref.at[1 - core], limits.at[core]),
    ]
    staying = [
        pltpu.make_async_copy(bnd_ref.at[0, core, 0], blocks.at[core, z], own_sem.at[0]),
        pltpu.make_async_copy(ops_ref.at[core], ops.at[core], own_sem.at[1]),
        pltpu.make_async_copy(limit_ref.at[core], limits.at[core], own_sem.at[2]),
    ]
    for copy in crossing + staying:
        copy.start()

    def ring(flow, way, d, half):
        block = lax.rem(z + size + (d - 1 if way else 1 - d), size)
        lines = slice(32 * half, 32 * half + 32)
        if flow == 0:
            part = blocks.at[0, block, lines]
        elif flow == 1:
            part = blocks.at[1, block, lines, 0:OWN]
        elif flow == 2:
            part = blocks.at[1, block, lines, OWN : N * N]
        else:
            part = guests.at[block, lines]
        return pltpu.make_async_remote_copy(
            src_ref=part, dst_ref=part, send_sem=ring_send.at[flow, way, d - 1, half],
            recv_sem=ring_recv.at[flow, way, d - 1, half],
            device_id=(me, down if way else up), device_id_type=MESH,
        )

    def gift(half):
        lines = slice(32 * half, 32 * half + 32)
        return pltpu.make_async_remote_copy(
            src_ref=blocks.at[1, z, lines, OWN : N * N], dst_ref=guests.at[z, lines],
            send_sem=gift_send.at[half], recv_sem=gift_recv.at[half], device_id=(peer, z), device_id_type=MESH,
        )

    def back(way, d, half):
        block = lax.rem(z + size + (d if way else -d), size)
        lines = slice(32 * half, 32 * half + 32)
        return pltpu.make_async_remote_copy(
            src_ref=guests.at[block, lines], dst_ref=blocks.at[1, block, lines, OWN : N * N],
            send_sem=back_send.at[way, d - 1, half], recv_sem=back_recv.at[way, d - 1, half],
            device_id=(peer, z), device_id_type=MESH,
        )

    def parts(d):
        return [(way, d, half) for half in range(2) for way in range(2) if d < 4 or half == way]

    def ready(q):
        @pl.when(core == q)
        def _():
            staying[0].wait()

        @pl.when(core != q)
        def _():
            crossing[0].wait_recv()

    def begin(flow):
        for part in parts(1):
            ring(flow, *part).start()

    def turn(flow, d, then=None):
        for way, _, half in parts(d):
            ring(flow, way, d, half).wait_recv()
            if (way, d + 1, half) in parts(d + 1) and d < 4:
                ring(flow, way, d + 1, half).start()
            if then is not None:
                then(way, d, half).start()

    def turn_second(d):
        turn(1, d)

        @pl.when(is_early)
        def _():
            for part in parts(d):
                back(*part).wait_recv()

        @pl.when(jnp.logical_not(is_early))
        def _():
            turn(2, d)

    def sectors(d):
        before, after = lax.rem(z + size - d, size), lax.rem(z + d, size)
        return [z] if d == 0 else [after] if d == 4 else [before, after]

    @pl.when(is_helper)
    def _():
        for half in range(2):
            gift(half).wait_recv()
            for way in range(2):
                ring(3, way, 1, half).start()
        for d in range(1, 5):
            turn(3, d, back)

    ready(0)
    begin(0)
    ready(1)

    @pl.when(is_early)
    def _():
        for half in range(2):
            gift(half).start()

    for copy in staying[1:]:
        copy.wait()
    for copy in crossing[1:]:
        copy.wait_recv()
    for d in range(5):
        if d > 0:
            turn(0, d)
        if d == 3:
            begin(1)

            @pl.when(jnp.logical_not(is_early))
            def _():
                begin(2)

        absorb(ops, blocks, acc, 0, sectors(d), d == 0)
    turn_second(1)
    to_columns(acc, rows, at, 0)
    absorb(ops, blocks, acc, 1, sectors(0), True)
    absorb(ops, blocks, acc, 1, sectors(1), False)
    for d in range(2, 5):
        turn_second(d)
        absorb(ops, blocks, acc, 1, sectors(d), False)
    to_columns(acc, rows, at, 1)

    line, low, place, eye = patterns()

    def along(part, start, size):
        return pltpu.make_async_remote_copy(
            src_ref=l_out.at[start : start + size], dst_ref=l_in.at[start : start + size],
            send_sem=l_send.at[part], recv_sem=l_recv.at[part], device_id=(after, z), device_id_type=MESH,
        )

    pieces = {5: along(0, 0, 48), 7: along(1, 48, 16)}

    @pl.when(is_first)
    def _():
        left_ref[...] = eye

    @pl.when(jnp.logical_not(is_first))
    def _():
        for piece in pieces.values():
            piece.wait_recv()
        left_ref[...] = l_in[...]

    def keep(q):
        return line.astype(jnp.float32) < limits[q, 0:1, :]

    def begin_piece(p):
        if p in pieces:
            pieces[p].start()

    advance(left_ref[...], is_first, keep(0), at, mixed, left_ref, inverses, 0, None)
    advance(left_ref[...], False, keep(1), at, mixed, l_out, inverses, 1, begin_piece)

    across = pltpu.make_async_remote_copy(
        src_ref=out.at[1 - core], dst_ref=out_ref.at[0, core, 0], send_sem=out_send, recv_sem=out_recv,
        device_id=(partner, z), device_id_type=MESH,
    )
    home = pltpu.make_async_copy(out.at[core], out_ref.at[0, core, 0], out_own)

    for q in range(2):
        results(inverses, mixed, rows, out, q)

        @pl.when(core == q)
        def _():
            home.start()

        @pl.when(core != q)
        def _():
            across.start()

    home.wait()
    across.wait()

    for piece in pieces.values():
        piece.wait_send()

    @pl.when(is_first)
    def _():
        for piece in pieces.values():
            piece.wait_recv()

    for copy in crossing:
        copy.wait_send()
    every = [part for d in range(1, 5) for part in parts(d)]
    for part in every:
        ring(0, *part).wait_send()
        ring(1, *part).wait_send()

    @pl.when(is_early)
    def _():
        for half in range(2):
            gift(half).wait_send()

    @pl.when(jnp.logical_not(is_early))
    def _():
        for part in every:
            ring(2, *part).wait_send()

    @pl.when(is_helper)
    def _():
        for part in every:
            ring(3, *part).wait_send()
            back(*part).wait_send()


def sweep(ops, limits, boundaries):
    vmem = pl.BlockSpec(memory_space=pltpu.VMEM)
    anywhere = pl.BlockSpec(memory_space=pl.ANY)
    bf16, f32 = jnp.bfloat16, jnp.float32
    dma = pltpu.SemaphoreType.DMA
    return pl.pallas_call(
        sweep_kernel,
        out_shape=jax.ShapeDtypeStruct(boundaries.shape, bf16),
        in_specs=[vmem, vmem, anywhere],
        out_specs=anywhere,
        scratch_shapes=[
            pltpu.VMEM((2, 8, N, N * N), bf16),
            pltpu.VMEM((2, 8, N, N), bf16),
            pltpu.VMEM((2, 8, 128), f32),
            pltpu.VMEM((N, N * N), f32),
            pltpu.VMEM((2048, 128), f32),
            pltpu.VMEM((2, 2048, 256), bf16),
            pltpu.VMEM((2, 256, 2048), bf16),
            pltpu.VMEM((2, N, N * N), bf16),
            pltpu.VMEM((2, N, 128), f32),
            pltpu.VMEM((N, 128), f32),
            pltpu.VMEM((N, 128), f32),
            pltpu.VMEM((N, 128), f32),
            pltpu.VMEM((8, N, N * N - OWN), bf16),
            dma((3,)), dma((3,)), dma((3,)),
            dma((4, 2, 4, 2)), dma((4, 2, 4, 2)),
            dma((2,)), dma((2,)), dma, dma, dma,
            dma((2,)), dma((2,)), dma((2, 4, 2)), dma((2, 4, 2)),
        ],
        compiler_params=pltpu.CompilerParams(
            collective_id=0, has_side_effects=True, vmem_limit_bytes=40 * 1024 * 1024
        ),
    )(ops, limits, boundaries)


def on_device(boundaries, row_ops, ranks):
    my_sector = lax.axis_index("sec")
    ops = lax.dynamic_slice_in_dim(row_ops, my_sector, 1, 3).reshape(2, 8, N, N)
    ops = jnp.swapaxes(ops, 2, 3)
    limits = jnp.broadcast_to(ranks.reshape(2, 1, 1).astype(jnp.float32), (2, 8, 128))
    return sweep(ops, limits, boundaries)


def solution(mesh):
    placed = (
        P("sec", None, "col", None, None),
        P(None, "col", None, None, None, None),
        P("sec", None, "col"),
    )
    return jax.shard_map(
        on_device,
        mesh=mesh,
        in_specs=placed,
        out_specs=P("sec", None, "col", None, None),
        check_vma=False,
    )
```

```python
import functools
import math

import jax
import jax.numpy as jnp
from jax import lax
from jax.experimental import pallas as pl
from jax.experimental.pallas import tpu as pltpu
from jax.sharding import PartitionSpec as P

MESH = pl.DeviceIdType.MESH
N = 64
OWN = 512
CHUNK = 896
MIDDLE = OWN + 2 * CHUNK
NT = (((1,), (1,)), ((), ()))
NN = (((1,), (0,)), ((), ()))


def dot(a, b, dims):
    return lax.dot_general(a, b, dims, preferred_element_type=jnp.float32)


def split(x):
    hi = x.astype(jnp.bfloat16)
    lo = (x - hi.astype(jnp.float32)).astype(jnp.bfloat16)
    return hi, lo


WIDE = (8, 128)


def on_lines(x, i):
    return jnp.broadcast_to(x[i : i + 1, :], WIDE)


def on_lanes(x, i):
    return jnp.broadcast_to(x[:, i : i + 1], WIDE)


def factor(g, emit):
    rows = [g[8 * i : 8 * i + 8] for i in range(8)]
    cols = [on_lanes(rows[0], a) for a in range(8)]
    for p in range(8):
        mine, steps, done = rows[p], [], []
        if p < 7:
            beside = [on_lanes(rows[p + 1], 8 * p + a) for a in range(8)]
            ahead = [on_lanes(rows[p + 1], 8 * p + 8 + a) for a in range(8)]
        for a in range(8):
            pivot = on_lines(cols[a], a)
            inverse = 1.0 / pivot
            row = on_lines(mine, a)
            done.append(row[0:1] * lax.rsqrt(pivot[0:1]))
            heads = [on_lines(cols[b], a) if b > a else None for b in range(8)]
            times = cols[a] * inverse
            for b in range(a + 1, 8):
                cols[b] = cols[b] - times * heads[b]
            mine = mine - times * row
            if p < 7:
                times = beside[a] * inverse
                for b in range(a + 1, 8):
                    beside[b] = beside[b] - times * heads[b]
                for b in range(8):
                    ahead[b] = ahead[b] - times * on_lines(beside[a], b)
                rows[p + 1] = rows[p + 1] - times * row
            steps.append((inverse, row, heads))
        for r in range(p + 2, 8):
            below = [on_lanes(rows[r], 8 * p + a) for a in range(8)]
            for a, (inverse, row, heads) in enumerate(steps):
                times = below[a] * inverse
                for b in range(a + 1, 8):
                    below[b] = below[b] - times * heads[b]
                rows[r] = rows[r] - times * row
        emit(p, jnp.concatenate(done, 0))
        if p < 7:
            cols = ahead


def patterns():
    lane = lax.broadcasted_iota(jnp.int32, (N, 128), 1)
    line = lax.broadcasted_iota(jnp.int32, (N, 128), 0)
    low = lane < N
    place = jnp.where(low, lane, lane - N)
    eye = jnp.where(place == line, 1.0, 0.0).astype(jnp.float32)
    return line, low, place, eye


def absorb(lefts, rights, acc, start, width, tiles, first):
    def tile(n, carry):
        at = pl.ds(pl.multiple_of(start + n * width, 128), width)
        total = sum(dot(left, right[:, at], NN) for left, right in zip(lefts, rights))
        acc[:, at] = total if first else acc[:, at] + total
        return carry

    if tiles == 1:
        tile(0, 0)
    else:
        lax.fori_loop(0, tiles, tile, 0)


def to_columns(acc, rows, at, q):
    low = lax.broadcasted_iota(jnp.int32, (32, 128), 1) < N
    for m in range(32):
        v = acc[:, 128 * m : 128 * m + 128]
        w = pltpu.roll(v, N, 1)
        rows[pl.ds(2 * m, 32, stride=N), :] = jnp.where(low, v[0:32], w[32:64])
        rows[pl.ds(2 * m + 1, 32, stride=N), :] = jnp.where(low, w[0:32], v[32:64])
    for t in range(16):
        hi, lo = split(rows[128 * t : 128 * t + 128, :].T)
        at[q, 128 * t : 128 * t + 128, 0:128] = hi
        at[q, 128 * t : 128 * t + 128, 128:256] = lo


def advance(left, unit, keep, at, mixed, next_left, inverses, q, begin):
    line, low, place, eye = patterns()
    both = jnp.concatenate([jnp.where(low, left, 0.0), jnp.where(low, 0.0, pltpu.roll(left, N, 1))], 0)
    hi, lo = split(both)
    weights = jnp.concatenate(
        [jnp.concatenate([hi, hi], 1), jnp.concatenate([lo, jnp.zeros_like(lo)], 1)], 0
    )
    for t in range(0, 16, 2):
        o = dot(at[q, 128 * t : 128 * t + 256, :], weights, NT)
        hi, lo = split(o[:, 0:128] + o[:, 128:256])
        for u in range(2):
            lanes = slice(128 * (t + u), 128 * (t + u) + 128)
            mixed[q, 0:128, lanes] = hi[128 * u : 128 * u + 128]
            mixed[q, 128:256, lanes] = lo[128 * u : 128 * u + 128]
    y = mixed[q]
    g = dot(y, y, NT)
    g = g[0:128] + g[128:256]
    g = g[:, 0:128] + g[:, 128:256]
    total = jnp.sum(jnp.where(low, left * left, 0.0), keepdims=True)
    scale = lax.rsqrt(total * (1.0 / (N * N)) + 1e-06)
    scale = jnp.ones_like(scale) if unit else scale
    full = (g[0:N] + pltpu.roll(g[N:], N, 1)) * (scale * scale)

    def emit(p, rows):
        part = slice(8 * p, 8 * p + 8)
        upper = jnp.logical_and(low[part], place[part] >= line[part])
        next_left[part, :] = jnp.where(jnp.logical_and(keep[part], upper), rows, 0.0)
        inverses[q, part, :] = jnp.where(jnp.logical_or(low[part], jnp.logical_not(keep[part])), 0.0, rows) * (scale * float(N))
        if begin is not None:
            begin(p)

    factor(jnp.where(low, full, eye), emit)


def results(inverses, mixed, rows, out, q):
    inverse = inverses[q]
    pair = jnp.concatenate([pltpu.roll(inverse, N, 1), inverse], 0)
    p_hi, p_lo = split(pair)
    wide = jnp.concatenate([p_hi, p_hi], 1)
    for c in range(8):
        y = mixed[q, :, 256 * c : 256 * c + 256]
        o = dot(wide, y, NN) + dot(p_lo, y[0:128], NN)
        rows[256 * c : 256 * c + 128, :] = o[:, 0:128].T
        rows[256 * c + 128 : 256 * c + 256, :] = o[:, 128:256].T
    low = lax.broadcasted_iota(jnp.int32, (32, 128), 1) < N
    for m in range(32):
        e = rows[pl.ds(2 * m, 32, stride=N), :]
        d = rows[pl.ds(2 * m + 1, 32, stride=N), :]
        at = slice(128 * m, 128 * m + 128)
        out[q, 0:32, at] = jnp.where(low, e, pltpu.roll(d, N, 1)).astype(jnp.bfloat16)
        out[q, 32:64, at] = jnp.where(low, pltpu.roll(e, N, 1), d).astype(jnp.bfloat16)


def sweep_kernel(
    ops_ref, limit_ref, bnd_ref, out_ref,
    blocks, ops, limits, acc, second, rows, at, mixed, out, inverses, l_in, l_out, left_ref,
    guests, guest_ops, guest_sums, part_send, part_recv, own_sem, ring_send, ring_recv, l_send, l_recv, out_send, out_recv, out_own,
    gift_send, gift_recv, back_send, back_recv, lent_send, lent_recv,
):
    me = lax.axis_index("col")
    columns = lax.axis_size("col")
    z = lax.axis_index("sec")
    size = lax.axis_size("sec")
    core = lax.rem(me, 2)
    partner = me + 1 - 2 * core
    up, down = lax.rem(z + 1, size), lax.rem(z + size - 1, size)
    after, before = lax.rem(me + 2, columns), lax.rem(me + columns - 2, columns)
    is_first = me < 2
    band = columns // 4
    row = me // band
    peer = me + band * (3 - 2 * row)

    barrier = pltpu.get_barrier_semaphore()
    for to in ((partner, z), (me, up), (me, down), (before, z), (peer, z)):
        pl.semaphore_signal(barrier, inc=1, device_id=to, device_id_type=MESH)
    pl.semaphore_wait(barrier, 5)

    def to_partner(n, source, target):
        return pltpu.make_async_remote_copy(
            src_ref=source, dst_ref=target, send_sem=part_send.at[n], recv_sem=part_recv.at[n],
            device_id=(partner, z), device_id_type=MESH,
        )

    crossing = [
        to_partner(0, bnd_ref.at[0, 1 - core, 0], blocks.at[core, z]),
        to_partner(1, ops_ref.at[1 - core], ops.at[core]),
        to_partner(2, limit_ref.at[1 - core], limits.at[core]),
    ]
    staying = [
        pltpu.make_async_copy(bnd_ref.at[0, core, 0], blocks.at[core, z], own_sem.at[0]),
        pltpu.make_async_copy(ops_ref.at[core], ops.at[core], own_sem.at[1]),
        pltpu.make_async_copy(limit_ref.at[core], limits.at[core], own_sem.at[2]),
    ]
    for copy in crossing + staying:
        copy.start()

    edges = {1: (0, OWN), 2: (OWN, MIDDLE), 3: (MIDDLE, N * N)}

    def chunk(c):
        return slice(CHUNK * c, CHUNK * c + CHUNK)

    def far_chunk(c):
        return slice(OWN + CHUNK * c, OWN + CHUNK * c + CHUNK)

    def ring(flow, way, d, half):
        block = lax.rem(z + size + (d - 1 if way else 1 - d), size)
        lines = slice(32 * half, 32 * half + 32)
        if flow == 0:
            part = blocks.at[0, block, lines]
        elif flow < 4:
            part = blocks.at[1, block, lines, edges[flow][0] : edges[flow][1]]
        else:
            part = guests.at[block, lines, chunk(flow - 4)]
        return pltpu.make_async_remote_copy(
            src_ref=part, dst_ref=part, send_sem=ring_send.at[flow, way, d - 1, half],
            recv_sem=ring_recv.at[flow, way, d - 1, half],
            device_id=(me, down if way else up), device_id_type=MESH,
        )

    def gift(c, half):
        lines = slice(32 * half, 32 * half + 32)
        return pltpu.make_async_remote_copy(
            src_ref=blocks.at[1, z, lines, far_chunk(c)], dst_ref=guests.at[z, lines, chunk(c)],
            send_sem=gift_send.at[c, half], recv_sem=gift_recv.at[c, half],
            device_id=(peer, z), device_id_type=MESH,
        )

    lent = pltpu.make_async_remote_copy(
        src_ref=ops.at[1], dst_ref=guest_ops, send_sem=lent_send, recv_sem=lent_recv,
        device_id=(peer, z), device_id_type=MESH,
    )

    def back(c):
        return pltpu.make_async_remote_copy(
            src_ref=guest_sums.at[:, chunk(c)], dst_ref=second.at[:, far_chunk(c)],
            send_sem=back_send.at[c], recv_sem=back_recv.at[c], device_id=(peer, z), device_id_type=MESH,
        )

    def parts(d):
        return [(way, d, half) for half in range(2) for way in range(2) if d < 4 or half == way]

    def ready(q):
        @pl.when(core == q)
        def _():
            staying[0].wait()

        @pl.when(core != q)
        def _():
            crossing[0].wait_recv()

    def begin(flow):
        for part in parts(1):
            ring(flow, *part).start()

    def turn(flow, d):
        for way, _, half in parts(d):
            ring(flow, way, d, half).wait_recv()
            if d < 4 and (way, d + 1, half) in parts(d + 1):
                ring(flow, way, d + 1, half).start()

    def sectors(d):
        before, after = lax.rem(z + size - d, size), lax.rem(z + d, size)
        return [z] if d == 0 else [after] if d == 4 else [before, after]

    def absorb_flow(flow, d):
        q = 0 if flow == 0 else 1
        start, width, tiles = {0: (0, 512, 8), 1: (0, 512, 1), 2: (OWN, 256, 7), 3: (MIDDLE, 256, 7)}[flow]
        absorb(
            [ops[q, s] for s in sectors(d)], [blocks.at[q, s] for s in sectors(d)],
            second if q else acc, start, width, tiles, d == 0,
        )

    def open_guest(c):
        for half in range(2):
            gift(c, half).wait_recv()
            for way in range(2):
                ring(4 + c, way, 1, half).start()

    def serve(c, then):
        for d in range(1, 5):
            turn(4 + c, d)
            if d == 3:
                then()
        if c == 0:
            lent.wait_recv()
        lefts = [guest_ops[s] for s in range(8)]
        rights = [guests.at[s] for s in range(8)]
        for start, width in ((0, 256), (256, 256), (512, 256), (768, 128)):
            absorb(lefts, rights, guest_sums, CHUNK * c + start, width, 1, True)
        back(c).start()

    def if_last_row(do):
        def run():
            @pl.when(row == 3)
            def _():
                do()

        return run

    def nothing():
        pass

    @pl.when(row >= 2)
    def _():
        open_guest(0)
        serve(0, lambda: open_guest(1))
        serve(1, if_last_row(lambda: open_guest(2)))

    @pl.when(row == 3)
    def _():
        serve(2, lambda: open_guest(3))
        serve(3, nothing)

    ready(0)
    begin(0)
    ready(1)

    @pl.when(row < 2)
    def _():
        for c in range(2):
            for half in range(2):
                gift(c, half).start()

    @pl.when(row == 0)
    def _():
        for c in range(2, 4):
            for half in range(2):
                gift(c, half).start()

    for copy in staying[1:]:
        copy.wait()
    for copy in crossing[1:]:
        copy.wait_recv()

    @pl.when(row < 2)
    def _():
        lent.start()

    for d in range(5):
        if d > 0:
            turn(0, d)
        if d == 3:
            begin(1)

            @pl.when(row >= 2)
            def _():
                begin(2)

            @pl.when(row >= 1)
            def _():
                begin(3)

        absorb_flow(0, d)
    for d in range(5):
        if d > 0:
            turn(1, d)
        if d == 1:
            to_columns(acc, rows, at, 0)
        absorb_flow(1, d)

        @pl.when(row >= 2)
        def _():
            if d > 0:
                turn(2, d)
            absorb_flow(2, d)

        @pl.when(row >= 1)
        def _():
            if d > 0:
                turn(3, d)
            absorb_flow(3, d)

    line, low, place, eye = patterns()

    def along(part, start, size):
        return pltpu.make_async_remote_copy(
            src_ref=l_out.at[start : start + size], dst_ref=l_in.at[start : start + size],
            send_sem=l_send.at[part], recv_sem=l_recv.at[part], device_id=(after, z), device_id_type=MESH,
        )

    pieces = {3: along(0, 0, 32), 5: along(1, 32, 16), 6: along(2, 48, 8), 7: along(3, 56, 8)}

    def keep(q):
        return line.astype(jnp.float32) < limits[q, 0:1, :]

    def begin_piece(p):
        if p in pieces:
            pieces[p].start()

    @pl.when(is_first)
    def _():
        advance(eye, True, keep(0), at, mixed, left_ref, inverses, 0, None)

    @pl.when(row < 2)
    def _():
        for c in range(2):
            back(c).wait_recv()

    @pl.when(row == 0)
    def _():
        for c in range(2, 4):
            back(c).wait_recv()

    to_columns(second, rows, at, 1)

    @pl.when(jnp.logical_not(is_first))
    def _():
        for piece in pieces.values():
            piece.wait_recv()
        advance(l_in[...], False, keep(0), at, mixed, left_ref, inverses, 0, None)

    advance(left_ref[...], False, keep(1), at, mixed, l_out, inverses, 1, begin_piece)

    across = pltpu.make_async_remote_copy(
        src_ref=out.at[1 - core], dst_ref=out_ref.at[0, core, 0], send_sem=out_send, recv_sem=out_recv,
        device_id=(partner, z), device_id_type=MESH,
    )
    home = pltpu.make_async_copy(out.at[core], out_ref.at[0, core, 0], out_own)

    for q in range(2):
        results(inverses, mixed, rows, out, q)

        @pl.when(core == q)
        def _():
            home.start()

        @pl.when(core != q)
        def _():
            across.start()

    home.wait()
    across.wait()

    for piece in pieces.values():
        piece.wait_send()

    @pl.when(is_first)
    def _():
        for piece in pieces.values():
            piece.wait_recv()

    for copy in crossing:
        copy.wait_send()
    every = [part for d in range(1, 5) for part in parts(d)]

    def sent(*flows):
        for flow in flows:
            for part in every:
                ring(flow, *part).wait_send()

    sent(0, 1)

    @pl.when(row >= 2)
    def _():
        sent(2, 4, 5)
        for c in range(2):
            back(c).wait_send()

    @pl.when(row >= 1)
    def _():
        sent(3)

    @pl.when(row == 3)
    def _():
        sent(6, 7)
        for c in range(2, 4):
            back(c).wait_send()

    @pl.when(row < 2)
    def _():
        lent.wait_send()
        for c in range(2):
            for half in range(2):
                gift(c, half).wait_send()

    @pl.when(row == 0)
    def _():
        for c in range(2, 4):
            for half in range(2):
                gift(c, half).wait_send()


def sweep(ops, limits, boundaries):
    vmem = pl.BlockSpec(memory_space=pltpu.VMEM)
    anywhere = pl.BlockSpec(memory_space=pl.ANY)
    bf16, f32 = jnp.bfloat16, jnp.float32
    dma = pltpu.SemaphoreType.DMA
    return pl.pallas_call(
        sweep_kernel,
        out_shape=jax.ShapeDtypeStruct(boundaries.shape, bf16),
        in_specs=[vmem, vmem, anywhere],
        out_specs=anywhere,
        scratch_shapes=[
            pltpu.VMEM((2, 8, N, N * N), bf16),
            pltpu.VMEM((2, 8, N, N), bf16),
            pltpu.VMEM((2, 8, 128), f32),
            pltpu.VMEM((N, N * N), f32),
            pltpu.VMEM((N, N * N), f32),
            pltpu.VMEM((2048, 128), f32),
            pltpu.VMEM((2, 2048, 256), bf16),
            pltpu.VMEM((2, 256, 2048), bf16),
            pltpu.VMEM((2, N, N * N), bf16),
            pltpu.VMEM((2, N, 128), f32),
            pltpu.VMEM((N, 128), f32),
            pltpu.VMEM((N, 128), f32),
            pltpu.VMEM((N, 128), f32),
            pltpu.VMEM((8, N, 4 * CHUNK), bf16),
            pltpu.VMEM((8, N, N), bf16),
            pltpu.VMEM((N, 4 * CHUNK), f32),
            dma((3,)), dma((3,)), dma((3,)),
            dma((8, 2, 4, 2)), dma((8, 2, 4, 2)),
            dma((4,)), dma((4,)), dma, dma, dma,
            dma((4, 2)), dma((4, 2)), dma((4,)), dma((4,)), dma, dma,
        ],
        compiler_params=pltpu.CompilerParams(
            collective_id=0, has_side_effects=True, vmem_limit_bytes=40 * 1024 * 1024
        ),
    )(ops, limits, boundaries)


def on_device(boundaries, row_ops, ranks):
    my_sector = lax.axis_index("sec")
    ops = lax.dynamic_slice_in_dim(row_ops, my_sector, 1, 3).reshape(2, 8, N, N)
    ops = jnp.swapaxes(ops, 2, 3)
    limits = jnp.broadcast_to(ranks.reshape(2, 1, 1).astype(jnp.float32), (2, 8, 128))
    return sweep(ops, limits, boundaries)


def solution(mesh):
    placed = (
        P("sec", None, "col", None, None),
        P(None, "col", None, None, None, None),
        P("sec", None, "col"),
    )
    return jax.shard_map(
        on_device,
        mesh=mesh,
        in_specs=placed,
        out_specs=P("sec", None, "col", None, None),
        check_vma=False,
    )
```

```python
import functools
import math

import jax
import jax.numpy as jnp
from jax import lax
from jax.experimental import pallas as pl
from jax.experimental.pallas import tpu as pltpu
from jax.sharding import PartitionSpec as P

MESH = pl.DeviceIdType.MESH
N = 64
OWN = 512
CHUNK = 896
MIDDLE = OWN + 2 * CHUNK
NT = (((1,), (1,)), ((), ()))
NN = (((1,), (0,)), ((), ()))


def dot(a, b, dims):
    return lax.dot_general(a, b, dims, preferred_element_type=jnp.float32)


def split(x):
    hi = x.astype(jnp.bfloat16)
    lo = (x - hi.astype(jnp.float32)).astype(jnp.bfloat16)
    return hi, lo


WIDE = (8, 128)


def on_lines(x, i):
    return jnp.broadcast_to(x[i : i + 1, :], WIDE)


def on_lanes(x, i):
    return jnp.broadcast_to(x[:, i : i + 1], WIDE)


def factor(g, emit):
    rows = [g[8 * i : 8 * i + 8] for i in range(8)]
    cols = [on_lanes(rows[0], a) for a in range(8)]
    for p in range(8):
        mine, steps, done = rows[p], [], []
        if p < 7:
            beside = [on_lanes(rows[p + 1], 8 * p + a) for a in range(8)]
            ahead = [on_lanes(rows[p + 1], 8 * p + 8 + a) for a in range(8)]
        for a in range(8):
            pivot = on_lines(cols[a], a)
            inverse = 1.0 / pivot
            row = on_lines(mine, a)
            done.append(row[0:1] * lax.rsqrt(pivot[0:1]))
            heads = [on_lines(cols[b], a) if b > a else None for b in range(8)]
            times = cols[a] * inverse
            for b in range(a + 1, 8):
                cols[b] = cols[b] - times * heads[b]
            mine = mine - times * row
            if p < 7:
                times = beside[a] * inverse
                for b in range(a + 1, 8):
                    beside[b] = beside[b] - times * heads[b]
                for b in range(8):
                    ahead[b] = ahead[b] - times * on_lines(beside[a], b)
                rows[p + 1] = rows[p + 1] - times * row
            steps.append((inverse, row, heads))
        for r in range(p + 2, 8):
            below = [on_lanes(rows[r], 8 * p + a) for a in range(8)]
            for a, (inverse, row, heads) in enumerate(steps):
                times = below[a] * inverse
                for b in range(a + 1, 8):
                    below[b] = below[b] - times * heads[b]
                rows[r] = rows[r] - times * row
        emit(p, jnp.concatenate(done, 0))
        if p < 7:
            cols = ahead


def patterns():
    lane = lax.broadcasted_iota(jnp.int32, (N, 128), 1)
    line = lax.broadcasted_iota(jnp.int32, (N, 128), 0)
    low = lane < N
    place = jnp.where(low, lane, lane - N)
    eye = jnp.where(place == line, 1.0, 0.0).astype(jnp.float32)
    return line, low, place, eye


def absorb(lefts, rights, acc, start, width, tiles, first):
    def tile(n, carry):
        at = pl.ds(pl.multiple_of(start + n * width, 128), width)
        total = sum(dot(left, right[:, at], NN) for left, right in zip(lefts, rights))
        acc[:, at] = total if first else acc[:, at] + total
        return carry

    if tiles == 1:
        tile(0, 0)
    else:
        lax.fori_loop(0, tiles, tile, 0)


def to_columns(acc, rows, at, q):
    low = lax.broadcasted_iota(jnp.int32, (32, 128), 1) < N
    for m in range(32):
        v = acc[:, 128 * m : 128 * m + 128]
        w = pltpu.roll(v, N, 1)
        rows[pl.ds(2 * m, 32, stride=N), :] = jnp.where(low, v[0:32], w[32:64])
        rows[pl.ds(2 * m + 1, 32, stride=N), :] = jnp.where(low, w[0:32], v[32:64])
    for t in range(16):
        hi, lo = split(rows[128 * t : 128 * t + 128, :].T)
        at[q, 128 * t : 128 * t + 128, 0:128] = hi
        at[q, 128 * t : 128 * t + 128, 128:256] = lo


def advance(left, unit, keep, at, mixed, next_left, inverses, q, begin):
    line, low, place, eye = patterns()
    both = jnp.concatenate([jnp.where(low, left, 0.0), jnp.where(low, 0.0, pltpu.roll(left, N, 1))], 0)
    hi, lo = split(both)
    weights = jnp.concatenate(
        [jnp.concatenate([hi, hi], 1), jnp.concatenate([lo, jnp.zeros_like(lo)], 1)], 0
    )
    for t in range(0, 16, 2):
        o = dot(at[q, 128 * t : 128 * t + 256, :], weights, NT)
        hi, lo = split(o[:, 0:128] + o[:, 128:256])
        for u in range(2):
            lanes = slice(128 * (t + u), 128 * (t + u) + 128)
            mixed[q, 0:128, lanes] = hi[128 * u : 128 * u + 128]
            mixed[q, 128:256, lanes] = lo[128 * u : 128 * u + 128]
    y = mixed[q]
    g = dot(y, y, NT)
    g = g[0:128] + g[128:256]
    g = g[:, 0:128] + g[:, 128:256]
    total = jnp.sum(jnp.where(low, left * left, 0.0), keepdims=True)
    scale = lax.rsqrt(total * (1.0 / (N * N)) + 1e-06)
    scale = jnp.ones_like(scale) if unit else scale
    full = (g[0:N] + pltpu.roll(g[N:], N, 1)) * (scale * scale)

    def emit(p, rows):
        part = slice(8 * p, 8 * p + 8)
        upper = jnp.logical_and(low[part], place[part] >= line[part])
        next_left[part, :] = jnp.where(jnp.logical_and(keep[part], upper), rows, 0.0)
        inverses[q, part, :] = jnp.where(jnp.logical_or(low[part], jnp.logical_not(keep[part])), 0.0, rows) * (scale * float(N))
        if begin is not None:
            begin(p)

    factor(jnp.where(low, full, eye), emit)


def results(inverses, mixed, rows, out, q):
    inverse = inverses[q]
    pair = jnp.concatenate([pltpu.roll(inverse, N, 1), inverse], 0)
    p_hi, p_lo = split(pair)
    wide = jnp.concatenate([p_hi, p_hi], 1)
    for c in range(8):
        y = mixed[q, :, 256 * c : 256 * c + 256]
        o = dot(wide, y, NN) + dot(p_lo, y[0:128], NN)
        rows[256 * c : 256 * c + 128, :] = o[:, 0:128].T
        rows[256 * c + 128 : 256 * c + 256, :] = o[:, 128:256].T
    low = lax.broadcasted_iota(jnp.int32, (32, 128), 1) < N
    for m in range(32):
        e = rows[pl.ds(2 * m, 32, stride=N), :]
        d = rows[pl.ds(2 * m + 1, 32, stride=N), :]
        at = slice(128 * m, 128 * m + 128)
        out[q, 0:32, at] = jnp.where(low, e, pltpu.roll(d, N, 1)).astype(jnp.bfloat16)
        out[q, 32:64, at] = jnp.where(low, pltpu.roll(e, N, 1), d).astype(jnp.bfloat16)


def sweep_kernel(
    ops_ref, limit_ref, bnd_ref, out_ref,
    blocks, ops, limits, acc, second, rows, at, mixed, out, inverses, l_in, l_out, left_ref,
    guests, guest_ops, guest_sums, part_send, part_recv, own_sem, ring_send, ring_recv, l_send, l_recv, out_send, out_recv, out_own,
    gift_send, gift_recv, back_send, back_recv, lent_send, lent_recv, hop_send,
):
    me = lax.axis_index("col")
    columns = lax.axis_size("col")
    z = lax.axis_index("sec")
    size = lax.axis_size("sec")
    core = lax.rem(me, 2)
    partner = me + 1 - 2 * core
    up, down = lax.rem(z + 1, size), lax.rem(z + size - 1, size)
    after, before = lax.rem(me + 2, columns), lax.rem(me + columns - 2, columns)
    is_first = me < 2
    band = columns // 4
    row = me // band
    peer = me + band * (3 - 2 * row)

    barrier = pltpu.get_barrier_semaphore()
    peer_partner = peer + 1 - 2 * core
    greeted = (
        (partner, z), (me, up), (me, down), (partner, up), (partner, down), (before, z), (peer, z), (peer_partner, z),
    )
    for to in greeted:
        pl.semaphore_signal(barrier, inc=1, device_id=to, device_id_type=MESH)
    pl.semaphore_wait(barrier, len(greeted))

    def to_partner(n, source, target):
        return pltpu.make_async_remote_copy(
            src_ref=source, dst_ref=target, send_sem=part_send.at[n], recv_sem=part_recv.at[n],
            device_id=(partner, z), device_id_type=MESH,
        )

    crossing = [
        to_partner(0, bnd_ref.at[0, 1 - core, 0], blocks.at[core, z]),
        to_partner(1, ops_ref.at[1 - core], ops.at[core]),
        to_partner(2, limit_ref.at[1 - core], limits.at[core]),
    ]
    staying = [
        pltpu.make_async_copy(bnd_ref.at[0, core, 0], blocks.at[core, z], own_sem.at[0]),
        pltpu.make_async_copy(ops_ref.at[core], ops.at[core], own_sem.at[1]),
        pltpu.make_async_copy(limit_ref.at[core], limits.at[core], own_sem.at[2]),
    ]
    for copy in crossing + staying:
        copy.start()

    edges = {1: (0, OWN), 2: (OWN, MIDDLE), 3: (MIDDLE, N * N)}

    def chunk(c):
        return slice(CHUNK * c, CHUNK * c + CHUNK)

    def far_chunk(c):
        return slice(OWN + CHUNK * c, OWN + CHUNK * c + CHUNK)

    def ring(flow, way, d, half):
        block = lax.rem(z + size + (d - 1 if way else 1 - d), size)
        lines = slice(32 * half, 32 * half + 32)
        if flow == 0:
            part = blocks.at[0, block, lines]
        elif flow < 4:
            part = blocks.at[1, block, lines, edges[flow][0] : edges[flow][1]]
        else:
            part = guests.at[block, lines, chunk(flow - 4)]
        return pltpu.make_async_remote_copy(
            src_ref=part, dst_ref=part, send_sem=ring_send.at[flow, way, d - 1, half],
            recv_sem=ring_recv.at[flow, way, d - 1, half],
            device_id=(me, down if way else up), device_id_type=MESH,
        )

    def first_hop(flow, way, half, b):
        q = 0 if flow == 0 else 1
        lines = slice(32 * half, 32 * half + 32)
        lanes = slice(*edges[flow]) if flow else slice(0, N * N)
        return pltpu.make_async_remote_copy(
            src_ref=bnd_ref.at[0, b, 0, lines, lanes], dst_ref=blocks.at[q, z, lines, lanes],
            send_sem=hop_send.at[flow, way, half, b], recv_sem=ring_recv.at[flow, way, 0, half],
            device_id=(me - core + b, down if way else up), device_id_type=MESH,
        )

    def gift(c, half, b):
        lines = slice(32 * half, 32 * half + 32)
        return pltpu.make_async_remote_copy(
            src_ref=bnd_ref.at[0, b, 0, lines, far_chunk(c)], dst_ref=guests.at[z, lines, chunk(c)],
            send_sem=gift_send.at[c, half, b], recv_sem=gift_recv.at[c, half],
            device_id=(peer - core + b, z), device_id_type=MESH,
        )

    def lent(b):
        return pltpu.make_async_remote_copy(
            src_ref=ops_ref.at[b], dst_ref=guest_ops, send_sem=lent_send.at[b], recv_sem=lent_recv,
            device_id=(peer - core + b, z), device_id_type=MESH,
        )

    def back(c):
        return pltpu.make_async_remote_copy(
            src_ref=guest_sums.at[:, chunk(c)], dst_ref=second.at[:, far_chunk(c)],
            send_sem=back_send.at[c], recv_sem=back_recv.at[c], device_id=(peer, z), device_id_type=MESH,
        )

    def parts(d):
        return [(way, d, half) for half in range(2) for way in range(2) if d < 4 or half == way]

    def ready(q):
        @pl.when(core == q)
        def _():
            staying[0].wait()

        @pl.when(core != q)
        def _():
            crossing[0].wait_recv()

    def hops():
        return [(way, half, b) for half in range(2) for way in range(2) for b in range(2)]

    def begin(flow):
        @pl.when(core == (0 if flow == 0 else 1))
        def _():
            for hop in hops():
                first_hop(flow, *hop).start()

    def turn(flow, d):
        for way, _, half in parts(d):
            ring(flow, way, d, half).wait_recv()
            if d < 4 and (way, d + 1, half) in parts(d + 1):
                ring(flow, way, d + 1, half).start()

    def sectors(d):
        before, after = lax.rem(z + size - d, size), lax.rem(z + d, size)
        return [z] if d == 0 else [after] if d == 4 else [before, after]

    def absorb_flow(flow, d):
        q = 0 if flow == 0 else 1
        start, width, tiles = {0: (0, 512, 8), 1: (0, 512, 1), 2: (OWN, 256, 7), 3: (MIDDLE, 256, 7)}[flow]
        absorb(
            [ops[q, s] for s in sectors(d)], [blocks.at[q, s] for s in sectors(d)],
            second if q else acc, start, width, tiles, d == 0,
        )

    def open_guest(c):
        for half in range(2):
            gift(c, half, 0).wait_recv()
            for way in range(2):
                ring(4 + c, way, 1, half).start()

    def serve(count, at_end):
        open_guest(0)
        open_guest(1)
        for slot in range(1, 2 * count + 3):
            for c in range(count):
                d = slot - 2 * c
                if not 1 <= d <= 4:
                    continue
                turn(4 + c, d)
                if d == 3 and c + 2 < count:
                    open_guest(c + 2)
                if d == 3 and c == count - 1:
                    at_end()
                if d == 4:
                    if c == 0:
                        lent(0).wait_recv()
                    lefts = [guest_ops[s] for s in range(8)]
                    rights = [guests.at[s] for s in range(8)]
                    for start, width in ((0, 256), (256, 256), (512, 256), (768, 128)):
                        absorb(lefts, rights, guest_sums, CHUNK * c + start, width, 1, True)
                    back(c).start()

    def begin_own():
        begin(0)
        begin(1)

    @pl.when(jnp.logical_and(row < 2, core == 1))
    def _():
        for c in range(2):
            for half in range(2):
                for b in range(2):
                    gift(c, half, b).start()

    @pl.when(row < 3)
    def _():
        begin_own()

    @pl.when(jnp.logical_and(row == 0, core == 1))
    def _():
        for c in range(2, 4):
            for half in range(2):
                for b in range(2):
                    gift(c, half, b).start()

    @pl.when(jnp.logical_and(row < 2, core == 1))
    def _():
        for b in range(2):
            lent(b).start()

    @pl.when(row == 2)
    def _():
        serve(2, lambda: None)

    @pl.when(row == 3)
    def _():
        serve(4, begin_own)

    ready(0)
    ready(1)
    for copy in staying[1:]:
        copy.wait()
    for copy in crossing[1:]:
        copy.wait_recv()

    for d in range(5):
        if d > 0:
            turn(0, d)
            turn(1, d)
        if d == 3:

            @pl.when(row >= 2)
            def _():
                begin(2)

            @pl.when(row >= 1)
            def _():
                begin(3)

        absorb_flow(0, d)
        absorb_flow(1, d)
    to_columns(acc, rows, at, 0)
    for d in range(5):

        @pl.when(row >= 2)
        def _():
            if d > 0:
                turn(2, d)
            absorb_flow(2, d)

        @pl.when(row >= 1)
        def _():
            if d > 0:
                turn(3, d)
            absorb_flow(3, d)

    line, low, place, eye = patterns()

    def along(part, start, size):
        return pltpu.make_async_remote_copy(
            src_ref=l_out.at[start : start + size], dst_ref=l_in.at[start : start + size],
            send_sem=l_send.at[part], recv_sem=l_recv.at[part], device_id=(after, z), device_id_type=MESH,
        )

    pieces = {3: along(0, 0, 32), 5: along(1, 32, 16), 6: along(2, 48, 8), 7: along(3, 56, 8)}

    def keep(q):
        return line.astype(jnp.float32) < limits[q, 0:1, :]

    def begin_piece(p):
        if p in pieces:
            pieces[p].start()

    @pl.when(is_first)
    def _():
        advance(eye, True, keep(0), at, mixed, left_ref, inverses, 0, None)

    @pl.when(row < 2)
    def _():
        for c in range(2):
            back(c).wait_recv()

    @pl.when(row == 0)
    def _():
        for c in range(2, 4):
            back(c).wait_recv()

    to_columns(second, rows, at, 1)

    @pl.when(jnp.logical_not(is_first))
    def _():
        for piece in pieces.values():
            piece.wait_recv()
        advance(l_in[...], False, keep(0), at, mixed, left_ref, inverses, 0, None)

    advance(left_ref[...], False, keep(1), at, mixed, l_out, inverses, 1, begin_piece)

    across = pltpu.make_async_remote_copy(
        src_ref=out.at[1 - core], dst_ref=out_ref.at[0, core, 0], send_sem=out_send, recv_sem=out_recv,
        device_id=(partner, z), device_id_type=MESH,
    )
    home = pltpu.make_async_copy(out.at[core], out_ref.at[0, core, 0], out_own)

    for q in range(2):
        results(inverses, mixed, rows, out, q)

        @pl.when(core == q)
        def _():
            home.start()

        @pl.when(core != q)
        def _():
            across.start()

    home.wait()
    across.wait()

    for piece in pieces.values():
        piece.wait_send()

    @pl.when(is_first)
    def _():
        for piece in pieces.values():
            piece.wait_recv()

    for copy in crossing:
        copy.wait_send()
    late = [part for d in range(2, 5) for part in parts(d)]

    def sent(*flows):
        for flow in flows:
            for part in late + (parts(1) if flow > 3 else []):
                ring(flow, *part).wait_send()
            if flow < 4:

                @pl.when(core == (0 if flow == 0 else 1))
                def _():
                    for hop in hops():
                        first_hop(flow, *hop).wait_send()

    sent(0, 1)

    @pl.when(row >= 2)
    def _():
        sent(2, 4, 5)
        for c in range(2):
            back(c).wait_send()

    @pl.when(row >= 1)
    def _():
        sent(3)

    @pl.when(row == 3)
    def _():
        sent(6, 7)
        for c in range(2, 4):
            back(c).wait_send()

    @pl.when(jnp.logical_and(row < 2, core == 1))
    def _():
        for b in range(2):
            lent(b).wait_send()
            for c in range(2):
                for half in range(2):
                    gift(c, half, b).wait_send()

    @pl.when(jnp.logical_and(row == 0, core == 1))
    def _():
        for b in range(2):
            for c in range(2, 4):
                for half in range(2):
                    gift(c, half, b).wait_send()


def sweep(ops, limits, boundaries):
    vmem = pl.BlockSpec(memory_space=pltpu.VMEM)
    anywhere = pl.BlockSpec(memory_space=pl.ANY)
    bf16, f32 = jnp.bfloat16, jnp.float32
    dma = pltpu.SemaphoreType.DMA
    return pl.pallas_call(
        sweep_kernel,
        out_shape=jax.ShapeDtypeStruct(boundaries.shape, bf16),
        in_specs=[vmem, vmem, anywhere],
        out_specs=anywhere,
        scratch_shapes=[
            pltpu.VMEM((2, 8, N, N * N), bf16),
            pltpu.VMEM((2, 8, N, N), bf16),
            pltpu.VMEM((2, 8, 128), f32),
            pltpu.VMEM((N, N * N), f32),
            pltpu.VMEM((N, N * N), f32),
            pltpu.VMEM((2048, 128), f32),
            pltpu.VMEM((2, 2048, 256), bf16),
            pltpu.VMEM((2, 256, 2048), bf16),
            pltpu.VMEM((2, N, N * N), bf16),
            pltpu.VMEM((2, N, 128), f32),
            pltpu.VMEM((N, 128), f32),
            pltpu.VMEM((N, 128), f32),
            pltpu.VMEM((N, 128), f32),
            pltpu.VMEM((8, N, 4 * CHUNK), bf16),
            pltpu.VMEM((8, N, N), bf16),
            pltpu.VMEM((N, 4 * CHUNK), f32),
            dma((3,)), dma((3,)), dma((3,)),
            dma((8, 2, 4, 2)), dma((8, 2, 4, 2)),
            dma((4,)), dma((4,)), dma, dma, dma,
            dma((4, 2, 2)), dma((4, 2)), dma((4,)), dma((4,)), dma((2,)), dma, dma((4, 2, 2, 2)),
        ],
        compiler_params=pltpu.CompilerParams(
            collective_id=0, has_side_effects=True, vmem_limit_bytes=40 * 1024 * 1024
        ),
    )(ops, limits, boundaries)


def on_device(boundaries, row_ops, ranks):
    my_sector = lax.axis_index("sec")
    ops = lax.dynamic_slice_in_dim(row_ops, my_sector, 1, 3).reshape(2, 8, N, N)
    ops = jnp.swapaxes(ops, 2, 3)
    limits = jnp.broadcast_to(ranks.reshape(2, 1, 1).astype(jnp.float32), (2, 8, 128))
    return sweep(ops, limits, boundaries)


def solution(mesh):
    placed = (
        P("sec", None, "col", None, None),
        P(None, "col", None, None, None, None),
        P("sec", None, "col"),
    )
    return jax.shard_map(
        on_device,
        mesh=mesh,
        in_specs=placed,
        out_specs=P("sec", None, "col", None, None),
        check_vma=False,
    )
```

```python
import functools
import math

import jax
import jax.numpy as jnp
from jax import lax
from jax.experimental import pallas as pl
from jax.experimental.pallas import tpu as pltpu
from jax.sharding import PartitionSpec as P

MESH = pl.DeviceIdType.MESH
N = 64
OWN = 1024
CHUNK = 768
MIDDLE = OWN + 2 * CHUNK
NT = (((1,), (1,)), ((), ()))
NN = (((1,), (0,)), ((), ()))


def dot(a, b, dims):
    return lax.dot_general(a, b, dims, preferred_element_type=jnp.float32)


def split(x):
    hi = x.astype(jnp.bfloat16)
    lo = (x - hi.astype(jnp.float32)).astype(jnp.bfloat16)
    return hi, lo


WIDE = (8, 128)


def on_lines(x, i):
    return jnp.broadcast_to(x[i : i + 1, :], WIDE)


def on_lanes(x, i):
    return jnp.broadcast_to(x[:, i : i + 1], WIDE)


def factor(g, emit):
    rows = [g[8 * i : 8 * i + 8] for i in range(8)]
    cols = [on_lanes(rows[0], a) for a in range(8)]
    for p in range(8):
        mine, steps, done = rows[p], [], []
        if p < 7:
            beside = [on_lanes(rows[p + 1], 8 * p + a) for a in range(8)]
            ahead = [on_lanes(rows[p + 1], 8 * p + 8 + a) for a in range(8)]
        for a in range(8):
            pivot = on_lines(cols[a], a)
            inverse = 1.0 / pivot
            row = on_lines(mine, a)
            done.append(row[0:1] * lax.rsqrt(pivot[0:1]))
            heads = [on_lines(cols[b], a) if b > a else None for b in range(8)]
            times = cols[a] * inverse
            for b in range(a + 1, 8):
                cols[b] = cols[b] - times * heads[b]
            mine = mine - times * row
            if p < 7:
                times = beside[a] * inverse
                for b in range(a + 1, 8):
                    beside[b] = beside[b] - times * heads[b]
                for b in range(8):
                    ahead[b] = ahead[b] - times * on_lines(beside[a], b)
                rows[p + 1] = rows[p + 1] - times * row
            steps.append((inverse, row, heads))
        for r in range(p + 2, 8):
            below = [on_lanes(rows[r], 8 * p + a) for a in range(8)]
            for a, (inverse, row, heads) in enumerate(steps):
                times = below[a] * inverse
                for b in range(a + 1, 8):
                    below[b] = below[b] - times * heads[b]
                rows[r] = rows[r] - times * row
        emit(p, jnp.concatenate(done, 0))
        if p < 7:
            cols = ahead


def patterns():
    lane = lax.broadcasted_iota(jnp.int32, (N, 128), 1)
    line = lax.broadcasted_iota(jnp.int32, (N, 128), 0)
    low = lane < N
    place = jnp.where(low, lane, lane - N)
    eye = jnp.where(place == line, 1.0, 0.0).astype(jnp.float32)
    return line, low, place, eye


def absorb(lefts, rights, acc, start, width, tiles, first):
    def tile(n, carry):
        at = pl.ds(pl.multiple_of(start + n * width, 128), width)
        total = sum(dot(left, right[:, at], NN) for left, right in zip(lefts, rights))
        acc[:, at] = total if first else acc[:, at] + total
        return carry

    if tiles == 1:
        tile(0, 0)
    else:
        lax.fori_loop(0, tiles, tile, 0)


def flip(raw, ops):
    def one(s, carry):
        ops[s] = raw[s].astype(jnp.float32).T.astype(jnp.bfloat16)
        return carry

    lax.fori_loop(0, 8, one, 0)


def to_columns(acc, rows, at, q):
    low = lax.broadcasted_iota(jnp.int32, (32, 128), 1) < N
    for m in range(32):
        v = acc[:, 128 * m : 128 * m + 128]
        w = pltpu.roll(v, N, 1)
        rows[pl.ds(2 * m, 32, stride=N), :] = jnp.where(low, v[0:32], w[32:64])
        rows[pl.ds(2 * m + 1, 32, stride=N), :] = jnp.where(low, w[0:32], v[32:64])
    for t in range(16):
        hi, lo = split(rows[128 * t : 128 * t + 128, :].T)
        at[q, 128 * t : 128 * t + 128, 0:128] = hi
        at[q, 128 * t : 128 * t + 128, 128:256] = lo


def advance(left, unit, keep, at, mixed, next_left, inverses, q, begin):
    line, low, place, eye = patterns()
    both = jnp.concatenate([jnp.where(low, left, 0.0), jnp.where(low, 0.0, pltpu.roll(left, N, 1))], 0)
    hi, lo = split(both)
    weights = jnp.concatenate(
        [jnp.concatenate([hi, hi], 1), jnp.concatenate([lo, jnp.zeros_like(lo)], 1)], 0
    )
    for t in range(0, 16, 2):
        o = dot(at[q, 128 * t : 128 * t + 256, :], weights, NT)
        hi, lo = split(o[:, 0:128] + o[:, 128:256])
        for u in range(2):
            lanes = slice(128 * (t + u), 128 * (t + u) + 128)
            mixed[q, 0:128, lanes] = hi[128 * u : 128 * u + 128]
            mixed[q, 128:256, lanes] = lo[128 * u : 128 * u + 128]
    y = mixed[q]
    g = dot(y, y, NT)
    g = g[0:128] + g[128:256]
    g = g[:, 0:128] + g[:, 128:256]
    total = jnp.sum(jnp.where(low, left * left, 0.0), keepdims=True)
    scale = lax.rsqrt(total * (1.0 / (N * N)) + 1e-06)
    scale = jnp.ones_like(scale) if unit else scale
    full = (g[0:N] + pltpu.roll(g[N:], N, 1)) * (scale * scale)

    def emit(p, rows):
        part = slice(8 * p, 8 * p + 8)
        upper = jnp.logical_and(low[part], place[part] >= line[part])
        next_left[part, :] = jnp.where(jnp.logical_and(keep[part], upper), rows, 0.0)
        inverses[q, part, :] = jnp.where(jnp.logical_or(low[part], jnp.logical_not(keep[part])), 0.0, rows) * (scale * float(N))
        if begin is not None:
            begin(p)

    factor(jnp.where(low, full, eye), emit)


def results(inverses, mixed, rows, out, q):
    inverse = inverses[q]
    pair = jnp.concatenate([pltpu.roll(inverse, N, 1), inverse], 0)
    p_hi, p_lo = split(pair)
    wide = jnp.concatenate([p_hi, p_hi], 1)
    for c in range(8):
        y = mixed[q, :, 256 * c : 256 * c + 256]
        o = dot(wide, y, NN) + dot(p_lo, y[0:128], NN)
        rows[256 * c : 256 * c + 128, :] = o[:, 0:128].T
        rows[256 * c + 128 : 256 * c + 256, :] = o[:, 128:256].T
    low = lax.broadcasted_iota(jnp.int32, (32, 128), 1) < N
    for m in range(32):
        e = rows[pl.ds(2 * m, 32, stride=N), :]
        d = rows[pl.ds(2 * m + 1, 32, stride=N), :]
        at = slice(128 * m, 128 * m + 128)
        out[q, 0:32, at] = jnp.where(low, e, pltpu.roll(d, N, 1)).astype(jnp.bfloat16)
        out[q, 32:64, at] = jnp.where(low, pltpu.roll(e, N, 1), d).astype(jnp.bfloat16)


def sweep_kernel(
    ranks_ref, ops_ref, bnd_ref, out_ref,
    blocks, raw, ops, ranks, limits, acc, second, rows, at, mixed, out, inverses, l_in, l_out, left_ref,
    guests, guest_raw, guest_ops, guest_sums, part_send, part_recv, own_sem, ring_send, ring_recv, l_send, l_recv, out_send, out_recv, out_own,
    gift_send, gift_recv, back_send, back_recv, lent_send, lent_recv, hop_send,
):
    me = lax.axis_index("col")
    columns = lax.axis_size("col")
    z = lax.axis_index("sec")
    size = lax.axis_size("sec")
    core = lax.rem(me, 2)
    partner = me + 1 - 2 * core
    up, down = lax.rem(z + 1, size), lax.rem(z + size - 1, size)
    after, before = lax.rem(me + 2, columns), lax.rem(me + columns - 2, columns)
    is_first = me < 2
    band = columns // 4
    row = me // band
    peer = me + band * (3 - 2 * row)

    for b in range(2):
        ranks[b] = jnp.full((8, 128), ranks_ref[0, b, 0].astype(jnp.float32))
    barrier = pltpu.get_barrier_semaphore()
    peer_partner = peer + 1 - 2 * core
    greeted = (
        (partner, z), (me, up), (me, down), (partner, up), (partner, down), (before, z), (peer, z), (peer_partner, z),
    )
    for to in greeted:
        pl.semaphore_signal(barrier, inc=1, device_id=to, device_id_type=MESH)
    pl.semaphore_wait(barrier, len(greeted))

    def to_partner(n, source, target):
        return pltpu.make_async_remote_copy(
            src_ref=source, dst_ref=target, send_sem=part_send.at[n], recv_sem=part_recv.at[n],
            device_id=(partner, z), device_id_type=MESH,
        )

    crossing = [
        to_partner(0, bnd_ref.at[0, 1 - core, 0], blocks.at[core, z]),
        to_partner(1, ops_ref.at[1 - core, 0, :, z], raw.at[core]),
        to_partner(2, ranks.at[1 - core], limits.at[core]),
    ]
    staying = [
        pltpu.make_async_copy(bnd_ref.at[0, core, 0], blocks.at[core, z], own_sem.at[0]),
        pltpu.make_async_copy(ops_ref.at[core, 0, :, z], raw.at[core], own_sem.at[1]),
        pltpu.make_async_copy(ranks.at[core], limits.at[core], own_sem.at[2]),
    ]
    for copy in crossing + staying:
        copy.start()

    edges = {1: (0, OWN), 2: (OWN, MIDDLE), 3: (MIDDLE, N * N)}

    def chunk(c):
        return slice(CHUNK * c, CHUNK * c + CHUNK)

    def far_chunk(c):
        return slice(OWN + CHUNK * c, OWN + CHUNK * c + CHUNK)

    def ring(flow, way, d, half):
        block = lax.rem(z + size + (d - 1 if way else 1 - d), size)
        lines = slice(32 * half, 32 * half + 32)
        if flow == 0:
            part = blocks.at[0, block, lines]
        elif flow < 4:
            part = blocks.at[1, block, lines, edges[flow][0] : edges[flow][1]]
        else:
            part = guests.at[block, lines, chunk(flow - 4)]
        return pltpu.make_async_remote_copy(
            src_ref=part, dst_ref=part, send_sem=ring_send.at[flow, way, d - 1, half],
            recv_sem=ring_recv.at[flow, way, d - 1, half],
            device_id=(me, down if way else up), device_id_type=MESH,
        )

    def first_hop(flow, way, half, b):
        q = 0 if flow == 0 else 1
        lines = slice(32 * half, 32 * half + 32)
        lanes = slice(*edges[flow]) if flow else slice(0, N * N)
        return pltpu.make_async_remote_copy(
            src_ref=bnd_ref.at[0, b, 0, lines, lanes], dst_ref=blocks.at[q, z, lines, lanes],
            send_sem=hop_send.at[flow, way, half, b], recv_sem=ring_recv.at[flow, way, 0, half],
            device_id=(me - core + b, down if way else up), device_id_type=MESH,
        )

    def gift(c, half, b):
        lines = slice(32 * half, 32 * half + 32)
        return pltpu.make_async_remote_copy(
            src_ref=bnd_ref.at[0, b, 0, lines, far_chunk(c)], dst_ref=guests.at[z, lines, chunk(c)],
            send_sem=gift_send.at[c, half, b], recv_sem=gift_recv.at[c, half],
            device_id=(peer - core + b, z), device_id_type=MESH,
        )

    def lent(b):
        return pltpu.make_async_remote_copy(
            src_ref=ops_ref.at[b, 0, :, z], dst_ref=guest_raw, send_sem=lent_send.at[b], recv_sem=lent_recv,
            device_id=(peer - core + b, z), device_id_type=MESH,
        )

    def back(c):
        return pltpu.make_async_remote_copy(
            src_ref=guest_sums.at[:, chunk(c)], dst_ref=second.at[:, far_chunk(c)],
            send_sem=back_send.at[c], recv_sem=back_recv.at[c], device_id=(peer, z), device_id_type=MESH,
        )

    def parts(d):
        return [(way, d, half) for half in range(2) for way in range(2) if d < 4 or half == way]

    def ready(q):
        @pl.when(core == q)
        def _():
            staying[0].wait()

        @pl.when(core != q)
        def _():
            crossing[0].wait_recv()

    def hops():
        return [(way, half, b) for half in range(2) for way in range(2) for b in range(2)]

    def begin(flow):
        @pl.when(core == (0 if flow == 0 else 1))
        def _():
            for hop in hops():
                first_hop(flow, *hop).start()

    def turn(flow, d):
        for way, _, half in parts(d):
            ring(flow, way, d, half).wait_recv()
            if d < 4 and (way, d + 1, half) in parts(d + 1):
                ring(flow, way, d + 1, half).start()

    def sectors(d):
        before, after = lax.rem(z + size - d, size), lax.rem(z + d, size)
        return [z] if d == 0 else [after] if d == 4 else [before, after]

    def absorb_flow(flow, d):
        q = 0 if flow == 0 else 1
        start, width, tiles = {0: (0, 512, 8), 1: (0, 512, 2), 2: (OWN, 256, 6), 3: (MIDDLE, 256, 6)}[flow]
        absorb(
            [ops[q, s] for s in sectors(d)], [blocks.at[q, s] for s in sectors(d)],
            second if q else acc, start, width, tiles, d == 0,
        )

    def open_guest(c):
        for half in range(2):
            gift(c, half, 0).wait_recv()
            for way in range(2):
                ring(4 + c, way, 1, half).start()

    def serve(count, at_end):
        open_guest(0)
        open_guest(1)
        for slot in range(1, 2 * count + 3):
            for c in range(count):
                d = slot - 2 * c
                if not 1 <= d <= 4:
                    continue
                turn(4 + c, d)
                if d == 3 and c + 2 < count:
                    open_guest(c + 2)
                if d == 3 and c == count - 1:
                    at_end()
                if d == 4:
                    if c == 0:
                        lent(0).wait_recv()
                        flip(guest_raw, guest_ops)
                    lefts = [guest_ops[s] for s in range(8)]
                    rights = [guests.at[s] for s in range(8)]
                    absorb(lefts, rights, guest_sums, CHUNK * c, 256, 3, True)
                    back(c).start()

    def begin_own():
        begin(0)
        begin(1)

    @pl.when(jnp.logical_and(row < 2, core == 1))
    def _():
        for c in range(2):
            for half in range(2):
                for b in range(2):
                    gift(c, half, b).start()

    @pl.when(row < 3)
    def _():
        begin_own()

    @pl.when(jnp.logical_and(row == 0, core == 1))
    def _():
        for c in range(2, 4):
            for half in range(2):
                for b in range(2):
                    gift(c, half, b).start()

    @pl.when(jnp.logical_and(row < 2, core == 1))
    def _():
        for b in range(2):
            lent(b).start()

    @pl.when(row == 2)
    def _():
        serve(2, lambda: None)

    @pl.when(row == 3)
    def _():
        serve(4, begin_own)

    ready(0)
    ready(1)
    for copy in staying[1:]:
        copy.wait()
    for copy in crossing[1:]:
        copy.wait_recv()
    for q in range(2):
        flip(raw.at[q], ops.at[q])

    for d in range(5):
        if d > 0:
            turn(0, d)
            turn(1, d)
        if d == 3:

            @pl.when(row >= 2)
            def _():
                begin(2)

            @pl.when(row >= 1)
            def _():
                begin(3)

        absorb_flow(0, d)
        absorb_flow(1, d)
    to_columns(acc, rows, at, 0)
    for d in range(5):

        @pl.when(row >= 2)
        def _():
            if d > 0:
                turn(2, d)
            absorb_flow(2, d)

        @pl.when(row >= 1)
        def _():
            if d > 0:
                turn(3, d)
            absorb_flow(3, d)

    line, low, place, eye = patterns()

    def along(part, start, size):
        return pltpu.make_async_remote_copy(
            src_ref=l_out.at[start : start + size], dst_ref=l_in.at[start : start + size],
            send_sem=l_send.at[part], recv_sem=l_recv.at[part], device_id=(after, z), device_id_type=MESH,
        )

    pieces = {3: along(0, 0, 32), 5: along(1, 32, 16), 6: along(2, 48, 8), 7: along(3, 56, 8)}

    def keep(q):
        return line.astype(jnp.float32) < limits[q, 0:1, :]

    def begin_piece(p):
        if p in pieces:
            pieces[p].start()

    @pl.when(is_first)
    def _():
        advance(eye, True, keep(0), at, mixed, left_ref, inverses, 0, None)

    @pl.when(row < 2)
    def _():
        for c in range(2):
            back(c).wait_recv()

    @pl.when(row == 0)
    def _():
        for c in range(2, 4):
            back(c).wait_recv()

    to_columns(second, rows, at, 1)

    @pl.when(jnp.logical_not(is_first))
    def _():
        for piece in pieces.values():
            piece.wait_recv()
        advance(l_in[...], False, keep(0), at, mixed, left_ref, inverses, 0, None)

    advance(left_ref[...], False, keep(1), at, mixed, l_out, inverses, 1, begin_piece)

    across = pltpu.make_async_remote_copy(
        src_ref=out.at[1 - core], dst_ref=out_ref.at[0, core, 0], send_sem=out_send, recv_sem=out_recv,
        device_id=(partner, z), device_id_type=MESH,
    )
    home = pltpu.make_async_copy(out.at[core], out_ref.at[0, core, 0], out_own)

    for q in range(2):
        results(inverses, mixed, rows, out, q)

        @pl.when(core == q)
        def _():
            home.start()

        @pl.when(core != q)
        def _():
            across.start()

    home.wait()
    across.wait()

    for piece in pieces.values():
        piece.wait_send()

    @pl.when(is_first)
    def _():
        for piece in pieces.values():
            piece.wait_recv()

    for copy in crossing:
        copy.wait_send()
    late = [part for d in range(2, 5) for part in parts(d)]

    def sent(*flows):
        for flow in flows:
            for part in late + (parts(1) if flow > 3 else []):
                ring(flow, *part).wait_send()
            if flow < 4:

                @pl.when(core == (0 if flow == 0 else 1))
                def _():
                    for hop in hops():
                        first_hop(flow, *hop).wait_send()

    sent(0, 1)

    @pl.when(row >= 2)
    def _():
        sent(2, 4, 5)
        for c in range(2):
            back(c).wait_send()

    @pl.when(row >= 1)
    def _():
        sent(3)

    @pl.when(row == 3)
    def _():
        sent(6, 7)
        for c in range(2, 4):
            back(c).wait_send()

    @pl.when(jnp.logical_and(row < 2, core == 1))
    def _():
        for b in range(2):
            lent(b).wait_send()
            for c in range(2):
                for half in range(2):
                    gift(c, half, b).wait_send()

    @pl.when(jnp.logical_and(row == 0, core == 1))
    def _():
        for b in range(2):
            for c in range(2, 4):
                for half in range(2):
                    gift(c, half, b).wait_send()


def sweep(ranks, ops, boundaries):
    anywhere = pl.BlockSpec(memory_space=pltpu.HBM)
    bf16, f32 = jnp.bfloat16, jnp.float32
    dma = pltpu.SemaphoreType.DMA
    return pl.pallas_call(
        sweep_kernel,
        out_shape=jax.ShapeDtypeStruct(boundaries.shape, bf16),
        in_specs=[pl.BlockSpec(memory_space=pltpu.SMEM), anywhere, anywhere],
        out_specs=anywhere,
        scratch_shapes=[
            pltpu.VMEM((2, 8, N, N * N), bf16),
            pltpu.VMEM((2, 8, N, N), bf16),
            pltpu.VMEM((2, 8, N, N), bf16),
            pltpu.VMEM((2, 8, 128), f32),
            pltpu.VMEM((2, 8, 128), f32),
            pltpu.VMEM((N, N * N), f32),
            pltpu.VMEM((N, N * N), f32),
            pltpu.VMEM((2048, 128), f32),
            pltpu.VMEM((2, 2048, 256), bf16),
            pltpu.VMEM((2, 256, 2048), bf16),
            pltpu.VMEM((2, N, N * N), bf16),
            pltpu.VMEM((2, N, 128), f32),
            pltpu.VMEM((N, 128), f32),
            pltpu.VMEM((N, 128), f32),
            pltpu.VMEM((N, 128), f32),
            pltpu.VMEM((8, N, 4 * CHUNK), bf16),
            pltpu.VMEM((8, N, N), bf16),
            pltpu.VMEM((8, N, N), bf16),
            pltpu.VMEM((N, 4 * CHUNK), f32),
            dma((3,)), dma((3,)), dma((3,)),
            dma((8, 2, 4, 2)), dma((8, 2, 4, 2)),
            dma((4,)), dma((4,)), dma, dma, dma,
            dma((4, 2, 2)), dma((4, 2)), dma((4,)), dma((4,)), dma((2,)), dma, dma((4, 2, 2, 2)),
        ],
        compiler_params=pltpu.CompilerParams(
            collective_id=0, has_side_effects=True, vmem_limit_bytes=40 * 1024 * 1024
        ),
    )(ranks, ops, boundaries)


def on_device(boundaries, row_ops, ranks):
    return sweep(ranks, row_ops, boundaries)


def solution(mesh):
    placed = (
        P("sec", None, "col", None, None),
        P(None, "col", None, None, None, None),
        P("sec", None, "col"),
    )
    return jax.shard_map(
        on_device,
        mesh=mesh,
        in_specs=placed,
        out_specs=P("sec", None, "col", None, None),
        check_vma=False,
    )
```

```python
import functools
import math

import jax
import jax.numpy as jnp
from jax import lax
from jax.experimental import pallas as pl
from jax.experimental.pallas import tpu as pltpu
from jax.sharding import PartitionSpec as P

MESH = pl.DeviceIdType.MESH
N = 64
OWN = 512
CHUNK = 896
MIDDLE = OWN + 2 * CHUNK
NT = (((1,), (1,)), ((), ()))
NN = (((1,), (0,)), ((), ()))


def dot(a, b, dims):
    return lax.dot_general(a, b, dims, preferred_element_type=jnp.float32)


def split(x):
    hi = x.astype(jnp.bfloat16)
    lo = (x - hi.astype(jnp.float32)).astype(jnp.bfloat16)
    return hi, lo


WIDE = (8, 128)


def on_lines(x, i):
    return jnp.broadcast_to(x[i : i + 1, :], WIDE)


def on_lanes(x, i):
    return jnp.broadcast_to(x[:, i : i + 1], WIDE)


def factor(g, emit):
    rows = [g[8 * i : 8 * i + 8] for i in range(8)]
    cols = [on_lanes(rows[0], a) for a in range(8)]
    for p in range(8):
        mine, steps, done = rows[p], [], []
        if p < 7:
            beside = [on_lanes(rows[p + 1], 8 * p + a) for a in range(8)]
            ahead = [on_lanes(rows[p + 1], 8 * p + 8 + a) for a in range(8)]
        for a in range(8):
            pivot = on_lines(cols[a], a)
            inverse = 1.0 / pivot
            row = on_lines(mine, a)
            done.append(row[0:1] * lax.rsqrt(pivot[0:1]))
            heads = [on_lines(cols[b], a) if b > a else None for b in range(8)]
            times = cols[a] * inverse
            for b in range(a + 1, 8):
                cols[b] = cols[b] - times * heads[b]
            mine = mine - times * row
            if p < 7:
                times = beside[a] * inverse
                for b in range(a + 1, 8):
                    beside[b] = beside[b] - times * heads[b]
                for b in range(8):
                    ahead[b] = ahead[b] - times * on_lines(beside[a], b)
                rows[p + 1] = rows[p + 1] - times * row
            steps.append((inverse, row, heads))
        for r in range(p + 2, 8):
            below = [on_lanes(rows[r], 8 * p + a) for a in range(8)]
            for a, (inverse, row, heads) in enumerate(steps):
                times = below[a] * inverse
                for b in range(a + 1, 8):
                    below[b] = below[b] - times * heads[b]
                rows[r] = rows[r] - times * row
        emit(p, jnp.concatenate(done, 0))
        if p < 7:
            cols = ahead


def patterns():
    lane = lax.broadcasted_iota(jnp.int32, (N, 128), 1)
    line = lax.broadcasted_iota(jnp.int32, (N, 128), 0)
    low = lane < N
    place = jnp.where(low, lane, lane - N)
    eye = jnp.where(place == line, 1.0, 0.0).astype(jnp.float32)
    return line, low, place, eye


def absorb(lefts, rights, acc, start, width, tiles, first):
    def tile(n, carry):
        at = pl.ds(pl.multiple_of(start + n * width, 128), width)
        total = sum(dot(left, right[:, at], NN) for left, right in zip(lefts, rights))
        acc[:, at] = total if first else acc[:, at] + total
        return carry

    if tiles == 1:
        tile(0, 0)
    else:
        lax.fori_loop(0, tiles, tile, 0)


def flip(raw, ops):
    def one(s, carry):
        ops[s] = raw[s].astype(jnp.float32).T.astype(jnp.bfloat16)
        return carry

    lax.fori_loop(0, 8, one, 0)


def to_columns(acc, rows, at, q):
    low = lax.broadcasted_iota(jnp.int32, (32, 128), 1) < N
    for m in range(32):
        v = acc[:, 128 * m : 128 * m + 128]
        w = pltpu.roll(v, N, 1)
        rows[pl.ds(2 * m, 32, stride=N), :] = jnp.where(low, v[0:32], w[32:64])
        rows[pl.ds(2 * m + 1, 32, stride=N), :] = jnp.where(low, w[0:32], v[32:64])
    for t in range(16):
        hi, lo = split(rows[128 * t : 128 * t + 128, :].T)
        at[q, 128 * t : 128 * t + 128, 0:128] = hi
        at[q, 128 * t : 128 * t + 128, 128:256] = lo


def advance(left, unit, keep, at, mixed, next_left, inverses, q, begin):
    line, low, place, eye = patterns()
    both = jnp.concatenate([jnp.where(low, left, 0.0), jnp.where(low, 0.0, pltpu.roll(left, N, 1))], 0)
    hi, lo = split(both)
    weights = jnp.concatenate(
        [jnp.concatenate([hi, hi], 1), jnp.concatenate([lo, jnp.zeros_like(lo)], 1)], 0
    )
    for t in range(0, 16, 2):
        o = dot(at[q, 128 * t : 128 * t + 256, :], weights, NT)
        hi, lo = split(o[:, 0:128] + o[:, 128:256])
        for u in range(2):
            lanes = slice(128 * (t + u), 128 * (t + u) + 128)
            mixed[q, 0:128, lanes] = hi[128 * u : 128 * u + 128]
            mixed[q, 128:256, lanes] = lo[128 * u : 128 * u + 128]
    y = mixed[q]
    g = dot(y, y, NT)
    g = g[0:128] + g[128:256]
    g = g[:, 0:128] + g[:, 128:256]
    total = jnp.sum(jnp.where(low, left * left, 0.0), keepdims=True)
    scale = lax.rsqrt(total * (1.0 / (N * N)) + 1e-06)
    scale = jnp.ones_like(scale) if unit else scale
    full = (g[0:N] + pltpu.roll(g[N:], N, 1)) * (scale * scale)

    def emit(p, rows):
        part = slice(8 * p, 8 * p + 8)
        upper = jnp.logical_and(low[part], place[part] >= line[part])
        next_left[part, :] = jnp.where(jnp.logical_and(keep[part], upper), rows, 0.0)
        inverses[q, part, :] = jnp.where(jnp.logical_or(low[part], jnp.logical_not(keep[part])), 0.0, rows) * (scale * float(N))
        if begin is not None:
            begin(p)

    factor(jnp.where(low, full, eye), emit)


def results(inverses, mixed, rows, out, q):
    inverse = inverses[q]
    pair = jnp.concatenate([pltpu.roll(inverse, N, 1), inverse], 0)
    p_hi, p_lo = split(pair)
    wide = jnp.concatenate([p_hi, p_hi], 1)
    for c in range(8):
        y = mixed[q, :, 256 * c : 256 * c + 256]
        o = dot(wide, y, NN) + dot(p_lo, y[0:128], NN)
        rows[256 * c : 256 * c + 128, :] = o[:, 0:128].T
        rows[256 * c + 128 : 256 * c + 256, :] = o[:, 128:256].T
    low = lax.broadcasted_iota(jnp.int32, (32, 128), 1) < N
    for m in range(32):
        e = rows[pl.ds(2 * m, 32, stride=N), :]
        d = rows[pl.ds(2 * m + 1, 32, stride=N), :]
        at = slice(128 * m, 128 * m + 128)
        out[q, 0:32, at] = jnp.where(low, e, pltpu.roll(d, N, 1)).astype(jnp.bfloat16)
        out[q, 32:64, at] = jnp.where(low, pltpu.roll(e, N, 1), d).astype(jnp.bfloat16)


def sweep_kernel(
    ranks_ref, ops_ref, bnd_ref, out_ref,
    blocks, raw, ops, ranks, limits, acc, second, rows, at, mixed, out, inverses, l_in, l_out, left_ref,
    guests, guest_raw, guest_ops, guest_sums, part_send, part_recv, own_sem, ring_send, ring_recv, l_send, l_recv, out_send, out_recv, out_own,
    gift_send, gift_recv, back_send, back_recv, lent_send, lent_recv, hop_send,
):
    me = lax.axis_index("col")
    columns = lax.axis_size("col")
    z = lax.axis_index("sec")
    size = lax.axis_size("sec")
    core = lax.rem(me, 2)
    partner = me + 1 - 2 * core
    up, down = lax.rem(z + 1, size), lax.rem(z + size - 1, size)
    after, before = lax.rem(me + 2, columns), lax.rem(me + columns - 2, columns)
    is_first = me < 2
    band = columns // 4
    row = me // band
    peer = me + band * (3 - 2 * row)

    for b in range(2):
        ranks[b] = jnp.full((8, 128), ranks_ref[0, b, 0].astype(jnp.float32))
    barrier = pltpu.get_barrier_semaphore()
    peer_partner = peer + 1 - 2 * core
    beside = me + band * (1 - 2 * lax.rem(row, 2))
    beside_partner = beside + 1 - 2 * core
    greeted = (
        (partner, z), (me, up), (me, down), (partner, up), (partner, down), (before, z), (peer, z), (peer_partner, z),
        (beside, z), (beside_partner, z),
    )
    for to in greeted:
        pl.semaphore_signal(barrier, inc=1, device_id=to, device_id_type=MESH)
    pl.semaphore_wait(barrier, len(greeted))

    def to_partner(n, source, target):
        return pltpu.make_async_remote_copy(
            src_ref=source, dst_ref=target, send_sem=part_send.at[n], recv_sem=part_recv.at[n],
            device_id=(partner, z), device_id_type=MESH,
        )

    crossing = [
        to_partner(0, bnd_ref.at[0, 1 - core, 0], blocks.at[core, z]),
        to_partner(1, ops_ref.at[1 - core, 0, :, z], raw.at[core]),
        to_partner(2, ranks.at[1 - core], limits.at[core]),
    ]
    staying = [
        pltpu.make_async_copy(bnd_ref.at[0, core, 0], blocks.at[core, z], own_sem.at[0]),
        pltpu.make_async_copy(ops_ref.at[core, 0, :, z], raw.at[core], own_sem.at[1]),
        pltpu.make_async_copy(ranks.at[core], limits.at[core], own_sem.at[2]),
    ]
    for copy in crossing + staying:
        copy.start()

    edges = {1: (0, OWN), 2: (OWN, MIDDLE), 3: (MIDDLE, N * N)}

    def chunk(c):
        return slice(CHUNK * c, CHUNK * c + CHUNK)

    def far_chunk(c):
        return slice(OWN + CHUNK * c, OWN + CHUNK * c + CHUNK)

    def ring(flow, way, d, half):
        block = lax.rem(z + size + (d - 1 if way else 1 - d), size)
        lines = slice(32 * half, 32 * half + 32)
        if flow == 0:
            part = blocks.at[0, block, lines]
        elif flow < 4:
            part = blocks.at[1, block, lines, edges[flow][0] : edges[flow][1]]
        else:
            part = guests.at[block, lines, chunk(flow - 4)]
        return pltpu.make_async_remote_copy(
            src_ref=part, dst_ref=part, send_sem=ring_send.at[flow, way, d - 1, half],
            recv_sem=ring_recv.at[flow, way, d - 1, half],
            device_id=(me, down if way else up), device_id_type=MESH,
        )

    def first_hop(flow, way, half, b):
        q = 0 if flow == 0 else 1
        lines = slice(32 * half, 32 * half + 32)
        lanes = slice(*edges[flow]) if flow else slice(0, N * N)
        return pltpu.make_async_remote_copy(
            src_ref=bnd_ref.at[0, b, 0, lines, lanes], dst_ref=blocks.at[q, z, lines, lanes],
            send_sem=hop_send.at[flow, way, half, b], recv_sem=ring_recv.at[flow, way, 0, half],
            device_id=(me - core + b, down if way else up), device_id_type=MESH,
        )

    def gift(c, half, b):
        lines = slice(32 * half, 32 * half + 32)
        return pltpu.make_async_remote_copy(
            src_ref=bnd_ref.at[0, b, 0, lines, far_chunk(c)], dst_ref=guests.at[z, lines, chunk(c)],
            send_sem=gift_send.at[c, half, b], recv_sem=gift_recv.at[c, half],
            device_id=((beside if c == 3 else peer) - core + b, z), device_id_type=MESH,
        )

    def lent(b, to_beside):
        return pltpu.make_async_remote_copy(
            src_ref=ops_ref.at[b, 0, :, z], dst_ref=guest_raw, send_sem=lent_send.at[to_beside, b], recv_sem=lent_recv,
            device_id=((beside if to_beside else peer) - core + b, z), device_id_type=MESH,
        )

    def back(c):
        return pltpu.make_async_remote_copy(
            src_ref=guest_sums.at[:, chunk(c)], dst_ref=second.at[:, far_chunk(c)],
            send_sem=back_send.at[c], recv_sem=back_recv.at[c],
            device_id=(beside if c == 3 else peer, z), device_id_type=MESH,
        )

    def parts(d):
        return [(way, d, half) for half in range(2) for way in range(2) if d < 4 or half == way]

    def ready(q):
        @pl.when(core == q)
        def _():
            staying[0].wait()

        @pl.when(core != q)
        def _():
            crossing[0].wait_recv()

    def hops():
        return [(way, half, b) for half in range(2) for way in range(2) for b in range(2)]

    def begin(flow):
        @pl.when(core == (0 if flow == 0 else 1))
        def _():
            for hop in hops():
                first_hop(flow, *hop).start()

    def turn(flow, d):
        for way, _, half in parts(d):
            ring(flow, way, d, half).wait_recv()
            if d < 4 and (way, d + 1, half) in parts(d + 1):
                ring(flow, way, d + 1, half).start()

    def sectors(d):
        before, after = lax.rem(z + size - d, size), lax.rem(z + d, size)
        return [z] if d == 0 else [after] if d == 4 else [before, after]

    def absorb_flow(flow, d):
        q = 0 if flow == 0 else 1
        start, width, tiles = {0: (0, 512, 8), 1: (0, 512, 1), 2: (OWN, 256, 7), 3: (MIDDLE, 256, 7)}[flow]
        absorb(
            [ops[q, s] for s in sectors(d)], [blocks.at[q, s] for s in sectors(d)],
            second if q else acc, start, width, tiles, d == 0,
        )

    def open_guest(c):
        for half in range(2):
            gift(c, half, 0).wait_recv()
            for way in range(2):
                ring(4 + c, way, 1, half).start()

    def borrow():
        lent(0, 0).wait_recv()
        flip(guest_raw, guest_ops)

    def give_back(c):
        lefts = [guest_ops[s] for s in range(8)]
        rights = [guests.at[s] for s in range(8)]
        for start, width in ((0, 256), (256, 256), (512, 256), (768, 128)):
            absorb(lefts, rights, guest_sums, CHUNK * c + start, width, 1, True)
        back(c).start()

    def serve(count, at_end):
        open_guest(0)
        open_guest(1)
        for slot in range(1, 2 * count + 3):
            for c in range(count):
                d = slot - 2 * c
                if not 1 <= d <= 4:
                    continue
                turn(4 + c, d)
                if d == 3 and c + 2 < count:
                    open_guest(c + 2)
                if d == 3 and c == count - 1:
                    at_end()
                if d == 4:
                    if c == 0:
                        borrow()
                    give_back(c)

    def begin_own():
        begin(0)
        begin(1)

    @pl.when(jnp.logical_and(row < 2, core == 1))
    def _():
        for c in range(2):
            for half in range(2):
                for b in range(2):
                    gift(c, half, b).start()

    @pl.when(row < 3)
    def _():
        begin_own()

    @pl.when(jnp.logical_and(row == 0, core == 1))
    def _():
        for c in (3, 2):
            for half in range(2):
                for b in range(2):
                    gift(c, half, b).start()
        for b in range(2):
            lent(b, 1).start()

    @pl.when(jnp.logical_and(row < 2, core == 1))
    def _():
        for b in range(2):
            lent(b, 0).start()

    @pl.when(row == 1)
    def _():
        open_guest(3)

    @pl.when(row == 2)
    def _():
        open_guest(0)
        open_guest(1)

    @pl.when(row == 3)
    def _():
        serve(3, begin_own)

    ready(0)
    ready(1)
    for copy in staying[1:]:
        copy.wait()
    for copy in crossing[1:]:
        copy.wait_recv()
    for q in range(2):
        flip(raw.at[q], ops.at[q])

    for d in range(5):
        if d > 0:
            @pl.when(row == 1)
            def _():
                if d < 3:
                    turn(7, 2 * d - 1)

            turn(0, d)
            turn(1, d)

            @pl.when(row == 1)
            def _():
                if d < 3:
                    turn(7, 2 * d)
                if d == 2:
                    borrow()
                    give_back(3)

            @pl.when(row == 2)
            def _():
                turn(4, d)
                turn(5, d)
                if d == 4:
                    borrow()
                    give_back(0)
                    give_back(1)

        if d == 3:

            @pl.when(row >= 2)
            def _():
                begin(2)

            @pl.when(row >= 1)
            def _():
                begin(3)

        absorb_flow(0, d)
        absorb_flow(1, d)
    to_columns(acc, rows, at, 0)
    for d in range(5):

        @pl.when(row >= 2)
        def _():
            if d > 0:
                turn(2, d)
            absorb_flow(2, d)

        @pl.when(row >= 1)
        def _():
            if d > 0:
                turn(3, d)
            absorb_flow(3, d)

    line, low, place, eye = patterns()

    def along(part, start, size):
        return pltpu.make_async_remote_copy(
            src_ref=l_out.at[start : start + size], dst_ref=l_in.at[start : start + size],
            send_sem=l_send.at[part], recv_sem=l_recv.at[part], device_id=(after, z), device_id_type=MESH,
        )

    pieces = {3: along(0, 0, 32), 5: along(1, 32, 16), 6: along(2, 48, 8), 7: along(3, 56, 8)}

    def keep(q):
        return line.astype(jnp.float32) < limits[q, 0:1, :]

    def begin_piece(p):
        if p in pieces:
            pieces[p].start()

    @pl.when(is_first)
    def _():
        advance(eye, True, keep(0), at, mixed, left_ref, inverses, 0, None)

    @pl.when(row < 2)
    def _():
        for c in range(2):
            back(c).wait_recv()

    @pl.when(row == 0)
    def _():
        for c in range(2, 4):
            back(c).wait_recv()

    to_columns(second, rows, at, 1)

    @pl.when(jnp.logical_not(is_first))
    def _():
        for piece in pieces.values():
            piece.wait_recv()
        advance(l_in[...], False, keep(0), at, mixed, left_ref, inverses, 0, None)

    advance(left_ref[...], False, keep(1), at, mixed, l_out, inverses, 1, begin_piece)

    across = pltpu.make_async_remote_copy(
        src_ref=out.at[1 - core], dst_ref=out_ref.at[0, core, 0], send_sem=out_send, recv_sem=out_recv,
        device_id=(partner, z), device_id_type=MESH,
    )
    home = pltpu.make_async_copy(out.at[core], out_ref.at[0, core, 0], out_own)

    for q in range(2):
        results(inverses, mixed, rows, out, q)

        @pl.when(core == q)
        def _():
            home.start()

        @pl.when(core != q)
        def _():
            across.start()

    home.wait()
    across.wait()

    for piece in pieces.values():
        piece.wait_send()

    @pl.when(is_first)
    def _():
        for piece in pieces.values():
            piece.wait_recv()

    for copy in crossing:
        copy.wait_send()
    late = [part for d in range(2, 5) for part in parts(d)]

    def sent(*flows):
        for flow in flows:
            for part in late + (parts(1) if flow > 3 else []):
                ring(flow, *part).wait_send()
            if flow < 4:

                @pl.when(core == (0 if flow == 0 else 1))
                def _():
                    for hop in hops():
                        first_hop(flow, *hop).wait_send()

    sent(0, 1)

    @pl.when(row >= 2)
    def _():
        sent(2, 4, 5)
        for c in range(2):
            back(c).wait_send()

    @pl.when(row >= 1)
    def _():
        sent(3)

    @pl.when(row == 3)
    def _():
        sent(6)
        back(2).wait_send()

    @pl.when(row == 1)
    def _():
        sent(7)
        back(3).wait_send()

    @pl.when(jnp.logical_and(row < 2, core == 1))
    def _():
        for b in range(2):
            lent(b, 0).wait_send()
            for c in range(2):
                for half in range(2):
                    gift(c, half, b).wait_send()

    @pl.when(jnp.logical_and(row == 0, core == 1))
    def _():
        for b in range(2):
            lent(b, 1).wait_send()
            for c in range(2, 4):
                for half in range(2):
                    gift(c, half, b).wait_send()


def sweep(ranks, ops, boundaries):
    anywhere = pl.BlockSpec(memory_space=pltpu.HBM)
    bf16, f32 = jnp.bfloat16, jnp.float32
    dma = pltpu.SemaphoreType.DMA
    return pl.pallas_call(
        sweep_kernel,
        out_shape=jax.ShapeDtypeStruct(boundaries.shape, bf16),
        in_specs=[pl.BlockSpec(memory_space=pltpu.SMEM), anywhere, anywhere],
        out_specs=anywhere,
        scratch_shapes=[
            pltpu.VMEM((2, 8, N, N * N), bf16),
            pltpu.VMEM((2, 8, N, N), bf16),
            pltpu.VMEM((2, 8, N, N), bf16),
            pltpu.VMEM((2, 8, 128), f32),
            pltpu.VMEM((2, 8, 128), f32),
            pltpu.VMEM((N, N * N), f32),
            pltpu.VMEM((N, N * N), f32),
            pltpu.VMEM((2048, 128), f32),
            pltpu.VMEM((2, 2048, 256), bf16),
            pltpu.VMEM((2, 256, 2048), bf16),
            pltpu.VMEM((2, N, N * N), bf16),
            pltpu.VMEM((2, N, 128), f32),
            pltpu.VMEM((N, 128), f32),
            pltpu.VMEM((N, 128), f32),
            pltpu.VMEM((N, 128), f32),
            pltpu.VMEM((8, N, 4 * CHUNK), bf16),
            pltpu.VMEM((8, N, N), bf16),
            pltpu.VMEM((8, N, N), bf16),
            pltpu.VMEM((N, 4 * CHUNK), f32),
            dma((3,)), dma((3,)), dma((3,)),
            dma((8, 2, 4, 2)), dma((8, 2, 4, 2)),
            dma((4,)), dma((4,)), dma, dma, dma,
            dma((4, 2, 2)), dma((4, 2)), dma((4,)), dma((4,)), dma((2, 2)), dma, dma((4, 2, 2, 2)),
        ],
        compiler_params=pltpu.CompilerParams(
            collective_id=0, has_side_effects=True, vmem_limit_bytes=60 * 1024 * 1024
        ),
    )(ranks, ops, boundaries)


def on_device(boundaries, row_ops, ranks):
    return sweep(ranks, row_ops, boundaries)


def solution(mesh):
    placed = (
        P("sec", None, "col", None, None),
        P(None, "col", None, None, None, None),
        P("sec", None, "col"),
    )
    return jax.shard_map(
        on_device,
        mesh=mesh,
        in_specs=placed,
        out_specs=P("sec", None, "col", None, None),
        check_vma=False,
    )
```

```python
import functools
import math

import jax
import jax.numpy as jnp
from jax import lax
from jax.experimental import pallas as pl
from jax.experimental.pallas import tpu as pltpu
from jax.sharding import PartitionSpec as P

MESH = pl.DeviceIdType.MESH
N = 64
CHUNKS = (1024, 1024, 640, 896)
OWN = 512
MIDDLE = OWN + CHUNKS[0] + CHUNKS[1]
NT = (((1,), (1,)), ((), ()))
NN = (((1,), (0,)), ((), ()))


def dot(a, b, dims):
    return lax.dot_general(a, b, dims, preferred_element_type=jnp.float32)


def split(x):
    hi = x.astype(jnp.bfloat16)
    lo = (x - hi.astype(jnp.float32)).astype(jnp.bfloat16)
    return hi, lo


WIDE = (8, 128)


def on_lines(x, i):
    return jnp.broadcast_to(x[i : i + 1, :], WIDE)


def on_lanes(x, i):
    return jnp.broadcast_to(x[:, i : i + 1], WIDE)


def factor(g, emit):
    rows = [g[8 * i : 8 * i + 8] for i in range(8)]
    cols = [on_lanes(rows[0], a) for a in range(8)]
    for p in range(8):
        mine, steps, done = rows[p], [], []
        if p < 7:
            beside = [on_lanes(rows[p + 1], 8 * p + a) for a in range(8)]
            ahead = [on_lanes(rows[p + 1], 8 * p + 8 + a) for a in range(8)]
        for a in range(8):
            pivot = on_lines(cols[a], a)
            inverse = 1.0 / pivot
            row = on_lines(mine, a)
            done.append(row[0:1] * lax.rsqrt(pivot[0:1]))
            heads = [on_lines(cols[b], a) if b > a else None for b in range(8)]
            times = cols[a] * inverse
            for b in range(a + 1, 8):
                cols[b] = cols[b] - times * heads[b]
            mine = mine - times * row
            if p < 7:
                times = beside[a] * inverse
                for b in range(a + 1, 8):
                    beside[b] = beside[b] - times * heads[b]
                for b in range(8):
                    ahead[b] = ahead[b] - times * on_lines(beside[a], b)
                rows[p + 1] = rows[p + 1] - times * row
            steps.append((inverse, row, heads))
        for r in range(p + 2, 8):
            below = [on_lanes(rows[r], 8 * p + a) for a in range(8)]
            for a, (inverse, row, heads) in enumerate(steps):
                times = below[a] * inverse
                for b in range(a + 1, 8):
                    below[b] = below[b] - times * heads[b]
                rows[r] = rows[r] - times * row
        emit(p, jnp.concatenate(done, 0))
        if p < 7:
            cols = ahead


def patterns():
    lane = lax.broadcasted_iota(jnp.int32, (N, 128), 1)
    line = lax.broadcasted_iota(jnp.int32, (N, 128), 0)
    low = lane < N
    place = jnp.where(low, lane, lane - N)
    eye = jnp.where(place == line, 1.0, 0.0).astype(jnp.float32)
    return line, low, place, eye


def absorb(lefts, rights, acc, start, width, tiles, first):
    def tile(n, carry):
        at = pl.ds(pl.multiple_of(start + n * width, 128), width)
        total = sum(dot(left, right[:, at], NN) for left, right in zip(lefts, rights))
        acc[:, at] = total if first else acc[:, at] + total
        return carry

    if tiles == 1:
        tile(0, 0)
    else:
        lax.fori_loop(0, tiles, tile, 0)


def flip(raw, ops):
    def one(s, carry):
        ops[s] = raw[s].astype(jnp.float32).T.astype(jnp.bfloat16)
        return carry

    lax.fori_loop(0, 8, one, 0)


def to_columns(acc, rows, at, q):
    low = lax.broadcasted_iota(jnp.int32, (32, 128), 1) < N
    for m in range(32):
        v = acc[:, 128 * m : 128 * m + 128]
        w = pltpu.roll(v, N, 1)
        rows[pl.ds(2 * m, 32, stride=N), :] = jnp.where(low, v[0:32], w[32:64])
        rows[pl.ds(2 * m + 1, 32, stride=N), :] = jnp.where(low, w[0:32], v[32:64])
    for t in range(16):
        hi, lo = split(rows[128 * t : 128 * t + 128, :].T)
        at[q, 128 * t : 128 * t + 128, 0:128] = hi
        at[q, 128 * t : 128 * t + 128, 128:256] = lo


def advance(left, unit, keep, at, mixed, next_left, inverses, q, begin):
    line, low, place, eye = patterns()
    both = jnp.concatenate([jnp.where(low, left, 0.0), jnp.where(low, 0.0, pltpu.roll(left, N, 1))], 0)
    hi, lo = split(both)
    weights = jnp.concatenate(
        [jnp.concatenate([hi, hi], 1), jnp.concatenate([lo, jnp.zeros_like(lo)], 1)], 0
    )
    for t in range(0, 16, 2):
        o = dot(at[q, 128 * t : 128 * t + 256, :], weights, NT)
        hi, lo = split(o[:, 0:128] + o[:, 128:256])
        for u in range(2):
            lanes = slice(128 * (t + u), 128 * (t + u) + 128)
            mixed[q, 0:128, lanes] = hi[128 * u : 128 * u + 128]
            mixed[q, 128:256, lanes] = lo[128 * u : 128 * u + 128]
    y = mixed[q]
    g = dot(y, y, NT)
    g = g[0:128] + g[128:256]
    g = g[:, 0:128] + g[:, 128:256]
    total = jnp.sum(jnp.where(low, left * left, 0.0), keepdims=True)
    scale = lax.rsqrt(total * (1.0 / (N * N)) + 1e-06)
    scale = jnp.ones_like(scale) if unit else scale
    full = (g[0:N] + pltpu.roll(g[N:], N, 1)) * (scale * scale)

    def emit(p, rows):
        part = slice(8 * p, 8 * p + 8)
        upper = jnp.logical_and(low[part], place[part] >= line[part])
        next_left[part, :] = jnp.where(jnp.logical_and(keep[part], upper), rows, 0.0)
        inverses[q, part, :] = jnp.where(jnp.logical_or(low[part], jnp.logical_not(keep[part])), 0.0, rows) * (scale * float(N))
        if begin is not None:
            begin(p)

    factor(jnp.where(low, full, eye), emit)


def results(inverses, mixed, rows, out, q):
    inverse = inverses[q]
    pair = jnp.concatenate([pltpu.roll(inverse, N, 1), inverse], 0)
    p_hi, p_lo = split(pair)
    wide = jnp.concatenate([p_hi, p_hi], 1)
    for c in range(8):
        y = mixed[q, :, 256 * c : 256 * c + 256]
        o = dot(wide, y, NN) + dot(p_lo, y[0:128], NN)
        rows[256 * c : 256 * c + 128, :] = o[:, 0:128].T
        rows[256 * c + 128 : 256 * c + 256, :] = o[:, 128:256].T
    low = lax.broadcasted_iota(jnp.int32, (32, 128), 1) < N
    for m in range(32):
        e = rows[pl.ds(2 * m, 32, stride=N), :]
        d = rows[pl.ds(2 * m + 1, 32, stride=N), :]
        at = slice(128 * m, 128 * m + 128)
        out[q, 0:32, at] = jnp.where(low, e, pltpu.roll(d, N, 1)).astype(jnp.bfloat16)
        out[q, 32:64, at] = jnp.where(low, pltpu.roll(e, N, 1), d).astype(jnp.bfloat16)


def sweep_kernel(
    ranks_ref, ops_ref, bnd_ref, out_ref,
    blocks, raw, ops, ranks, limits, acc, second, rows, at, mixed, out, inverses, l_in, l_out, left_ref,
    guests, guest_raw, guest_ops, guest_sums, part_send, part_recv, own_sem, ring_send, ring_recv, l_send, l_recv, out_send, out_recv, out_own,
    gift_send, gift_recv, back_send, back_recv, lent_send, lent_recv, hop_send,
):
    me = lax.axis_index("col")
    columns = lax.axis_size("col")
    z = lax.axis_index("sec")
    size = lax.axis_size("sec")
    core = lax.rem(me, 2)
    partner = me + 1 - 2 * core
    up, down = lax.rem(z + 1, size), lax.rem(z + size - 1, size)
    after, before = lax.rem(me + 2, columns), lax.rem(me + columns - 2, columns)
    is_first = me < 2
    band = columns // 4
    row = me // band
    peer = me + band * (3 - 2 * row)

    for b in range(2):
        ranks[b] = jnp.full((8, 128), ranks_ref[b].astype(jnp.float32))
    barrier = pltpu.get_barrier_semaphore()
    peer_partner = peer + 1 - 2 * core
    beside = me + band * (1 - 2 * lax.rem(row, 2))
    beside_partner = beside + 1 - 2 * core
    greeted = (
        (partner, z), (me, up), (me, down), (partner, up), (partner, down), (before, z), (peer, z), (peer_partner, z),
        (beside, z), (beside_partner, z),
    )
    for to in greeted:
        pl.semaphore_signal(barrier, inc=1, device_id=to, device_id_type=MESH)
    pl.semaphore_wait(barrier, len(greeted))

    def to_partner(n, source, target):
        return pltpu.make_async_remote_copy(
            src_ref=source, dst_ref=target, send_sem=part_send.at[n], recv_sem=part_recv.at[n],
            device_id=(partner, z), device_id_type=MESH,
        )

    crossing = [
        to_partner(0, bnd_ref.at[0, 1 - core, 0], blocks.at[core, z]),
        to_partner(1, ops_ref.at[1 - core, 0, :, z], raw.at[core]),
        to_partner(2, ranks.at[1 - core], limits.at[core]),
    ]
    staying = [
        pltpu.make_async_copy(bnd_ref.at[0, core, 0], blocks.at[core, z], own_sem.at[0]),
        pltpu.make_async_copy(ops_ref.at[core, 0, :, z], raw.at[core], own_sem.at[1]),
        pltpu.make_async_copy(ranks.at[core], limits.at[core], own_sem.at[2]),
    ]
    for copy in crossing + staying:
        copy.start()

    edges = {1: (0, OWN), 2: (OWN, MIDDLE), 3: (MIDDLE, N * N)}

    def chunk(c):
        return slice(sum(CHUNKS[:c]), sum(CHUNKS[: c + 1]))

    def far_chunk(c):
        return slice(OWN + sum(CHUNKS[:c]), OWN + sum(CHUNKS[: c + 1]))

    def ring(flow, way, d, half):
        block = lax.rem(z + size + (d - 1 if way else 1 - d), size)
        lines = slice(32 * half, 32 * half + 32)
        if flow == 0:
            part = blocks.at[0, block, lines]
        elif flow < 4:
            part = blocks.at[1, block, lines, edges[flow][0] : edges[flow][1]]
        else:
            part = guests.at[block, lines, chunk(flow - 4)]
        return pltpu.make_async_remote_copy(
            src_ref=part, dst_ref=part, send_sem=ring_send.at[flow, way, d - 1, half],
            recv_sem=ring_recv.at[flow, way, d - 1, half],
            device_id=(me, down if way else up), device_id_type=MESH,
        )

    def first_hop(flow, way, half, b):
        q = 0 if flow == 0 else 1
        lines = slice(32 * half, 32 * half + 32)
        lanes = slice(*edges[flow]) if flow else slice(0, N * N)
        return pltpu.make_async_remote_copy(
            src_ref=bnd_ref.at[0, b, 0, lines, lanes], dst_ref=blocks.at[q, z, lines, lanes],
            send_sem=hop_send.at[flow, way, half, b], recv_sem=ring_recv.at[flow, way, 0, half],
            device_id=(me - core + b, down if way else up), device_id_type=MESH,
        )

    def gift(c, half, b):
        lines = slice(32 * half, 32 * half + 32)
        return pltpu.make_async_remote_copy(
            src_ref=bnd_ref.at[0, b, 0, lines, far_chunk(c)], dst_ref=guests.at[z, lines, chunk(c)],
            send_sem=gift_send.at[c, half, b], recv_sem=gift_recv.at[c, half],
            device_id=((beside if c == 3 else peer) - core + b, z), device_id_type=MESH,
        )

    def lent(b, to_beside):
        return pltpu.make_async_remote_copy(
            src_ref=ops_ref.at[b, 0, :, z], dst_ref=guest_raw, send_sem=lent_send.at[to_beside, b], recv_sem=lent_recv,
            device_id=((beside if to_beside else peer) - core + b, z), device_id_type=MESH,
        )

    def back(c):
        return pltpu.make_async_remote_copy(
            src_ref=guest_sums.at[:, chunk(c)], dst_ref=second.at[:, far_chunk(c)],
            send_sem=back_send.at[c], recv_sem=back_recv.at[c],
            device_id=(beside if c == 3 else peer, z), device_id_type=MESH,
        )

    def parts(d):
        return [(way, d, half) for half in range(2) for way in range(2) if d < 4 or half == way]

    def ready(q):
        @pl.when(core == q)
        def _():
            staying[0].wait()

        @pl.when(core != q)
        def _():
            crossing[0].wait_recv()

    def hops():
        return [(way, half, b) for half in range(2) for way in range(2) for b in range(2)]

    def begin(flow):
        @pl.when(core == (0 if flow == 0 else 1))
        def _():
            for hop in hops():
                first_hop(flow, *hop).start()

    def turn(flow, d):
        for way, _, half in parts(d):
            ring(flow, way, d, half).wait_recv()
            if d < 4 and (way, d + 1, half) in parts(d + 1):
                ring(flow, way, d + 1, half).start()

    def sectors(d):
        before, after = lax.rem(z + size - d, size), lax.rem(z + d, size)
        return [z] if d == 0 else [after] if d == 4 else [before, after]

    def absorb_flow(flow, d):
        q = 0 if flow == 0 else 1
        start, width, tiles = {0: (0, 512, 8), 1: (0, 512, 1), 2: (OWN, 256, 8), 3: (MIDDLE, 256, 6)}[flow]
        absorb(
            [ops[q, s] for s in sectors(d)], [blocks.at[q, s] for s in sectors(d)],
            second if q else acc, start, width, tiles, d == 0,
        )

    def open_guest(c):
        for half in range(2):
            gift(c, half, 0).wait_recv()
            for way in range(2):
                ring(4 + c, way, 1, half).start()

    def borrow():
        lent(0, 0).wait_recv()
        flip(guest_raw, guest_ops)

    def give_back(c):
        lefts = [guest_ops[s] for s in range(8)]
        rights = [guests.at[s] for s in range(8)]
        wide, rest = CHUNKS[c] // 256, CHUNKS[c] % 256
        absorb(lefts, rights, guest_sums, chunk(c).start, 256, wide, True)
        if rest:
            absorb(lefts, rights, guest_sums, chunk(c).stop - rest, rest, 1, True)
        back(c).start()

    def serve(count, at_end):
        open_guest(0)
        open_guest(1)
        for slot in range(1, 2 * count + 3):
            for c in range(count):
                d = slot - 2 * c
                if not 1 <= d <= 4:
                    continue
                turn(4 + c, d)
                if d == 3 and c + 2 < count:
                    open_guest(c + 2)
                if d == 3 and c == count - 1:
                    at_end()
                if d == 4:
                    if c == 0:
                        borrow()
                    give_back(c)

    def begin_own():
        begin(0)
        begin(1)

    @pl.when(jnp.logical_and(row < 2, core == 1))
    def _():
        for c in range(2):
            for half in range(2):
                for b in range(2):
                    gift(c, half, b).start()

    @pl.when(row < 3)
    def _():
        begin_own()

    @pl.when(jnp.logical_and(row == 0, core == 1))
    def _():
        for c in (3, 2):
            for half in range(2):
                for b in range(2):
                    gift(c, half, b).start()
        for b in range(2):
            lent(b, 1).start()

    @pl.when(jnp.logical_and(row < 2, core == 1))
    def _():
        for b in range(2):
            lent(b, 0).start()

    @pl.when(row == 1)
    def _():
        open_guest(3)

    @pl.when(row == 2)
    def _():
        open_guest(0)
        open_guest(1)

    @pl.when(row == 3)
    def _():
        serve(3, begin_own)

    ready(0)
    ready(1)
    for copy in staying[1:]:
        copy.wait()
    for copy in crossing[1:]:
        copy.wait_recv()
    for q in range(2):
        flip(raw.at[q], ops.at[q])

    for d in range(5):
        if d > 0:

            def guests_turn(step):
                @pl.when(row == 1)
                def _():
                    turn(7, step)

                @pl.when(row == 2)
                def _():
                    turn(4, step)
                    turn(5, step)

            if d < 3:
                guests_turn(2 * d - 1)
            turn(0, d)
            turn(1, d)
            if d < 3:
                guests_turn(2 * d)
            if d == 2:

                @pl.when(row == 1)
                def _():
                    borrow()
                    give_back(3)

                @pl.when(row == 2)
                def _():
                    borrow()
                    give_back(0)
                    give_back(1)

        if d == 3:

            @pl.when(row >= 2)
            def _():
                begin(2)

            @pl.when(row >= 1)
            def _():
                begin(3)

        absorb_flow(0, d)
        absorb_flow(1, d)
    to_columns(acc, rows, at, 0)
    for d in range(5):

        @pl.when(row >= 2)
        def _():
            if d > 0:
                turn(2, d)
            absorb_flow(2, d)

        @pl.when(row >= 1)
        def _():
            if d > 0:
                turn(3, d)
            absorb_flow(3, d)

    line, low, place, eye = patterns()

    def along(part, start, size):
        return pltpu.make_async_remote_copy(
            src_ref=l_out.at[start : start + size], dst_ref=l_in.at[start : start + size],
            send_sem=l_send.at[part], recv_sem=l_recv.at[part], device_id=(after, z), device_id_type=MESH,
        )

    pieces = {3: along(0, 0, 32), 5: along(1, 32, 16), 6: along(2, 48, 8), 7: along(3, 56, 8)}

    def keep(q):
        return line.astype(jnp.float32) < limits[q, 0:1, :]

    def begin_piece(p):
        if p in pieces:
            pieces[p].start()

    @pl.when(is_first)
    def _():
        advance(eye, True, keep(0), at, mixed, left_ref, inverses, 0, None)

    @pl.when(row < 2)
    def _():
        for c in range(2):
            back(c).wait_recv()

    @pl.when(row == 0)
    def _():
        for c in range(2, 4):
            back(c).wait_recv()

    to_columns(second, rows, at, 1)

    @pl.when(jnp.logical_not(is_first))
    def _():
        for piece in pieces.values():
            piece.wait_recv()
        advance(l_in[...], False, keep(0), at, mixed, left_ref, inverses, 0, None)

    advance(left_ref[...], False, keep(1), at, mixed, l_out, inverses, 1, begin_piece)

    across = pltpu.make_async_remote_copy(
        src_ref=out.at[1 - core], dst_ref=out_ref.at[0, core, 0], send_sem=out_send, recv_sem=out_recv,
        device_id=(partner, z), device_id_type=MESH,
    )
    home = pltpu.make_async_copy(out.at[core], out_ref.at[0, core, 0], out_own)

    for q in range(2):
        results(inverses, mixed, rows, out, q)

        @pl.when(core == q)
        def _():
            home.start()

        @pl.when(core != q)
        def _():
            across.start()

    home.wait()
    across.wait()

    for piece in pieces.values():
        piece.wait_send()

    @pl.when(is_first)
    def _():
        for piece in pieces.values():
            piece.wait_recv()

    for copy in crossing:
        copy.wait_send()
    late = [part for d in range(2, 5) for part in parts(d)]

    def sent(*flows):
        for flow in flows:
            for part in late + (parts(1) if flow > 3 else []):
                ring(flow, *part).wait_send()
            if flow < 4:

                @pl.when(core == (0 if flow == 0 else 1))
                def _():
                    for hop in hops():
                        first_hop(flow, *hop).wait_send()

    sent(0, 1)

    @pl.when(row >= 2)
    def _():
        sent(2, 4, 5)
        for c in range(2):
            back(c).wait_send()

    @pl.when(row >= 1)
    def _():
        sent(3)

    @pl.when(row == 3)
    def _():
        sent(6)
        back(2).wait_send()

    @pl.when(row == 1)
    def _():
        sent(7)
        back(3).wait_send()

    @pl.when(jnp.logical_and(row < 2, core == 1))
    def _():
        for b in range(2):
            lent(b, 0).wait_send()
            for c in range(2):
                for half in range(2):
                    gift(c, half, b).wait_send()

    @pl.when(jnp.logical_and(row == 0, core == 1))
    def _():
        for b in range(2):
            lent(b, 1).wait_send()
            for c in range(2, 4):
                for half in range(2):
                    gift(c, half, b).wait_send()


def sweep(ranks, ops, boundaries):
    anywhere = pl.BlockSpec(memory_space=pltpu.HBM)
    bf16, f32 = jnp.bfloat16, jnp.float32
    dma = pltpu.SemaphoreType.DMA
    return pl.pallas_call(
        sweep_kernel,
        out_shape=jax.ShapeDtypeStruct(boundaries.shape, bf16),
        in_specs=[pl.BlockSpec(memory_space=pltpu.SMEM), anywhere, anywhere],
        out_specs=anywhere,
        scratch_shapes=[
            pltpu.VMEM((2, 8, N, N * N), bf16),
            pltpu.VMEM((2, 8, N, N), bf16),
            pltpu.VMEM((2, 8, N, N), bf16),
            pltpu.VMEM((2, 8, 128), f32),
            pltpu.VMEM((2, 8, 128), f32),
            pltpu.VMEM((N, N * N), f32),
            pltpu.VMEM((N, N * N), f32),
            pltpu.VMEM((2048, 128), f32),
            pltpu.VMEM((2, 2048, 256), bf16),
            pltpu.VMEM((2, 256, 2048), bf16),
            pltpu.VMEM((2, N, N * N), bf16),
            pltpu.VMEM((2, N, 128), f32),
            pltpu.VMEM((N, 128), f32),
            pltpu.VMEM((N, 128), f32),
            pltpu.VMEM((N, 128), f32),
            pltpu.VMEM((8, N, sum(CHUNKS)), bf16),
            pltpu.VMEM((8, N, N), bf16),
            pltpu.VMEM((8, N, N), bf16),
            pltpu.VMEM((N, sum(CHUNKS)), f32),
            dma((3,)), dma((3,)), dma((3,)),
            dma((8, 2, 4, 2)), dma((8, 2, 4, 2)),
            dma((4,)), dma((4,)), dma, dma, dma,
            dma((4, 2, 2)), dma((4, 2)), dma((4,)), dma((4,)), dma((2, 2)), dma, dma((4, 2, 2, 2)),
        ],
        compiler_params=pltpu.CompilerParams(
            collective_id=0, has_side_effects=True, vmem_limit_bytes=60 * 1024 * 1024
        ),
    )(ranks, ops, boundaries)


def on_device(boundaries, row_ops, ranks):
    return sweep(ranks.reshape(2), row_ops, boundaries)


def solution(mesh):
    placed = (
        P("sec", None, "col", None, None),
        P(None, "col", None, None, None, None),
        P("sec", None, "col"),
    )
    return jax.shard_map(
        on_device,
        mesh=mesh,
        in_specs=placed,
        out_specs=P("sec", None, "col", None, None),
        check_vma=False,
    )
```

```python
import functools
import math

import jax
import jax.numpy as jnp
from jax import lax
from jax.experimental import pallas as pl
from jax.experimental.pallas import tpu as pltpu
from jax.sharding import PartitionSpec as P

MESH = pl.DeviceIdType.MESH
N = 64
CHUNKS = (1024, 1024, 768, 1024)
OWN = 256
MIDDLE = OWN + CHUNKS[0] + CHUNKS[1]
NT = (((1,), (1,)), ((), ()))
NN = (((1,), (0,)), ((), ()))


def dot(a, b, dims):
    return lax.dot_general(a, b, dims, preferred_element_type=jnp.float32)


def split(x):
    hi = x.astype(jnp.bfloat16)
    lo = (x - hi.astype(jnp.float32)).astype(jnp.bfloat16)
    return hi, lo


WIDE = (8, 128)


def on_lines(x, i):
    return jnp.broadcast_to(x[i : i + 1, :], WIDE)


def on_lanes(x, i):
    return jnp.broadcast_to(x[:, i : i + 1], WIDE)


def factor(g, emit):
    rows = [g[8 * i : 8 * i + 8] for i in range(8)]
    cols = [on_lanes(rows[0], a) for a in range(8)]
    for p in range(8):
        mine, steps, done = rows[p], [], []
        if p < 7:
            beside = [on_lanes(rows[p + 1], 8 * p + a) for a in range(8)]
            ahead = [on_lanes(rows[p + 1], 8 * p + 8 + a) for a in range(8)]
        for a in range(8):
            pivot = on_lines(cols[a], a)
            inverse = 1.0 / pivot
            row = on_lines(mine, a)
            done.append(row[0:1] * lax.rsqrt(pivot[0:1]))
            heads = [on_lines(cols[b], a) if b > a else None for b in range(8)]
            times = cols[a] * inverse
            for b in range(a + 1, 8):
                cols[b] = cols[b] - times * heads[b]
            mine = mine - times * row
            if p < 7:
                times = beside[a] * inverse
                for b in range(a + 1, 8):
                    beside[b] = beside[b] - times * heads[b]
                for b in range(8):
                    ahead[b] = ahead[b] - times * on_lines(beside[a], b)
                rows[p + 1] = rows[p + 1] - times * row
            steps.append((inverse, row, heads))
        for r in range(p + 2, 8):
            below = [on_lanes(rows[r], 8 * p + a) for a in range(8)]
            for a, (inverse, row, heads) in enumerate(steps):
                times = below[a] * inverse
                for b in range(a + 1, 8):
                    below[b] = below[b] - times * heads[b]
                rows[r] = rows[r] - times * row
        emit(p, jnp.concatenate(done, 0))
        if p < 7:
            cols = ahead


def patterns():
    lane = lax.broadcasted_iota(jnp.int32, (N, 128), 1)
    line = lax.broadcasted_iota(jnp.int32, (N, 128), 0)
    low = lane < N
    place = jnp.where(low, lane, lane - N)
    eye = jnp.where(place == line, 1.0, 0.0).astype(jnp.float32)
    return line, low, place, eye


def absorb(lefts, rights, acc, start, width, tiles, first):
    def tile(n, carry):
        at = pl.ds(pl.multiple_of(start + n * width, 128), width)
        total = sum(dot(left, right[:, at], NN) for left, right in zip(lefts, rights))
        acc[:, at] = total if first else acc[:, at] + total
        return carry

    if tiles == 1:
        tile(0, 0)
    else:
        lax.fori_loop(0, tiles, tile, 0)


def flip(raw, ops):
    def one(s, carry):
        ops[s] = raw[s].astype(jnp.float32).T.astype(jnp.bfloat16)
        return carry

    lax.fori_loop(0, 8, one, 0)


def spread(acc, rows, start, stop):
    low = lax.broadcasted_iota(jnp.int32, (32, 128), 1) < N
    for m in range(start // 128, stop // 128):
        v = acc[:, 128 * m : 128 * m + 128]
        w = pltpu.roll(v, N, 1)
        rows[pl.ds(2 * m, 32, stride=N), :] = jnp.where(low, v[0:32], w[32:64])
        rows[pl.ds(2 * m + 1, 32, stride=N), :] = jnp.where(low, w[0:32], v[32:64])


def to_columns(rows, at, q):
    for t in range(16):
        hi, lo = split(rows[128 * t : 128 * t + 128, :].T)
        at[q, 128 * t : 128 * t + 128, 0:128] = hi
        at[q, 128 * t : 128 * t + 128, 128:256] = lo


def advance(left, unit, keep, at, mixed, next_left, inverses, q, begin):
    line, low, place, eye = patterns()
    both = jnp.concatenate([jnp.where(low, left, 0.0), jnp.where(low, 0.0, pltpu.roll(left, N, 1))], 0)
    hi, lo = split(both)
    weights = jnp.concatenate(
        [jnp.concatenate([hi, hi], 1), jnp.concatenate([lo, jnp.zeros_like(lo)], 1)], 0
    )
    for t in range(0, 16, 2):
        o = dot(at[q, 128 * t : 128 * t + 256, :], weights, NT)
        hi, lo = split(o[:, 0:128] + o[:, 128:256])
        for u in range(2):
            lanes = slice(128 * (t + u), 128 * (t + u) + 128)
            mixed[q, 0:128, lanes] = hi[128 * u : 128 * u + 128]
            mixed[q, 128:256, lanes] = lo[128 * u : 128 * u + 128]
    y = mixed[q]
    g = dot(y, y, NT)
    g = g[0:128] + g[128:256]
    g = g[:, 0:128] + g[:, 128:256]
    total = jnp.sum(jnp.where(low, left * left, 0.0), keepdims=True)
    scale = lax.rsqrt(total * (1.0 / (N * N)) + 1e-06)
    scale = jnp.ones_like(scale) if unit else scale
    full = (g[0:N] + pltpu.roll(g[N:], N, 1)) * (scale * scale)

    def emit(p, rows):
        part = slice(8 * p, 8 * p + 8)
        upper = jnp.logical_and(low[part], place[part] >= line[part])
        next_left[part, :] = jnp.where(jnp.logical_and(keep[part], upper), rows, 0.0)
        inverses[q, part, :] = jnp.where(jnp.logical_or(low[part], jnp.logical_not(keep[part])), 0.0, rows) * (scale * float(N))
        if begin is not None:
            begin(p)

    factor(jnp.where(low, full, eye), emit)


def results(inverses, mixed, rows, out, q):
    inverse = inverses[q]
    pair = jnp.concatenate([pltpu.roll(inverse, N, 1), inverse], 0)
    p_hi, p_lo = split(pair)
    wide = jnp.concatenate([p_hi, p_hi], 1)
    for c in range(8):
        y = mixed[q, :, 256 * c : 256 * c + 256]
        o = dot(wide, y, NN) + dot(p_lo, y[0:128], NN)
        rows[256 * c : 256 * c + 128, :] = o[:, 0:128].T
        rows[256 * c + 128 : 256 * c + 256, :] = o[:, 128:256].T
    low = lax.broadcasted_iota(jnp.int32, (32, 128), 1) < N
    for m in range(32):
        e = rows[pl.ds(2 * m, 32, stride=N), :]
        d = rows[pl.ds(2 * m + 1, 32, stride=N), :]
        at = slice(128 * m, 128 * m + 128)
        out[q, 0:32, at] = jnp.where(low, e, pltpu.roll(d, N, 1)).astype(jnp.bfloat16)
        out[q, 32:64, at] = jnp.where(low, pltpu.roll(e, N, 1), d).astype(jnp.bfloat16)


def sweep_kernel(
    ranks_ref, ops_ref, bnd_ref, out_ref,
    blocks, raw, ops, ranks, limits, acc, second, rows, at, mixed, out, inverses, l_in, l_out, left_ref,
    guests, guest_raw, guest_ops, guest_sums, part_send, part_recv, own_sem, ring_send, ring_recv, l_send, l_recv, out_send, out_recv, out_own,
    gift_send, gift_recv, back_send, back_recv, lent_send, lent_recv, hop_send,
):
    me = lax.axis_index("col")
    columns = lax.axis_size("col")
    z = lax.axis_index("sec")
    size = lax.axis_size("sec")
    core = lax.rem(me, 2)
    partner = me + 1 - 2 * core
    up, down = lax.rem(z + 1, size), lax.rem(z + size - 1, size)
    after, before = lax.rem(me + 2, columns), lax.rem(me + columns - 2, columns)
    is_first = me < 2
    band = columns // 4
    row = me // band
    peer = me + band * (3 - 2 * row)

    for b in range(2):
        ranks[b] = jnp.full((8, 128), ranks_ref[b].astype(jnp.float32))
    barrier = pltpu.get_barrier_semaphore()
    peer_partner = peer + 1 - 2 * core
    beside = me + band * (1 - 2 * lax.rem(row, 2))
    beside_partner = beside + 1 - 2 * core
    greeted = (
        (partner, z), (me, up), (me, down), (partner, up), (partner, down), (before, z), (peer, z), (peer_partner, z),
        (beside, z), (beside_partner, z),
    )
    for to in greeted:
        pl.semaphore_signal(barrier, inc=1, device_id=to, device_id_type=MESH)
    pl.semaphore_wait(barrier, len(greeted))

    def to_partner(n, source, target):
        return pltpu.make_async_remote_copy(
            src_ref=source, dst_ref=target, send_sem=part_send.at[n], recv_sem=part_recv.at[n],
            device_id=(partner, z), device_id_type=MESH,
        )

    crossing = [
        to_partner(0, bnd_ref.at[0, 1 - core, 0], blocks.at[core, z]),
        to_partner(1, ops_ref.at[1 - core, 0, :, z], raw.at[core]),
        to_partner(2, ranks.at[1 - core], limits.at[core]),
    ]
    staying = [
        pltpu.make_async_copy(bnd_ref.at[0, core, 0], blocks.at[core, z], own_sem.at[0]),
        pltpu.make_async_copy(ops_ref.at[core, 0, :, z], raw.at[core], own_sem.at[1]),
        pltpu.make_async_copy(ranks.at[core], limits.at[core], own_sem.at[2]),
    ]
    for copy in crossing + staying:
        copy.start()

    edges = {1: (0, OWN), 2: (OWN, MIDDLE), 3: (MIDDLE, N * N)}

    def chunk(c):
        return slice(sum(CHUNKS[:c]), sum(CHUNKS[: c + 1]))

    def far_chunk(c):
        return slice(OWN + sum(CHUNKS[:c]), OWN + sum(CHUNKS[: c + 1]))

    def ring(flow, way, d, half):
        block = lax.rem(z + size + (d - 1 if way else 1 - d), size)
        lines = slice(32 * half, 32 * half + 32)
        if flow == 0:
            part = blocks.at[0, block, lines]
        elif flow < 4:
            part = blocks.at[1, block, lines, edges[flow][0] : edges[flow][1]]
        else:
            part = guests.at[block, lines, chunk(flow - 4)]
        return pltpu.make_async_remote_copy(
            src_ref=part, dst_ref=part, send_sem=ring_send.at[flow, way, d - 1, half],
            recv_sem=ring_recv.at[flow, way, d - 1, half],
            device_id=(me, down if way else up), device_id_type=MESH,
        )

    def first_hop(flow, way, half, b):
        q = 0 if flow == 0 else 1
        lines = slice(32 * half, 32 * half + 32)
        lanes = slice(*edges[flow]) if flow else slice(0, N * N)
        return pltpu.make_async_remote_copy(
            src_ref=bnd_ref.at[0, b, 0, lines, lanes], dst_ref=blocks.at[q, z, lines, lanes],
            send_sem=hop_send.at[flow, way, half, b], recv_sem=ring_recv.at[flow, way, 0, half],
            device_id=(me - core + b, down if way else up), device_id_type=MESH,
        )

    def gift(c, half, b):
        lines = slice(32 * half, 32 * half + 32)
        return pltpu.make_async_remote_copy(
            src_ref=bnd_ref.at[0, b, 0, lines, far_chunk(c)], dst_ref=guests.at[z, lines, chunk(c)],
            send_sem=gift_send.at[c, half, b], recv_sem=gift_recv.at[c, half],
            device_id=((beside if c == 3 else peer) - core + b, z), device_id_type=MESH,
        )

    def lent(b, to_beside):
        return pltpu.make_async_remote_copy(
            src_ref=ops_ref.at[b, 0, :, z], dst_ref=guest_raw, send_sem=lent_send.at[to_beside, b], recv_sem=lent_recv,
            device_id=((beside if to_beside else peer) - core + b, z), device_id_type=MESH,
        )

    def back(c):
        return pltpu.make_async_remote_copy(
            src_ref=guest_sums.at[:, chunk(c)], dst_ref=second.at[:, far_chunk(c)],
            send_sem=back_send.at[c], recv_sem=back_recv.at[c],
            device_id=(beside if c == 3 else peer, z), device_id_type=MESH,
        )

    def parts(d):
        return [(way, d, half) for half in range(2) for way in range(2) if d < 4 or half == way]

    def ready(q):
        @pl.when(core == q)
        def _():
            staying[0].wait()

        @pl.when(core != q)
        def _():
            crossing[0].wait_recv()

    def hops():
        return [(way, half, b) for half in range(2) for way in range(2) for b in range(2)]

    def begin(flow):
        @pl.when(core == (0 if flow == 0 else 1))
        def _():
            for hop in hops():
                first_hop(flow, *hop).start()

    def turn(flow, d):
        for way, _, half in parts(d):
            ring(flow, way, d, half).wait_recv()
            if d < 4 and (way, d + 1, half) in parts(d + 1):
                ring(flow, way, d + 1, half).start()

    def sectors(d):
        before, after = lax.rem(z + size - d, size), lax.rem(z + d, size)
        return [z] if d == 0 else [after] if d == 4 else [before, after]

    def absorb_flow(flow, d):
        q = 0 if flow == 0 else 1
        start, width, tiles = {0: (0, 512, 8), 1: (0, 256, 1), 2: (OWN, 256, 8), 3: (MIDDLE, 256, 7)}[flow]
        absorb(
            [ops[q, s] for s in sectors(d)], [blocks.at[q, s] for s in sectors(d)],
            second if q else acc, start, width, tiles, d == 0,
        )

    def open_guest(c):
        for half in range(2):
            gift(c, half, 0).wait_recv()
            for way in range(2):
                ring(4 + c, way, 1, half).start()

    def borrow():
        lent(0, 0).wait_recv()
        flip(guest_raw, guest_ops)

    def give_back(c):
        lefts = [guest_ops[s] for s in range(8)]
        rights = [guests.at[s] for s in range(8)]
        wide, rest = CHUNKS[c] // 256, CHUNKS[c] % 256
        absorb(lefts, rights, guest_sums, chunk(c).start, 256, wide, True)
        if rest:
            absorb(lefts, rights, guest_sums, chunk(c).stop - rest, rest, 1, True)
        back(c).start()

    def serve(count, at_end):
        open_guest(0)
        open_guest(1)
        for slot in range(1, 2 * count + 3):
            for c in range(count):
                d = slot - 2 * c
                if not 1 <= d <= 4:
                    continue
                turn(4 + c, d)
                if d == 3 and c + 2 < count:
                    open_guest(c + 2)
                if d == 3 and c == count - 1:
                    at_end()
                if d == 4:
                    if c == 0:
                        borrow()
                    give_back(c)

    def begin_own():
        begin(0)
        begin(1)

    @pl.when(jnp.logical_and(row < 2, core == 1))
    def _():
        for c in range(2):
            for half in range(2):
                for b in range(2):
                    gift(c, half, b).start()

    @pl.when(row < 3)
    def _():
        begin_own()

    @pl.when(jnp.logical_and(row == 0, core == 1))
    def _():
        for c in (3, 2):
            for half in range(2):
                for b in range(2):
                    gift(c, half, b).start()
        for b in range(2):
            lent(b, 1).start()

    @pl.when(jnp.logical_and(row < 2, core == 1))
    def _():
        for b in range(2):
            lent(b, 0).start()

    @pl.when(row == 1)
    def _():
        open_guest(3)

    @pl.when(row == 2)
    def _():
        open_guest(0)
        open_guest(1)

    @pl.when(row == 3)
    def _():
        serve(3, begin_own)

    ready(0)
    ready(1)
    for copy in staying[1:]:
        copy.wait()
    for copy in crossing[1:]:
        copy.wait_recv()
    for q in range(2):
        flip(raw.at[q], ops.at[q])

    for d in range(5):
        if d > 0:

            def guests_turn(step):
                @pl.when(row == 1)
                def _():
                    turn(7, step)

                @pl.when(row == 2)
                def _():
                    turn(4, step)
                    turn(5, step)

            if d < 3:
                guests_turn(2 * d - 1)
            turn(0, d)
            turn(1, d)
            if d < 3:
                guests_turn(2 * d)
            if d == 2:

                @pl.when(row == 1)
                def _():
                    borrow()
                    give_back(3)

                @pl.when(row == 2)
                def _():
                    borrow()
                    give_back(0)
                    give_back(1)

        if d == 3:

            @pl.when(row >= 2)
            def _():
                begin(2)

            @pl.when(row >= 1)
            def _():
                begin(3)

        absorb_flow(0, d)
        absorb_flow(1, d)
    spread(acc, rows, 0, N * N)
    to_columns(rows, at, 0)
    for d in range(5):

        @pl.when(row >= 2)
        def _():
            if d > 0:
                turn(2, d)
            absorb_flow(2, d)

        @pl.when(row >= 1)
        def _():
            if d > 0:
                turn(3, d)
            absorb_flow(3, d)

    line, low, place, eye = patterns()

    def along(part, start, size):
        return pltpu.make_async_remote_copy(
            src_ref=l_out.at[start : start + size], dst_ref=l_in.at[start : start + size],
            send_sem=l_send.at[part], recv_sem=l_recv.at[part], device_id=(after, z), device_id_type=MESH,
        )

    pieces = {3: along(0, 0, 32), 5: along(1, 32, 16), 6: along(2, 48, 8), 7: along(3, 56, 8)}

    def keep(q):
        return line.astype(jnp.float32) < limits[q, 0:1, :]

    def begin_piece(p):
        if p in pieces:
            pieces[p].start()

    @pl.when(is_first)
    def _():
        advance(eye, True, keep(0), at, mixed, left_ref, inverses, 0, None)

    @pl.when(row < 2)
    def _():
        for c in range(2):
            back(c).wait_recv()

    spread(second, rows, 0, MIDDLE)

    @pl.when(row == 0)
    def _():
        for c in range(2, 4):
            back(c).wait_recv()

    spread(second, rows, MIDDLE, N * N)
    to_columns(rows, at, 1)

    @pl.when(jnp.logical_not(is_first))
    def _():
        for piece in pieces.values():
            piece.wait_recv()
        advance(l_in[...], False, keep(0), at, mixed, left_ref, inverses, 0, None)

    advance(left_ref[...], False, keep(1), at, mixed, l_out, inverses, 1, begin_piece)

    across = pltpu.make_async_remote_copy(
        src_ref=out.at[1 - core], dst_ref=out_ref.at[0, core, 0], send_sem=out_send, recv_sem=out_recv,
        device_id=(partner, z), device_id_type=MESH,
    )
    home = pltpu.make_async_copy(out.at[core], out_ref.at[0, core, 0], out_own)

    for q in range(2):
        results(inverses, mixed, rows, out, q)

        @pl.when(core == q)
        def _():
            home.start()

        @pl.when(core != q)
        def _():
            across.start()

    home.wait()
    across.wait()

    for piece in pieces.values():
        piece.wait_send()

    @pl.when(is_first)
    def _():
        for piece in pieces.values():
            piece.wait_recv()

    for copy in crossing:
        copy.wait_send()
    late = [part for d in range(2, 5) for part in parts(d)]

    def sent(*flows):
        for flow in flows:
            for part in late + (parts(1) if flow > 3 else []):
                ring(flow, *part).wait_send()
            if flow < 4:

                @pl.when(core == (0 if flow == 0 else 1))
                def _():
                    for hop in hops():
                        first_hop(flow, *hop).wait_send()

    sent(0, 1)

    @pl.when(row >= 2)
    def _():
        sent(2, 4, 5)
        for c in range(2):
            back(c).wait_send()

    @pl.when(row >= 1)
    def _():
        sent(3)

    @pl.when(row == 3)
    def _():
        sent(6)
        back(2).wait_send()

    @pl.when(row == 1)
    def _():
        sent(7)
        back(3).wait_send()

    @pl.when(jnp.logical_and(row < 2, core == 1))
    def _():
        for b in range(2):
            lent(b, 0).wait_send()
            for c in range(2):
                for half in range(2):
                    gift(c, half, b).wait_send()

    @pl.when(jnp.logical_and(row == 0, core == 1))
    def _():
        for b in range(2):
            lent(b, 1).wait_send()
            for c in range(2, 4):
                for half in range(2):
                    gift(c, half, b).wait_send()


def sweep(ranks, ops, boundaries):
    anywhere = pl.BlockSpec(memory_space=pltpu.HBM)
    bf16, f32 = jnp.bfloat16, jnp.float32
    dma = pltpu.SemaphoreType.DMA
    return pl.pallas_call(
        sweep_kernel,
        out_shape=jax.ShapeDtypeStruct(boundaries.shape, bf16),
        in_specs=[pl.BlockSpec(memory_space=pltpu.SMEM), anywhere, anywhere],
        out_specs=anywhere,
        scratch_shapes=[
            pltpu.VMEM((2, 8, N, N * N), bf16),
            pltpu.VMEM((2, 8, N, N), bf16),
            pltpu.VMEM((2, 8, N, N), bf16),
            pltpu.VMEM((2, 8, 128), f32),
            pltpu.VMEM((2, 8, 128), f32),
            pltpu.VMEM((N, N * N), f32),
            pltpu.VMEM((N, N * N), f32),
            pltpu.VMEM((2048, 128), f32),
            pltpu.VMEM((2, 2048, 256), bf16),
            pltpu.VMEM((2, 256, 2048), bf16),
            pltpu.VMEM((2, N, N * N), bf16),
            pltpu.VMEM((2, N, 128), f32),
            pltpu.VMEM((N, 128), f32),
            pltpu.VMEM((N, 128), f32),
            pltpu.VMEM((N, 128), f32),
            pltpu.VMEM((8, N, sum(CHUNKS)), bf16),
            pltpu.VMEM((8, N, N), bf16),
            pltpu.VMEM((8, N, N), bf16),
            pltpu.VMEM((N, sum(CHUNKS)), f32),
            dma((3,)), dma((3,)), dma((3,)),
            dma((8, 2, 4, 2)), dma((8, 2, 4, 2)),
            dma((4,)), dma((4,)), dma, dma, dma,
            dma((4, 2, 2)), dma((4, 2)), dma((4,)), dma((4,)), dma((2, 2)), dma, dma((4, 2, 2, 2)),
        ],
        compiler_params=pltpu.CompilerParams(
            collective_id=0, has_side_effects=True, vmem_limit_bytes=60 * 1024 * 1024
        ),
    )(ranks, ops, boundaries)


def on_device(boundaries, row_ops, ranks):
    return sweep(ranks.reshape(2), row_ops, boundaries)


def solution(mesh):
    placed = (
        P("sec", None, "col", None, None),
        P(None, "col", None, None, None, None),
        P("sec", None, "col"),
    )
    return jax.shard_map(
        on_device,
        mesh=mesh,
        in_specs=placed,
        out_specs=P("sec", None, "col", None, None),
        check_vma=False,
    )
```

```python
import functools
import math

import jax
import jax.numpy as jnp
from jax import lax
from jax.experimental import pallas as pl
from jax.experimental.pallas import tpu as pltpu
from jax.sharding import PartitionSpec as P

MESH = pl.DeviceIdType.MESH
N = 64
CHUNKS = (1152, 1152, 512, 1024)
OWN = 256
MIDDLE = OWN + CHUNKS[0] + CHUNKS[1]
NT = (((1,), (1,)), ((), ()))
NN = (((1,), (0,)), ((), ()))


def dot(a, b, dims):
    return lax.dot_general(a, b, dims, preferred_element_type=jnp.float32)


def split(x):
    hi = x.astype(jnp.bfloat16)
    lo = (x - hi.astype(jnp.float32)).astype(jnp.bfloat16)
    return hi, lo


WIDE = (8, 128)


def on_lines(x, i):
    return jnp.broadcast_to(x[i : i + 1, :], WIDE)


def on_lanes(x, i):
    return jnp.broadcast_to(x[:, i : i + 1], WIDE)


def factor(g, emit):
    rows = [g[8 * i : 8 * i + 8] for i in range(8)]
    cols = [on_lanes(rows[0], a) for a in range(8)]
    for p in range(8):
        mine, steps, done = rows[p], [], []
        if p < 7:
            beside = [on_lanes(rows[p + 1], 8 * p + a) for a in range(8)]
            ahead = [on_lanes(rows[p + 1], 8 * p + 8 + a) for a in range(8)]
        for a in range(8):
            pivot = on_lines(cols[a], a)
            inverse = 1.0 / pivot
            row = on_lines(mine, a)
            done.append(row[0:1] * lax.rsqrt(pivot[0:1]))
            heads = [on_lines(cols[b], a) if b > a else None for b in range(8)]
            times = cols[a] * inverse
            for b in range(a + 1, 8):
                cols[b] = cols[b] - times * heads[b]
            mine = mine - times * row
            if p < 7:
                times = beside[a] * inverse
                for b in range(a + 1, 8):
                    beside[b] = beside[b] - times * heads[b]
                for b in range(8):
                    ahead[b] = ahead[b] - times * on_lines(beside[a], b)
                rows[p + 1] = rows[p + 1] - times * row
            steps.append((inverse, row, heads))
        for r in range(p + 2, 8):
            below = [on_lanes(rows[r], 8 * p + a) for a in range(8)]
            for a, (inverse, row, heads) in enumerate(steps):
                times = below[a] * inverse
                for b in range(a + 1, 8):
                    below[b] = below[b] - times * heads[b]
                rows[r] = rows[r] - times * row
        emit(p, jnp.concatenate(done, 0))
        if p < 7:
            cols = ahead


def patterns():
    lane = lax.broadcasted_iota(jnp.int32, (N, 128), 1)
    line = lax.broadcasted_iota(jnp.int32, (N, 128), 0)
    low = lane < N
    place = jnp.where(low, lane, lane - N)
    eye = jnp.where(place == line, 1.0, 0.0).astype(jnp.float32)
    return line, low, place, eye


def absorb(lefts, rights, acc, start, width, tiles, first):
    def tile(n, carry):
        at = pl.ds(pl.multiple_of(start + n * width, 128), width)
        total = sum(dot(left, right[:, at], NN) for left, right in zip(lefts, rights))
        acc[:, at] = total if first else acc[:, at] + total
        return carry

    if tiles == 1:
        tile(0, 0)
    else:
        lax.fori_loop(0, tiles, tile, 0)


def flip(raw, ops):
    def one(s, carry):
        ops[s] = raw[s].astype(jnp.float32).T.astype(jnp.bfloat16)
        return carry

    lax.fori_loop(0, 8, one, 0)


def spread(acc, rows, start, stop):
    low = lax.broadcasted_iota(jnp.int32, (32, 128), 1) < N
    for m in range(start // 128, stop // 128):
        v = acc[:, 128 * m : 128 * m + 128]
        w = pltpu.roll(v, N, 1)
        rows[pl.ds(2 * m, 32, stride=N), :] = jnp.where(low, v[0:32], w[32:64])
        rows[pl.ds(2 * m + 1, 32, stride=N), :] = jnp.where(low, w[0:32], v[32:64])


def to_columns(rows, at, q):
    for t in range(16):
        hi, lo = split(rows[128 * t : 128 * t + 128, :].T)
        at[q, 128 * t : 128 * t + 128, 0:128] = hi
        at[q, 128 * t : 128 * t + 128, 128:256] = lo


def advance(left, unit, keep, at, mixed, next_left, inverses, q, begin):
    line, low, place, eye = patterns()
    both = jnp.concatenate([jnp.where(low, left, 0.0), jnp.where(low, 0.0, pltpu.roll(left, N, 1))], 0)
    hi, lo = split(both)
    weights = jnp.concatenate(
        [jnp.concatenate([hi, hi], 1), jnp.concatenate([lo, jnp.zeros_like(lo)], 1)], 0
    )
    for t in range(0, 16, 2):
        o = dot(at[q, 128 * t : 128 * t + 256, :], weights, NT)
        hi, lo = split(o[:, 0:128] + o[:, 128:256])
        for u in range(2):
            lanes = slice(128 * (t + u), 128 * (t + u) + 128)
            mixed[q, 0:128, lanes] = hi[128 * u : 128 * u + 128]
            mixed[q, 128:256, lanes] = lo[128 * u : 128 * u + 128]
    y = mixed[q]
    g = dot(y, y, NT)
    g = g[0:128] + g[128:256]
    g = g[:, 0:128] + g[:, 128:256]
    total = jnp.sum(jnp.where(low, left * left, 0.0), keepdims=True)
    scale = lax.rsqrt(total * (1.0 / (N * N)) + 1e-06)
    scale = jnp.ones_like(scale) if unit else scale
    full = (g[0:N] + pltpu.roll(g[N:], N, 1)) * (scale * scale)

    def emit(p, rows):
        part = slice(8 * p, 8 * p + 8)
        upper = jnp.logical_and(low[part], place[part] >= line[part])
        next_left[part, :] = jnp.where(jnp.logical_and(keep[part], upper), rows, 0.0)
        inverses[q, part, :] = jnp.where(jnp.logical_or(low[part], jnp.logical_not(keep[part])), 0.0, rows) * (scale * float(N))
        if begin is not None:
            begin(p)

    factor(jnp.where(low, full, eye), emit)


def results(inverses, mixed, rows, out, q):
    inverse = inverses[q]
    pair = jnp.concatenate([pltpu.roll(inverse, N, 1), inverse], 0)
    p_hi, p_lo = split(pair)
    wide = jnp.concatenate([p_hi, p_hi], 1)
    for c in range(8):
        y = mixed[q, :, 256 * c : 256 * c + 256]
        o = dot(wide, y, NN) + dot(p_lo, y[0:128], NN)
        rows[256 * c : 256 * c + 128, :] = o[:, 0:128].T
        rows[256 * c + 128 : 256 * c + 256, :] = o[:, 128:256].T
    low = lax.broadcasted_iota(jnp.int32, (32, 128), 1) < N
    for m in range(32):
        e = rows[pl.ds(2 * m, 32, stride=N), :]
        d = rows[pl.ds(2 * m + 1, 32, stride=N), :]
        at = slice(128 * m, 128 * m + 128)
        out[q, 0:32, at] = jnp.where(low, e, pltpu.roll(d, N, 1)).astype(jnp.bfloat16)
        out[q, 32:64, at] = jnp.where(low, pltpu.roll(e, N, 1), d).astype(jnp.bfloat16)


def sweep_kernel(
    ranks_ref, ops_ref, bnd_ref, out_ref,
    blocks, raw, ops, ranks, limits, acc, second, rows, at, mixed, out, inverses, l_in, l_out, left_ref,
    guests, guest_raw, guest_ops, guest_sums, part_send, part_recv, own_sem, ring_send, ring_recv, l_send, l_recv, out_send, out_recv, out_own,
    gift_send, gift_recv, back_send, back_recv, lent_send, lent_recv, hop_send,
):
    me = lax.axis_index("col")
    columns = lax.axis_size("col")
    z = lax.axis_index("sec")
    size = lax.axis_size("sec")
    core = lax.rem(me, 2)
    partner = me + 1 - 2 * core
    up, down = lax.rem(z + 1, size), lax.rem(z + size - 1, size)
    after, before = lax.rem(me + 2, columns), lax.rem(me + columns - 2, columns)
    is_first = me < 2
    band = columns // 4
    row = me // band
    peer = me + band * (3 - 2 * row)

    for b in range(2):
        ranks[b] = jnp.full((8, 128), ranks_ref[b].astype(jnp.float32))
    barrier = pltpu.get_barrier_semaphore()
    peer_partner = peer + 1 - 2 * core
    beside = me + band * (1 - 2 * lax.rem(row, 2))
    beside_partner = beside + 1 - 2 * core
    greeted = (
        (partner, z), (me, up), (me, down), (partner, up), (partner, down), (before, z), (peer, z), (peer_partner, z),
        (beside, z), (beside_partner, z),
    )
    for to in greeted:
        pl.semaphore_signal(barrier, inc=1, device_id=to, device_id_type=MESH)
    pl.semaphore_wait(barrier, len(greeted))

    def to_partner(n, source, target):
        return pltpu.make_async_remote_copy(
            src_ref=source, dst_ref=target, send_sem=part_send.at[n], recv_sem=part_recv.at[n],
            device_id=(partner, z), device_id_type=MESH,
        )

    crossing = [
        to_partner(0, bnd_ref.at[0, 1 - core, 0], blocks.at[core, z]),
        to_partner(1, ops_ref.at[1 - core, 0, :, z], raw.at[core]),
        to_partner(2, ranks.at[1 - core], limits.at[core]),
    ]
    staying = [
        pltpu.make_async_copy(bnd_ref.at[0, core, 0], blocks.at[core, z], own_sem.at[0]),
        pltpu.make_async_copy(ops_ref.at[core, 0, :, z], raw.at[core], own_sem.at[1]),
        pltpu.make_async_copy(ranks.at[core], limits.at[core], own_sem.at[2]),
    ]
    for copy in crossing + staying:
        copy.start()

    edges = {1: (0, OWN), 2: (OWN, MIDDLE), 3: (MIDDLE, N * N)}

    def chunk(c):
        return slice(sum(CHUNKS[:c]), sum(CHUNKS[: c + 1]))

    def far_chunk(c):
        return slice(OWN + sum(CHUNKS[:c]), OWN + sum(CHUNKS[: c + 1]))

    def ring(flow, way, d, half):
        block = lax.rem(z + size + (d - 1 if way else 1 - d), size)
        lines = slice(32 * half, 32 * half + 32)
        if flow == 0:
            part = blocks.at[0, block, lines]
        elif flow < 4:
            part = blocks.at[1, block, lines, edges[flow][0] : edges[flow][1]]
        else:
            part = guests.at[block, lines, chunk(flow - 4)]
        return pltpu.make_async_remote_copy(
            src_ref=part, dst_ref=part, send_sem=ring_send.at[flow, way, d - 1, half],
            recv_sem=ring_recv.at[flow, way, d - 1, half],
            device_id=(me, down if way else up), device_id_type=MESH,
        )

    def first_hop(flow, way, half, b):
        q = 0 if flow == 0 else 1
        lines = slice(32 * half, 32 * half + 32)
        lanes = slice(*edges[flow]) if flow else slice(0, N * N)
        return pltpu.make_async_remote_copy(
            src_ref=bnd_ref.at[0, b, 0, lines, lanes], dst_ref=blocks.at[q, z, lines, lanes],
            send_sem=hop_send.at[flow, way, half, b], recv_sem=ring_recv.at[flow, way, 0, half],
            device_id=(me - core + b, down if way else up), device_id_type=MESH,
        )

    def gift(c, half, b):
        lines = slice(32 * half, 32 * half + 32)
        return pltpu.make_async_remote_copy(
            src_ref=bnd_ref.at[0, b, 0, lines, far_chunk(c)], dst_ref=guests.at[z, lines, chunk(c)],
            send_sem=gift_send.at[c, half, b], recv_sem=gift_recv.at[c, half],
            device_id=((beside if c == 3 else peer) - core + b, z), device_id_type=MESH,
        )

    def lent(b, to_beside):
        return pltpu.make_async_remote_copy(
            src_ref=ops_ref.at[b, 0, :, z], dst_ref=guest_raw, send_sem=lent_send.at[to_beside, b], recv_sem=lent_recv,
            device_id=((beside if to_beside else peer) - core + b, z), device_id_type=MESH,
        )

    def back(c):
        return pltpu.make_async_remote_copy(
            src_ref=guest_sums.at[:, chunk(c)], dst_ref=second.at[:, far_chunk(c)],
            send_sem=back_send.at[c], recv_sem=back_recv.at[c],
            device_id=(beside if c == 3 else peer, z), device_id_type=MESH,
        )

    def parts(d):
        return [(way, d, half) for half in range(2) for way in range(2) if d < 4 or half == way]

    def ready(q):
        @pl.when(core == q)
        def _():
            staying[0].wait()

        @pl.when(core != q)
        def _():
            crossing[0].wait_recv()

    def hops():
        return [(way, half, b) for half in range(2) for way in range(2) for b in range(2)]

    def begin(flow):
        @pl.when(core == (0 if flow == 0 else 1))
        def _():
            for hop in hops():
                first_hop(flow, *hop).start()

    def turn(flow, d):
        for way, _, half in parts(d):
            ring(flow, way, d, half).wait_recv()
            if d < 4 and (way, d + 1, half) in parts(d + 1):
                ring(flow, way, d + 1, half).start()

    def sectors(d):
        before, after = lax.rem(z + size - d, size), lax.rem(z + d, size)
        return [z] if d == 0 else [after] if d == 4 else [before, after]

    def absorb_flow(flow, d):
        q = 0 if flow == 0 else 1
        start, width, tiles = {0: (0, 512, 8), 1: (0, 256, 1), 2: (OWN, 256, 9), 3: (MIDDLE, 256, 6)}[flow]
        absorb(
            [ops[q, s] for s in sectors(d)], [blocks.at[q, s] for s in sectors(d)],
            second if q else acc, start, width, tiles, d == 0,
        )

    def open_guest(c):
        for half in range(2):
            gift(c, half, 0).wait_recv()
            for way in range(2):
                ring(4 + c, way, 1, half).start()

    def borrow():
        lent(0, 0).wait_recv()
        flip(guest_raw, guest_ops)

    def give_back(c):
        lefts = [guest_ops[s] for s in range(8)]
        rights = [guests.at[s] for s in range(8)]
        wide, rest = CHUNKS[c] // 256, CHUNKS[c] % 256
        absorb(lefts, rights, guest_sums, chunk(c).start, 256, wide, True)
        if rest:
            absorb(lefts, rights, guest_sums, chunk(c).stop - rest, rest, 1, True)
        back(c).start()

    def serve(count, at_end):
        open_guest(0)
        open_guest(1)
        for slot in range(1, 2 * count + 3):
            for c in range(count):
                d = slot - 2 * c
                if not 1 <= d <= 4:
                    continue
                turn(4 + c, d)
                if d == 3 and c + 2 < count:
                    open_guest(c + 2)
                if d == 3 and c == count - 1:
                    at_end()
                if d == 4:
                    if c == 0:
                        borrow()
                    give_back(c)

    def begin_own():
        begin(0)
        begin(1)

    @pl.when(jnp.logical_and(row < 2, core == 1))
    def _():
        for c in range(2):
            for half in range(2):
                for b in range(2):
                    gift(c, half, b).start()

    @pl.when(row < 3)
    def _():
        begin_own()

    @pl.when(jnp.logical_and(row == 0, core == 1))
    def _():
        for c in (3, 2):
            for half in range(2):
                for b in range(2):
                    gift(c, half, b).start()
        for b in range(2):
            lent(b, 1).start()

    @pl.when(jnp.logical_and(row < 2, core == 1))
    def _():
        for b in range(2):
            lent(b, 0).start()

    @pl.when(row == 1)
    def _():
        open_guest(3)

    @pl.when(row == 2)
    def _():
        open_guest(0)
        open_guest(1)

    @pl.when(row == 3)
    def _():
        serve(3, begin_own)

    ready(0)
    ready(1)
    for copy in staying[1:]:
        copy.wait()
    for copy in crossing[1:]:
        copy.wait_recv()
    for q in range(2):
        flip(raw.at[q], ops.at[q])

    for d in range(5):
        if d > 0:

            def guests_turn(step):
                @pl.when(row == 1)
                def _():
                    turn(7, step)

                @pl.when(row == 2)
                def _():
                    turn(4, step)
                    turn(5, step)

            if d < 3:
                guests_turn(2 * d - 1)
            turn(0, d)
            turn(1, d)
            if d < 3:
                guests_turn(2 * d)
            if d == 2:

                @pl.when(row == 1)
                def _():
                    borrow()
                    give_back(3)

                @pl.when(row == 2)
                def _():
                    borrow()
                    give_back(0)
                    give_back(1)

        if d == 3:

            @pl.when(row >= 2)
            def _():
                begin(2)

            @pl.when(row >= 1)
            def _():
                begin(3)

        absorb_flow(0, d)
        absorb_flow(1, d)
    spread(acc, rows, 0, N * N)
    to_columns(rows, at, 0)
    for d in range(5):

        @pl.when(row >= 2)
        def _():
            if d > 0:
                turn(2, d)
            absorb_flow(2, d)

        @pl.when(row >= 1)
        def _():
            if d > 0:
                turn(3, d)
            absorb_flow(3, d)

    line, low, place, eye = patterns()

    def along(part, start, size):
        return pltpu.make_async_remote_copy(
            src_ref=l_out.at[start : start + size], dst_ref=l_in.at[start : start + size],
            send_sem=l_send.at[part], recv_sem=l_recv.at[part], device_id=(after, z), device_id_type=MESH,
        )

    pieces = {3: along(0, 0, 32), 5: along(1, 32, 16), 6: along(2, 48, 8), 7: along(3, 56, 8)}

    def keep(q):
        return line.astype(jnp.float32) < limits[q, 0:1, :]

    def begin_piece(p):
        if p in pieces:
            pieces[p].start()

    @pl.when(is_first)
    def _():
        advance(eye, True, keep(0), at, mixed, left_ref, inverses, 0, None)

    @pl.when(row < 2)
    def _():
        for c in range(2):
            back(c).wait_recv()

    spread(second, rows, 0, MIDDLE)

    @pl.when(row == 0)
    def _():
        for c in range(2, 4):
            back(c).wait_recv()

    spread(second, rows, MIDDLE, N * N)
    to_columns(rows, at, 1)

    @pl.when(jnp.logical_not(is_first))
    def _():
        for piece in pieces.values():
            piece.wait_recv()
        advance(l_in[...], False, keep(0), at, mixed, left_ref, inverses, 0, None)

    advance(left_ref[...], False, keep(1), at, mixed, l_out, inverses, 1, begin_piece)

    across = pltpu.make_async_remote_copy(
        src_ref=out.at[1 - core], dst_ref=out_ref.at[0, core, 0], send_sem=out_send, recv_sem=out_recv,
        device_id=(partner, z), device_id_type=MESH,
    )
    home = pltpu.make_async_copy(out.at[core], out_ref.at[0, core, 0], out_own)

    for q in range(2):
        results(inverses, mixed, rows, out, q)

        @pl.when(core == q)
        def _():
            home.start()

        @pl.when(core != q)
        def _():
            across.start()

    home.wait()
    across.wait()

    for piece in pieces.values():
        piece.wait_send()

    @pl.when(is_first)
    def _():
        for piece in pieces.values():
            piece.wait_recv()

    for copy in crossing:
        copy.wait_send()
    late = [part for d in range(2, 5) for part in parts(d)]

    def sent(*flows):
        for flow in flows:
            for part in late + (parts(1) if flow > 3 else []):
                ring(flow, *part).wait_send()
            if flow < 4:

                @pl.when(core == (0 if flow == 0 else 1))
                def _():
                    for hop in hops():
                        first_hop(flow, *hop).wait_send()

    sent(0, 1)

    @pl.when(row >= 2)
    def _():
        sent(2, 4, 5)
        for c in range(2):
            back(c).wait_send()

    @pl.when(row >= 1)
    def _():
        sent(3)

    @pl.when(row == 3)
    def _():
        sent(6)
        back(2).wait_send()

    @pl.when(row == 1)
    def _():
        sent(7)
        back(3).wait_send()

    @pl.when(jnp.logical_and(row < 2, core == 1))
    def _():
        for b in range(2):
            lent(b, 0).wait_send()
            for c in range(2):
                for half in range(2):
                    gift(c, half, b).wait_send()

    @pl.when(jnp.logical_and(row == 0, core == 1))
    def _():
        for b in range(2):
            lent(b, 1).wait_send()
            for c in range(2, 4):
                for half in range(2):
                    gift(c, half, b).wait_send()


def sweep(ranks, ops, boundaries):
    anywhere = pl.BlockSpec(memory_space=pltpu.HBM)
    bf16, f32 = jnp.bfloat16, jnp.float32
    dma = pltpu.SemaphoreType.DMA
    return pl.pallas_call(
        sweep_kernel,
        out_shape=jax.ShapeDtypeStruct(boundaries.shape, bf16),
        in_specs=[pl.BlockSpec(memory_space=pltpu.SMEM), anywhere, anywhere],
        out_specs=anywhere,
        scratch_shapes=[
            pltpu.VMEM((2, 8, N, N * N), bf16),
            pltpu.VMEM((2, 8, N, N), bf16),
            pltpu.VMEM((2, 8, N, N), bf16),
            pltpu.VMEM((2, 8, 128), f32),
            pltpu.VMEM((2, 8, 128), f32),
            pltpu.VMEM((N, N * N), f32),
            pltpu.VMEM((N, N * N), f32),
            pltpu.VMEM((2048, 128), f32),
            pltpu.VMEM((2, 2048, 256), bf16),
            pltpu.VMEM((2, 256, 2048), bf16),
            pltpu.VMEM((2, N, N * N), bf16),
            pltpu.VMEM((2, N, 128), f32),
            pltpu.VMEM((N, 128), f32),
            pltpu.VMEM((N, 128), f32),
            pltpu.VMEM((N, 128), f32),
            pltpu.VMEM((8, N, sum(CHUNKS)), bf16),
            pltpu.VMEM((8, N, N), bf16),
            pltpu.VMEM((8, N, N), bf16),
            pltpu.VMEM((N, sum(CHUNKS)), f32),
            dma((3,)), dma((3,)), dma((3,)),
            dma((8, 2, 4, 2)), dma((8, 2, 4, 2)),
            dma((4,)), dma((4,)), dma, dma, dma,
            dma((4, 2, 2)), dma((4, 2)), dma((4,)), dma((4,)), dma((2, 2)), dma, dma((4, 2, 2, 2)),
        ],
        compiler_params=pltpu.CompilerParams(
            collective_id=0, has_side_effects=True, vmem_limit_bytes=60 * 1024 * 1024
        ),
    )(ranks, ops, boundaries)


def on_device(boundaries, row_ops, ranks):
    return sweep(ranks.reshape(2), row_ops, boundaries)


def solution(mesh):
    placed = (
        P("sec", None, "col", None, None),
        P(None, "col", None, None, None, None),
        P("sec", None, "col"),
    )
    return jax.shard_map(
        on_device,
        mesh=mesh,
        in_specs=placed,
        out_specs=P("sec", None, "col", None, None),
        check_vma=False,
    )
```

```python
import functools
import math

import jax
import jax.numpy as jnp
from jax import lax
from jax.experimental import pallas as pl
from jax.experimental.pallas import tpu as pltpu
from jax.sharding import PartitionSpec as P

MESH = pl.DeviceIdType.MESH
N = 64
CHUNKS = (1280, 1280, 256, 1024)
OWN = 256
MIDDLE = OWN + CHUNKS[0] + CHUNKS[1]
NT = (((1,), (1,)), ((), ()))
NN = (((1,), (0,)), ((), ()))


def dot(a, b, dims):
    return lax.dot_general(a, b, dims, preferred_element_type=jnp.float32)


def split(x):
    hi = x.astype(jnp.bfloat16)
    lo = (x - hi.astype(jnp.float32)).astype(jnp.bfloat16)
    return hi, lo


WIDE = (8, 128)


def on_lines(x, i):
    return jnp.broadcast_to(x[i : i + 1, :], WIDE)


def on_lanes(x, i):
    return jnp.broadcast_to(x[:, i : i + 1], WIDE)


def factor(g, emit):
    rows = [g[8 * i : 8 * i + 8] for i in range(8)]
    cols = [on_lanes(rows[0], a) for a in range(8)]
    for p in range(8):
        mine, steps, done = rows[p], [], []
        if p < 7:
            beside = [on_lanes(rows[p + 1], 8 * p + a) for a in range(8)]
            ahead = [on_lanes(rows[p + 1], 8 * p + 8 + a) for a in range(8)]
        for a in range(8):
            pivot = on_lines(cols[a], a)
            inverse = 1.0 / pivot
            row = on_lines(mine, a)
            done.append(row[0:1] * lax.rsqrt(pivot[0:1]))
            heads = [on_lines(cols[b], a) if b > a else None for b in range(8)]
            times = cols[a] * inverse
            for b in range(a + 1, 8):
                cols[b] = cols[b] - times * heads[b]
            mine = mine - times * row
            if p < 7:
                times = beside[a] * inverse
                for b in range(a + 1, 8):
                    beside[b] = beside[b] - times * heads[b]
                for b in range(8):
                    ahead[b] = ahead[b] - times * on_lines(beside[a], b)
                rows[p + 1] = rows[p + 1] - times * row
            steps.append((inverse, row, heads))
        for r in range(p + 2, 8):
            below = [on_lanes(rows[r], 8 * p + a) for a in range(8)]
            for a, (inverse, row, heads) in enumerate(steps):
                times = below[a] * inverse
                for b in range(a + 1, 8):
                    below[b] = below[b] - times * heads[b]
                rows[r] = rows[r] - times * row
        emit(p, jnp.concatenate(done, 0))
        if p < 7:
            cols = ahead


def patterns():
    lane = lax.broadcasted_iota(jnp.int32, (N, 128), 1)
    line = lax.broadcasted_iota(jnp.int32, (N, 128), 0)
    low = lane < N
    place = jnp.where(low, lane, lane - N)
    eye = jnp.where(place == line, 1.0, 0.0).astype(jnp.float32)
    return line, low, place, eye


def absorb(lefts, rights, acc, start, width, tiles, first):
    def tile(n, carry):
        at = pl.ds(pl.multiple_of(start + n * width, 128), width)
        total = sum(dot(left, right[:, at], NN) for left, right in zip(lefts, rights))
        acc[:, at] = total if first else acc[:, at] + total
        return carry

    if tiles == 1:
        tile(0, 0)
    else:
        lax.fori_loop(0, tiles, tile, 0)


def flip(raw, ops):
    def one(s, carry):
        ops[s] = raw[s].astype(jnp.float32).T.astype(jnp.bfloat16)
        return carry

    lax.fori_loop(0, 8, one, 0)


def spread(acc, rows, start, stop):
    low = lax.broadcasted_iota(jnp.int32, (32, 128), 1) < N
    for m in range(start // 128, stop // 128):
        v = acc[:, 128 * m : 128 * m + 128]
        w = pltpu.roll(v, N, 1)
        rows[pl.ds(2 * m, 32, stride=N), :] = jnp.where(low, v[0:32], w[32:64])
        rows[pl.ds(2 * m + 1, 32, stride=N), :] = jnp.where(low, w[0:32], v[32:64])


def to_columns(rows, at, q):
    for t in range(16):
        hi, lo = split(rows[128 * t : 128 * t + 128, :].T)
        at[q, 128 * t : 128 * t + 128, 0:128] = hi
        at[q, 128 * t : 128 * t + 128, 128:256] = lo


def advance(left, unit, keep, at, mixed, next_left, inverses, q, begin):
    line, low, place, eye = patterns()
    both = jnp.concatenate([jnp.where(low, left, 0.0), jnp.where(low, 0.0, pltpu.roll(left, N, 1))], 0)
    hi, lo = split(both)
    weights = jnp.concatenate(
        [jnp.concatenate([hi, hi], 1), jnp.concatenate([lo, jnp.zeros_like(lo)], 1)], 0
    )
    for t in range(0, 16, 2):
        o = dot(at[q, 128 * t : 128 * t + 256, :], weights, NT)
        hi, lo = split(o[:, 0:128] + o[:, 128:256])
        for u in range(2):
            lanes = slice(128 * (t + u), 128 * (t + u) + 128)
            mixed[q, 0:128, lanes] = hi[128 * u : 128 * u + 128]
            mixed[q, 128:256, lanes] = lo[128 * u : 128 * u + 128]
    y = mixed[q]
    g = dot(y, y, NT)
    g = g[0:128] + g[128:256]
    g = g[:, 0:128] + g[:, 128:256]
    total = jnp.sum(jnp.where(low, left * left, 0.0), keepdims=True)
    scale = lax.rsqrt(total * (1.0 / (N * N)) + 1e-06)
    scale = jnp.ones_like(scale) if unit else scale
    full = (g[0:N] + pltpu.roll(g[N:], N, 1)) * (scale * scale)

    def emit(p, rows):
        part = slice(8 * p, 8 * p + 8)
        upper = jnp.logical_and(low[part], place[part] >= line[part])
        next_left[part, :] = jnp.where(jnp.logical_and(keep[part], upper), rows, 0.0)
        inverses[q, part, :] = jnp.where(jnp.logical_or(low[part], jnp.logical_not(keep[part])), 0.0, rows) * (scale * float(N))
        if begin is not None:
            begin(p)

    factor(jnp.where(low, full, eye), emit)


def results(inverses, mixed, rows, out, q):
    inverse = inverses[q]
    pair = jnp.concatenate([pltpu.roll(inverse, N, 1), inverse], 0)
    p_hi, p_lo = split(pair)
    wide = jnp.concatenate([p_hi, p_hi], 1)
    for c in range(8):
        y = mixed[q, :, 256 * c : 256 * c + 256]
        o = dot(wide, y, NN) + dot(p_lo, y[0:128], NN)
        rows[256 * c : 256 * c + 128, :] = o[:, 0:128].T
        rows[256 * c + 128 : 256 * c + 256, :] = o[:, 128:256].T
    low = lax.broadcasted_iota(jnp.int32, (32, 128), 1) < N
    for m in range(32):
        e = rows[pl.ds(2 * m, 32, stride=N), :]
        d = rows[pl.ds(2 * m + 1, 32, stride=N), :]
        at = slice(128 * m, 128 * m + 128)
        out[q, 0:32, at] = jnp.where(low, e, pltpu.roll(d, N, 1)).astype(jnp.bfloat16)
        out[q, 32:64, at] = jnp.where(low, pltpu.roll(e, N, 1), d).astype(jnp.bfloat16)


def sweep_kernel(
    ranks_ref, ops_ref, bnd_ref, out_ref,
    blocks, raw, ops, ranks, limits, acc, second, rows, at, mixed, out, inverses, l_in, l_out, left_ref,
    guests, guest_raw, guest_ops, guest_sums, part_send, part_recv, own_sem, ring_send, ring_recv, l_send, l_recv, out_send, out_recv, out_own,
    gift_send, gift_recv, back_send, back_recv, lent_send, lent_recv, hop_send,
):
    me = lax.axis_index("col")
    columns = lax.axis_size("col")
    z = lax.axis_index("sec")
    size = lax.axis_size("sec")
    core = lax.rem(me, 2)
    partner = me + 1 - 2 * core
    up, down = lax.rem(z + 1, size), lax.rem(z + size - 1, size)
    after, before = lax.rem(me + 2, columns), lax.rem(me + columns - 2, columns)
    is_first = me < 2
    band = columns // 4
    row = me // band
    peer = me + band * (3 - 2 * row)

    for b in range(2):
        ranks[b] = jnp.full((8, 128), ranks_ref[b].astype(jnp.float32))
    barrier = pltpu.get_barrier_semaphore()
    peer_partner = peer + 1 - 2 * core
    beside = me + band * (1 - 2 * lax.rem(row, 2))
    beside_partner = beside + 1 - 2 * core
    greeted = (
        (partner, z), (me, up), (me, down), (partner, up), (partner, down), (before, z), (peer, z), (peer_partner, z),
        (beside, z), (beside_partner, z),
    )
    for to in greeted:
        pl.semaphore_signal(barrier, inc=1, device_id=to, device_id_type=MESH)
    pl.semaphore_wait(barrier, len(greeted))

    def to_partner(n, source, target):
        return pltpu.make_async_remote_copy(
            src_ref=source, dst_ref=target, send_sem=part_send.at[n], recv_sem=part_recv.at[n],
            device_id=(partner, z), device_id_type=MESH,
        )

    crossing = [
        to_partner(0, bnd_ref.at[0, 1 - core, 0], blocks.at[core, z]),
        to_partner(1, ops_ref.at[1 - core, 0, :, z], raw.at[core]),
        to_partner(2, ranks.at[1 - core], limits.at[core]),
    ]
    staying = [
        pltpu.make_async_copy(bnd_ref.at[0, core, 0], blocks.at[core, z], own_sem.at[0]),
        pltpu.make_async_copy(ops_ref.at[core, 0, :, z], raw.at[core], own_sem.at[1]),
        pltpu.make_async_copy(ranks.at[core], limits.at[core], own_sem.at[2]),
    ]
    for copy in crossing + staying:
        copy.start()

    edges = {1: (0, OWN), 2: (OWN, MIDDLE), 3: (MIDDLE, N * N)}

    def chunk(c):
        return slice(sum(CHUNKS[:c]), sum(CHUNKS[: c + 1]))

    def far_chunk(c):
        return slice(OWN + sum(CHUNKS[:c]), OWN + sum(CHUNKS[: c + 1]))

    def ring(flow, way, d, half):
        block = lax.rem(z + size + (d - 1 if way else 1 - d), size)
        lines = slice(32 * half, 32 * half + 32)
        if flow == 0:
            part = blocks.at[0, block, lines]
        elif flow < 4:
            part = blocks.at[1, block, lines, edges[flow][0] : edges[flow][1]]
        else:
            part = guests.at[block, lines, chunk(flow - 4)]
        return pltpu.make_async_remote_copy(
            src_ref=part, dst_ref=part, send_sem=ring_send.at[flow, way, d - 1, half],
            recv_sem=ring_recv.at[flow, way, d - 1, half],
            device_id=(me, down if way else up), device_id_type=MESH,
        )

    def first_hop(flow, way, half, b):
        q = 0 if flow == 0 else 1
        lines = slice(32 * half, 32 * half + 32)
        lanes = slice(*edges[flow]) if flow else slice(0, N * N)
        return pltpu.make_async_remote_copy(
            src_ref=bnd_ref.at[0, b, 0, lines, lanes], dst_ref=blocks.at[q, z, lines, lanes],
            send_sem=hop_send.at[flow, way, half, b], recv_sem=ring_recv.at[flow, way, 0, half],
            device_id=(me - core + b, down if way else up), device_id_type=MESH,
        )

    def gift(c, half, b):
        lines = slice(32 * half, 32 * half + 32)
        return pltpu.make_async_remote_copy(
            src_ref=bnd_ref.at[0, b, 0, lines, far_chunk(c)], dst_ref=guests.at[z, lines, chunk(c)],
            send_sem=gift_send.at[c, half, b], recv_sem=gift_recv.at[c, half],
            device_id=((beside if c == 3 else peer) - core + b, z), device_id_type=MESH,
        )

    def lent(b, to_beside):
        return pltpu.make_async_remote_copy(
            src_ref=ops_ref.at[b, 0, :, z], dst_ref=guest_raw, send_sem=lent_send.at[to_beside, b], recv_sem=lent_recv,
            device_id=((beside if to_beside else peer) - core + b, z), device_id_type=MESH,
        )

    def back(c):
        return pltpu.make_async_remote_copy(
            src_ref=guest_sums.at[:, chunk(c)], dst_ref=second.at[:, far_chunk(c)],
            send_sem=back_send.at[c], recv_sem=back_recv.at[c],
            device_id=(beside if c == 3 else peer, z), device_id_type=MESH,
        )

    def parts(d):
        return [(way, d, half) for half in range(2) for way in range(2) if d < 4 or half == way]

    def ready(q):
        @pl.when(core == q)
        def _():
            staying[0].wait()

        @pl.when(core != q)
        def _():
            crossing[0].wait_recv()

    def hops():
        return [(way, half, b) for half in range(2) for way in range(2) for b in range(2)]

    def begin(flow):
        @pl.when(core == (0 if flow == 0 else 1))
        def _():
            for hop in hops():
                first_hop(flow, *hop).start()

    def turn(flow, d):
        for way, _, half in parts(d):
            ring(flow, way, d, half).wait_recv()
            if d < 4 and (way, d + 1, half) in parts(d + 1):
                ring(flow, way, d + 1, half).start()

    def sectors(d):
        before, after = lax.rem(z + size - d, size), lax.rem(z + d, size)
        return [z] if d == 0 else [after] if d == 4 else [before, after]

    def absorb_flow(flow, d):
        q = 0 if flow == 0 else 1
        start, width, tiles = {0: (0, 512, 8), 1: (0, 256, 1), 2: (OWN, 256, 10), 3: (MIDDLE, 256, 5)}[flow]
        absorb(
            [ops[q, s] for s in sectors(d)], [blocks.at[q, s] for s in sectors(d)],
            second if q else acc, start, width, tiles, d == 0,
        )

    def open_guest(c):
        for half in range(2):
            gift(c, half, 0).wait_recv()
            for way in range(2):
                ring(4 + c, way, 1, half).start()

    def borrow():
        lent(0, 0).wait_recv()
        flip(guest_raw, guest_ops)

    def give_back(c):
        lefts = [guest_ops[s] for s in range(8)]
        rights = [guests.at[s] for s in range(8)]
        wide, rest = CHUNKS[c] // 256, CHUNKS[c] % 256
        absorb(lefts, rights, guest_sums, chunk(c).start, 256, wide, True)
        if rest:
            absorb(lefts, rights, guest_sums, chunk(c).stop - rest, rest, 1, True)
        back(c).start()

    def serve(count, at_end):
        open_guest(0)
        open_guest(1)
        for slot in range(1, 2 * count + 3):
            for c in range(count):
                d = slot - 2 * c
                if not 1 <= d <= 4:
                    continue
                turn(4 + c, d)
                if d == 3 and c + 2 < count:
                    open_guest(c + 2)
                if d == 3 and c == count - 1:
                    at_end()
                if d == 4:
                    if c == 0:
                        borrow()
                    give_back(c)

    def begin_own():
        begin(0)
        begin(1)

    @pl.when(jnp.logical_and(row < 2, core == 1))
    def _():
        for c in range(2):
            for half in range(2):
                for b in range(2):
                    gift(c, half, b).start()

    @pl.when(row < 3)
    def _():
        begin_own()

    @pl.when(jnp.logical_and(row == 0, core == 1))
    def _():
        for c in (3, 2):
            for half in range(2):
                for b in range(2):
                    gift(c, half, b).start()
        for b in range(2):
            lent(b, 1).start()

    @pl.when(jnp.logical_and(row < 2, core == 1))
    def _():
        for b in range(2):
            lent(b, 0).start()

    @pl.when(row == 1)
    def _():
        open_guest(3)

    @pl.when(row == 2)
    def _():
        open_guest(0)
        open_guest(1)

    @pl.when(row == 3)
    def _():
        serve(3, begin_own)

    ready(0)
    ready(1)
    for copy in staying[1:]:
        copy.wait()
    for copy in crossing[1:]:
        copy.wait_recv()
    for q in range(2):
        flip(raw.at[q], ops.at[q])

    for d in range(5):
        if d > 0:

            def guests_turn(step):
                @pl.when(row == 1)
                def _():
                    turn(7, step)

                @pl.when(row == 2)
                def _():
                    turn(4, step)
                    turn(5, step)

            if d < 3:
                guests_turn(2 * d - 1)
            turn(0, d)
            turn(1, d)
            if d < 3:
                guests_turn(2 * d)
            if d == 2:

                @pl.when(row == 1)
                def _():
                    borrow()
                    give_back(3)

                @pl.when(row == 2)
                def _():
                    borrow()
                    give_back(0)
                    give_back(1)

        if d == 3:

            @pl.when(row >= 2)
            def _():
                begin(2)

            @pl.when(row >= 1)
            def _():
                begin(3)

        absorb_flow(0, d)
        absorb_flow(1, d)
    spread(acc, rows, 0, N * N)
    to_columns(rows, at, 0)
    for d in range(5):

        @pl.when(row >= 2)
        def _():
            if d > 0:
                turn(2, d)
            absorb_flow(2, d)

        @pl.when(row >= 1)
        def _():
            if d > 0:
                turn(3, d)
            absorb_flow(3, d)

    line, low, place, eye = patterns()

    def along(part, start, size):
        return pltpu.make_async_remote_copy(
            src_ref=l_out.at[start : start + size], dst_ref=l_in.at[start : start + size],
            send_sem=l_send.at[part], recv_sem=l_recv.at[part], device_id=(after, z), device_id_type=MESH,
        )

    pieces = {3: along(0, 0, 32), 5: along(1, 32, 16), 6: along(2, 48, 8), 7: along(3, 56, 8)}

    def keep(q):
        return line.astype(jnp.float32) < limits[q, 0:1, :]

    def begin_piece(p):
        if p in pieces:
            pieces[p].start()

    @pl.when(is_first)
    def _():
        advance(eye, True, keep(0), at, mixed, left_ref, inverses, 0, None)

    @pl.when(row < 2)
    def _():
        for c in range(2):
            back(c).wait_recv()

    spread(second, rows, 0, MIDDLE)

    @pl.when(row == 0)
    def _():
        for c in range(2, 4):
            back(c).wait_recv()

    spread(second, rows, MIDDLE, N * N)
    to_columns(rows, at, 1)

    @pl.when(jnp.logical_not(is_first))
    def _():
        for piece in pieces.values():
            piece.wait_recv()
        advance(l_in[...], False, keep(0), at, mixed, left_ref, inverses, 0, None)

    advance(left_ref[...], False, keep(1), at, mixed, l_out, inverses, 1, begin_piece)

    across = pltpu.make_async_remote_copy(
        src_ref=out.at[1 - core], dst_ref=out_ref.at[0, core, 0], send_sem=out_send, recv_sem=out_recv,
        device_id=(partner, z), device_id_type=MESH,
    )
    home = pltpu.make_async_copy(out.at[core], out_ref.at[0, core, 0], out_own)

    for q in range(2):
        results(inverses, mixed, rows, out, q)

        @pl.when(core == q)
        def _():
            home.start()

        @pl.when(core != q)
        def _():
            across.start()

    home.wait()
    across.wait()

    for piece in pieces.values():
        piece.wait_send()

    @pl.when(is_first)
    def _():
        for piece in pieces.values():
            piece.wait_recv()

    for copy in crossing:
        copy.wait_send()
    late = [part for d in range(2, 5) for part in parts(d)]

    def sent(*flows):
        for flow in flows:
            for part in late + (parts(1) if flow > 3 else []):
                ring(flow, *part).wait_send()
            if flow < 4:

                @pl.when(core == (0 if flow == 0 else 1))
                def _():
                    for hop in hops():
                        first_hop(flow, *hop).wait_send()

    sent(0, 1)

    @pl.when(row >= 2)
    def _():
        sent(2, 4, 5)
        for c in range(2):
            back(c).wait_send()

    @pl.when(row >= 1)
    def _():
        sent(3)

    @pl.when(row == 3)
    def _():
        sent(6)
        back(2).wait_send()

    @pl.when(row == 1)
    def _():
        sent(7)
        back(3).wait_send()

    @pl.when(jnp.logical_and(row < 2, core == 1))
    def _():
        for b in range(2):
            lent(b, 0).wait_send()
            for c in range(2):
                for half in range(2):
                    gift(c, half, b).wait_send()

    @pl.when(jnp.logical_and(row == 0, core == 1))
    def _():
        for b in range(2):
            lent(b, 1).wait_send()
            for c in range(2, 4):
                for half in range(2):
                    gift(c, half, b).wait_send()


def sweep(ranks, ops, boundaries):
    anywhere = pl.BlockSpec(memory_space=pltpu.HBM)
    bf16, f32 = jnp.bfloat16, jnp.float32
    dma = pltpu.SemaphoreType.DMA
    return pl.pallas_call(
        sweep_kernel,
        out_shape=jax.ShapeDtypeStruct(boundaries.shape, bf16),
        in_specs=[pl.BlockSpec(memory_space=pltpu.SMEM), anywhere, anywhere],
        out_specs=anywhere,
        scratch_shapes=[
            pltpu.VMEM((2, 8, N, N * N), bf16),
            pltpu.VMEM((2, 8, N, N), bf16),
            pltpu.VMEM((2, 8, N, N), bf16),
            pltpu.VMEM((2, 8, 128), f32),
            pltpu.VMEM((2, 8, 128), f32),
            pltpu.VMEM((N, N * N), f32),
            pltpu.VMEM((N, N * N), f32),
            pltpu.VMEM((2048, 128), f32),
            pltpu.VMEM((2, 2048, 256), bf16),
            pltpu.VMEM((2, 256, 2048), bf16),
            pltpu.VMEM((2, N, N * N), bf16),
            pltpu.VMEM((2, N, 128), f32),
            pltpu.VMEM((N, 128), f32),
            pltpu.VMEM((N, 128), f32),
            pltpu.VMEM((N, 128), f32),
            pltpu.VMEM((8, N, sum(CHUNKS)), bf16),
            pltpu.VMEM((8, N, N), bf16),
            pltpu.VMEM((8, N, N), bf16),
            pltpu.VMEM((N, sum(CHUNKS)), f32),
            dma((3,)), dma((3,)), dma((3,)),
            dma((8, 2, 4, 2)), dma((8, 2, 4, 2)),
            dma((4,)), dma((4,)), dma, dma, dma,
            dma((4, 2, 2)), dma((4, 2)), dma((4,)), dma((4,)), dma((2, 2)), dma, dma((4, 2, 2, 2)),
        ],
        compiler_params=pltpu.CompilerParams(
            collective_id=0, has_side_effects=True, vmem_limit_bytes=60 * 1024 * 1024
        ),
    )(ranks, ops, boundaries)


def on_device(boundaries, row_ops, ranks):
    return sweep(ranks.reshape(2), row_ops, boundaries)


def solution(mesh):
    placed = (
        P("sec", None, "col", None, None),
        P(None, "col", None, None, None, None),
        P("sec", None, "col"),
    )
    return jax.shard_map(
        on_device,
        mesh=mesh,
        in_specs=placed,
        out_specs=P("sec", None, "col", None, None),
        check_vma=False,
    )
```
